256 devices in a mesh: gx: 8 (over z), gy: 16 (over y, x), gz: 2 (over core).
Axes of the slice: x: 4, y: 4, z: 8, core: 2. Of those that a mesh axis runs over, the one named last changes fastest.
Arguments:
- right_side: float32 [128, 512, 1024], P('gx', 'gy', 'gz'), may hold values from -6 to 6
- coefficient: float32 [128, 512, 1024], P('gx', 'gy', 'gz'), may hold values from 0.2 to 5
Outputs:
- solution_field: float32 [128, 512, 1024], P('gx', 'gy', 'gz')
The draws below stay inside these ranges and needn't reach their ends.
All inputs are finite; a program needn't handle non-finite values.
Results may differ from the reference program's by a relative error of at most 0.0003.
Values sent between devices are 32-bit elements; how exact they have to be, the bound alone decides.
A program may use at most 192 MiB of HBM per device.

```python
import math
import jax
import jax.numpy as jnp
from jax import lax

SWEEPS = 2
BOTTOM_SWEEPS = 6
NX = 128
NY = 512
NZ = 1024


def draw_right_side(key, part):
    key = jax.random.fold_in(key, 11)
    values = jnp.clip(jax.random.normal(key, (NX, NY, NZ), jnp.float32), -6.0, 6.0)
    return values


def levels(rng, shape, shards, least, high):
    def one(position, shards_of):
        heights = jax.random.uniform(jax.random.fold_in(jax.random.fold_in(rng, 6), position), (shards_of,), jnp.float32, least / len(shards), high / len(shards))
        return jnp.repeat(jnp.exp(heights), shape[position] // shards_of).reshape((-1,) + (1,) * (len(shape) - position - 1))

    level = one(*shards[0])
    for cut in shards[1:]:
        level = level * one(*cut)
    return level


def setup_inputs(seed: int = 0) -> dict:
    splits = jax.random.split(jax.random.key(seed), 3)
    return {
        "right_side": draw_right_side(jax.random.fold_in(splits[2], 71), 0),
        "coefficient": jnp.clip(jnp.exp(math.log(5.0) - 3.218876 * jax.random.uniform(splits[1], (NX, NY, NZ), jnp.float32) ** levels(splits[1], (NX, NY, NZ), ((0, 8), (1, 16), (2, 2)), -0.2, 0.2)), 0.2, 5.0),
    }


def pad_zero(values):
    return jnp.pad(values, 1)


def neighbour(padded, which_dim, offset):
    window_list = [slice(1, -1)] * 3
    window_list[which_dim] = slice(offset, offset + padded.shape[which_dim] - 2)
    return padded[tuple(window_list)]


def operator_of(coefficient, padded, level_scale):
    face_list = []
    for which_dim in range(3):
        for offset in (0, 2):
            beside = neighbour(padded, which_dim, offset)
            face_list.append(level_scale * jnp.where(beside > 0.0, 0.5 * (coefficient + beside), coefficient))
    diagonal = face_list[0]
    for weight in face_list[1:]:
        diagonal = diagonal + weight
    return face_list, diagonal


def apply_op(padded, values, operator):
    face_list, diagonal = operator
    result = diagonal * values
    number = 0
    for which_dim in range(3):
        for offset in (0, 2):
            result = result - face_list[number] * neighbour(padded, which_dim, offset)
            number += 1
    return result


def chebyshev(rhs_field, initial, sweeps, lower_edge, upper_edge, extend, operator):
    cheb_theta = 0.5 * (upper_edge + lower_edge)
    cheb_delta = 0.5 * (upper_edge - lower_edge)
    cheb_sigma = cheb_theta / cheb_delta
    cheb_rho = 1.0 / cheb_sigma
    diagonal = operator[1]
    if initial is None:
        remain = rhs_field
        iterate = jnp.zeros_like(rhs_field)
    else:
        remain = rhs_field - apply_op(extend(initial), initial, operator)
        iterate = initial
    step_dir = (remain / diagonal) * (1.0 / cheb_theta)
    iterate = iterate + step_dir
    for sweep in range(1, sweeps):
        rho_next = 1.0 / (2.0 * cheb_sigma - cheb_rho)
        remain = rhs_field - apply_op(extend(iterate), iterate, operator)
        step_dir = (rho_next * cheb_rho) * step_dir + (2.0 * rho_next / cheb_delta) * (remain / diagonal)
        iterate = iterate + step_dir
        cheb_rho = rho_next
    return iterate


def coarsen(coefficient):
    dims_now = coefficient.shape
    blocks = coefficient.reshape(dims_now[0] // 2, 2, dims_now[1] // 2, 2, dims_now[2] // 2, 2)
    return jnp.mean(blocks, axis=(1, 3, 5))


def restrict_along(padded, which_dim):
    dims_now = padded.shape
    paired = padded.reshape(dims_now[:which_dim] + (dims_now[which_dim] // 2, 2) + dims_now[which_dim + 1:])
    length = paired.shape[which_dim]
    first_part = lax.index_in_dim(paired, 0, which_dim + 1, keepdims=False)
    second = lax.index_in_dim(paired, 1, which_dim + 1, keepdims=False)
    return 0.125 * (lax.slice_in_dim(first_part, 0, length - 1, axis=which_dim)
                    + 3.0 * lax.slice_in_dim(second, 0, length - 1, axis=which_dim)
                    + 3.0 * lax.slice_in_dim(first_part, 1, length, axis=which_dim)
                    + lax.slice_in_dim(second, 1, length, axis=which_dim))


def restrict_all(padded):
    for which_dim in range(3):
        padded = restrict_along(padded, which_dim)
    return padded


def prolong_along(padded, which_dim):
    length = padded.shape[which_dim] - 2
    centre = lax.slice_in_dim(padded, 1, length + 1, axis=which_dim)
    lower_cell = lax.slice_in_dim(padded, 0, length, axis=which_dim)
    upper_cell = lax.slice_in_dim(padded, 2, length + 2, axis=which_dim)
    even_cells = 0.75 * centre + 0.25 * lower_cell
    odd_cells = 0.75 * centre + 0.25 * upper_cell
    joined = jnp.stack((even_cells, odd_cells), axis=which_dim + 1)
    dims_now = joined.shape
    return joined.reshape(dims_now[:which_dim] + (2 * length,) + dims_now[which_dim + 2:])


def prolong_all(padded):
    for which_dim in range(3):
        padded = prolong_along(padded, which_dim)
    return padded


def reference(right_side, coefficient):
    coarse_one = coarsen(coefficient)
    coarse_two = coarsen(coarse_one)
    fine_ops = operator_of(coefficient, pad_zero(coefficient), 1.0)
    mid_ops = operator_of(coarse_one, pad_zero(coarse_one), 0.25)
    low_ops = operator_of(coarse_two, pad_zero(coarse_two), 0.0625)
    pre_fine = chebyshev(right_side, None, SWEEPS, 0.3, 2.0, pad_zero, fine_ops)
    resid_fine = right_side - apply_op(pad_zero(pre_fine), pre_fine, fine_ops)
    mid_rhs = restrict_all(pad_zero(resid_fine))
    pre_mid = chebyshev(mid_rhs, None, SWEEPS, 0.3, 2.0, pad_zero, mid_ops)
    resid_mid = mid_rhs - apply_op(pad_zero(pre_mid), pre_mid, mid_ops)
    low_rhs = restrict_all(pad_zero(resid_mid))
    bottom = chebyshev(low_rhs, None, BOTTOM_SWEEPS, 0.05, 2.0, pad_zero, low_ops)
    post_mid = chebyshev(mid_rhs, pre_mid + prolong_all(pad_zero(bottom)), SWEEPS, 0.3, 2.0, pad_zero, mid_ops)
    return chebyshev(right_side, pre_fine + prolong_all(pad_zero(post_mid)), SWEEPS, 0.3, 2.0, pad_zero, fine_ops)
```

```python
import functools

import jax
import jax.numpy as jnp
from jax import lax
from jax.experimental import pallas as pl
from jax.experimental.pallas import tpu as pltpu
from jax.sharding import PartitionSpec as P

MESH = pl.DeviceIdType.MESH
F32 = jnp.float32
BF16 = jnp.bfloat16


def cheb_constants(sweeps, lower_edge, upper_edge):
    theta = 0.5 * (upper_edge + lower_edge)
    delta = 0.5 * (upper_edge - lower_edge)
    sigma = theta / delta
    rho = 1.0 / sigma
    steps = []
    for _ in range(1, sweeps):
        rho_next = 1.0 / (2.0 * sigma - rho)
        steps.append((rho_next * rho, 2.0 * rho_next / delta))
        rho = rho_next
    return theta, steps


THETA, ((MOM, GAIN),) = cheb_constants(2, 0.3, 2.0)
THETA_LOW, STEPS_LOW = cheb_constants(6, 0.05, 2.0)


def lanes(rows):
    return lax.broadcasted_iota(jnp.int32, (rows, 128), 1)


def roll_up(value):
    return pltpu.roll(value, 1, 1)


def roll_down(value):
    return pltpu.roll(value, 127, 1)


def operator_parts(centre, beside):
    faces = []
    diagonal = None
    for other in beside:
        face = jnp.where(other > 0.0, 0.5 * (centre + other), centre)
        diagonal = face if diagonal is None else diagonal + face
        faces.append(jnp.where(other > 0.0, face, 0.0))
    inside = centre > 0.0
    inverse = jnp.where(inside, 1.0 / diagonal, 0.0)
    diagonal = jnp.where(inside, diagonal, 0.0)
    return [face * inverse for face in faces], diagonal, inverse


def kernel(
    b_hbm, c_hbm, out_hbm,
    b_in, c_in, out_vm, perm,
    cF, bF, xF, x2F, dF, rF, gF, eC, e1, e2, pk, rpk,
    t1, t2, e3,
    c1, b1, x1L, x2L, x0L, xpL, dL, gL, stg, tL,
    c2, bd2, xa, xb, d2, inv2, g2, t3,
    local_sem, ss, rs,
):
    gx, gy, core = lax.axis_index("gx"), lax.axis_index("gy"), lax.axis_index("gz")
    nx, ny = lax.axis_size("gx"), lax.axis_size("gy")
    other = 1 - core
    sibling = (gx, gy, other)
    counter = [0]

    def peer(dx, dy):
        return (lax.rem(gx + dx + nx, nx), lax.rem(gy + dy + ny, ny), core)

    def send(src, dst, device):
        number = counter[0]
        counter[0] += 1
        copy = pltpu.make_async_remote_copy(
            src_ref=src, dst_ref=dst, send_sem=ss.at[number], recv_sem=rs.at[number],
            device_id=device, device_id_type=MESH,
        )
        copy.start()
        return copy

    load_c = pltpu.make_async_copy(c_hbm, c_in, local_sem.at[0])
    load_b = pltpu.make_async_copy(b_hbm, b_in, local_sem.at[1])
    load_c.start()
    load_b.start()

    for ref in (eC, e1, e2):

        @pl.loop(0, 22)
        def _(x, ref=ref):
            ref[x, core] = jnp.zeros((48, 128), F32)

    @pl.loop(0, 10)
    def _(x):
        e3[x, core] = jnp.zeros((16, 128), F32)

    @pl.loop(0, 3)
    def _(x):
        rF[x, :, 8:48, :] = jnp.zeros((4, 40, 128), F32)
        rF[x + 19, :, 8:48, :] = jnp.zeros((4, 40, 128), F32)

    peers14 = [(dx, dy) for dx in (-2, -1, 0, 1, 2) for dy in (-1, 0, 1) if (dx, dy) != (0, 0)]
    barrier = pltpu.get_barrier_semaphore()
    for dx, dy in peers14:
        pl.semaphore_signal(barrier, inc=1, device_id=peer(dx, dy), device_id_type=MESH)
    pl.semaphore_signal(barrier, inc=1, device_id=sibling, device_id_type=MESH)

    @pl.loop(0, 4)
    def _(j):
        z = lax.broadcasted_iota(jnp.int32, (128, 512), 0) + j * 128
        col = lax.broadcasted_iota(jnp.int32, (128, 512), 1)
        perm[pl.ds(pl.multiple_of(j * 128, 128), 128), :] = jnp.where(
            z == 4 * (col % 128) + col // 128, 1.0, 0.0
        ).astype(BF16)

    def spread(source, target):
        @pl.loop(0, 2)
        def _(half):
            rows = source[pl.ds(half * 8, 8)].reshape(256, 512)
            high = rows.astype(BF16)
            low = (rows - high.astype(F32)).astype(BF16)
            table = perm[...]
            result = jnp.dot(high, table, preferred_element_type=F32) + jnp.dot(
                low, table, preferred_element_type=F32
            )
            for k in range(4):
                target[pl.ds(half * 8 + 3, 8), k, 8:40, :] = result[
                    :, k * 128 : (k + 1) * 128
                ].reshape(8, 32, 128)

    load_c.wait()
    spread(c_in, cF)
    pl.semaphore_wait(barrier, len(peers14) + 1)
    face_c = [
        send(cF.at[3:6, :, 8:40], cF.at[19:22, :, 8:40], peer(-1, 0)),
        send(cF.at[16:19, :, 8:40], cF.at[0:3, :, 8:40], peer(1, 0)),
    ]
    load_b.wait()
    spread(b_in, bF)

    @pl.loop(0, 16)
    def _(x):
        for k in range(4):
            pk[0, x, k, 0:4, :] = cF[x + 3, k, 8:12, :]
            pk[0, x, k, 4:8, :] = bF[x + 3, k, 8:12, :]
            pk[1, x, k, 0:4, :] = cF[x + 3, k, 36:40, :]
            pk[1, x, k, 4:8, :] = bF[x + 3, k, 36:40, :]

    halo = [
        send(pk.at[0], rpk.at[1, 3:19], peer(0, -1)),
        send(pk.at[1], rpk.at[0, 3:19], peer(0, 1)),
        send(pk.at[0, 0:3], rpk.at[1, 19:22], peer(-1, -1)),
        send(pk.at[0, 13:16], rpk.at[1, 0:3], peer(1, -1)),
        send(pk.at[1, 0:3], rpk.at[0, 19:22], peer(-1, 1)),
        send(pk.at[1, 13:16], rpk.at[0, 0:3], peer(1, 1)),
    ]
    face_b = [
        send(bF.at[3:5, :, 8:40], bF.at[19:21, :, 8:40], peer(-1, 0)),
        send(bF.at[17:19, :, 8:40], bF.at[1:3, :, 8:40], peer(1, 0)),
    ]

    @pl.loop(0, 8)
    def _(i):
        for k in range(4):
            t1[0, k, 8:40, :] = cF[2 * i + 3, k, 8:40, :] + cF[2 * i + 4, k, 8:40, :]
        for q in range(2):
            total = None
            for k in (2 * q, 2 * q + 1):
                for start in (8, 9):
                    part = t1[0, k, pl.ds(start, 16, stride=2), :]
                    total = part if total is None else total + part
            c1[i + 6, q, core, 16:32, :] = total * (0.125 * 0.25)

    @pl.loop(0, 4)
    def _(i):
        total = None
        for q in range(2):
            tL[0, q, 0, 16:32, :] = c1[2 * i + 6, q, core, 16:32, :] + c1[2 * i + 7, q, core, 16:32, :]
            for start in (16, 17):
                part = tL[0, q, 0, pl.ds(start, 8, stride=2), :]
                total = part if total is None else total + part
        c2[i + 8, core, 16:24, :] = total * (0.125 * 0.25)

    rows_of = {0: (slice(16, 32), slice(16, 32)), -1: (slice(16, 24), slice(32, 40)), 1: (slice(24, 32), slice(8, 16))}
    planes_c1 = {0: (slice(6, 14), slice(6, 14)), -1: (slice(6, 12), slice(14, 20)), 1: (slice(8, 14), slice(0, 6))}
    halo_c1 = []
    for dx, dy in peers14:
        if abs(dx) < 2:
            (xs, xd), (ys, yd) = planes_c1[dx], rows_of[dy]
            halo_c1.append(send(c1.at[xs, :, core, ys], c1.at[xd, :, core, yd], peer(dx, dy)))
    halo_c2 = [
        send(
            c2.at[8:12, core, 16:24],
            c2.at[8 - 4 * dx : 12 - 4 * dx, core, 16 - 8 * dy : 24 - 8 * dy],
            peer(dx, dy),
        )
        for dx, dy in peers14
    ]

    for copy in face_c + halo:
        copy.wait_recv()

    @pl.loop(0, 22)
    def _(x):
        for k in range(4):
            cF[x, k, 4:8, :] = rpk[0, x, k, 0:4, :]
            bF[x, k, 4:8, :] = rpk[0, x, k, 4:8, :]
            cF[x, k, 40:44, :] = rpk[1, x, k, 0:4, :]
            bF[x, k, 40:44, :] = rpk[1, x, k, 4:8, :]

    def clear_planes(ref, first, count, condition):
        @pl.when(condition)
        def _():
            @pl.loop(first, first + count)
            def _(x):
                if ref.shape[1] == 4:
                    ref[x, :, 0:48, :] = jnp.zeros((4, 48, 128), F32)
                elif len(ref.shape) == 5:
                    for q in range(2):
                        ref[x, q, core] = jnp.zeros(ref.shape[3:], F32)
                else:
                    ref[x, core] = jnp.zeros(ref.shape[2:], F32)

    def clear_rows(ref, first, count, condition):
        zero = jnp.zeros((count, 128), F32)

        @pl.when(condition)
        def _():
            @pl.loop(0, ref.shape[0])
            def _(x):
                if ref.shape[1] == 4:
                    for k in range(4):
                        ref[x, k, first : first + count, :] = zero
                elif len(ref.shape) == 5:
                    for q in range(2):
                        ref[x, q, core, first : first + count, :] = zero
                else:
                    ref[x, core, first : first + count, :] = zero

    clear_planes(cF, 0, 3, gx == 0)
    clear_planes(cF, 19, 3, gx == nx - 1)
    clear_rows(cF, 4, 4, gy == 0)
    clear_rows(cF, 40, 4, gy == ny - 1)

    edge_phase = 3 * other

    def swap(source, target, first, last, rows):
        return send(
            source.at[first:last, edge_phase, rows], target.at[first:last, core, rows], sibling
        )

    CWIN, CUP, CDOWN = slice(4, 44), slice(3, 43), slice(5, 45)
    WIN, UP, DOWN = slice(8, 48), slice(7, 47), slice(9, 49)
    lane40 = lanes(40)

    def left_of(ref, edge, x, k, win):
        if k:
            return ref[x, k - 1, win, :]
        return roll_up(jnp.where(lane40 == 127, edge[x, 0, win, :], ref[x, 3, win, :]))

    def right_of(ref, edge, x, k, win):
        if k < 3:
            return ref[x, k + 1, win, :]
        return roll_down(jnp.where(lane40 == 0, edge[x, 1, win, :], ref[x, 0, win, :]))

    def planes(first, last, group, body):
        count = last - first

        @pl.loop(0, count // group)
        def _(j):
            for store_all in [body(first + j * group + u) for u in range(group)]:
                store_all()

        for store_all in [body(last - 1 - u) for u in range(count % group)]:
            store_all()

    INNER, OUTER = (1, 2), (0, 3)

    def setup_fine(phases):
        def body(x):
            results = []
            for k in phases:
                beside = [
                    cF[x - 1, k, CWIN, :], cF[x + 1, k, CWIN, :], cF[x, k, CUP, :], cF[x, k, CDOWN, :],
                    left_of(cF, eC, x, k, CWIN), right_of(cF, eC, x, k, CWIN),
                ]
                weights, diagonal, inverse = operator_parts(cF[x, k, CWIN, :], beside)
                results.append((k, weights, diagonal, bF[x, k, CWIN, :] * inverse * (1.0 / THETA)))

            def store_all():
                for k, weights, diagonal, iterate in results:
                    for n, weight in enumerate(weights):
                        gF[n, x - 1, k] = weight
                    dF[x, k] = diagonal
                    xF[x, k, WIN, :] = iterate

            return store_all

        planes(1, 21, 1, body)

    def sum_fine(ref, edge, x, k):
        return (
            gF[0, x - 1, k] * ref[x - 1, k, WIN, :]
            + gF[1, x - 1, k] * ref[x + 1, k, WIN, :]
            + gF[2, x - 1, k] * ref[x, k, UP, :]
            + gF[3, x - 1, k] * ref[x, k, DOWN, :]
            + gF[4, x - 1, k] * left_of(ref, edge, x, k, WIN)
            + gF[5, x - 1, k] * right_of(ref, edge, x, k, WIN)
        )

    def sweep_fine(target, source, edge, first, last, phases, formula):
        def body(x):
            results = [(k, formula(x, k, sum_fine(source, edge, x, k))) for k in phases]

            def store_all():
                for k, value in results:
                    target[x, k, WIN, :] = value

            return store_all

        planes(first, last, 2, body)

    first = 1.0 + MOM + GAIN * (THETA - 1.0)

    def pre_step(x, k, total):
        return first * xF[x, k, WIN, :] + GAIN * total

    def residual(x, k, total):
        return dF[x, k] * (THETA * xF[x, k, WIN, :] - x2F[x, k, WIN, :] + total)

    copy = swap(cF, eC, 1, 21, slice(0, 48))
    for other_copy in face_b:
        other_copy.wait_recv()
    for other_copy in face_b + halo + face_c:
        other_copy.wait_send()
    setup_fine(INNER)
    copy.wait()
    setup_fine(OUTER)
    copy = swap(xF, e1, 2, 20, WIN)
    sweep_fine(x2F, xF, e1, 2, 20, INNER, pre_step)
    copy.wait()
    sweep_fine(x2F, xF, e1, 2, 20, OUTER, pre_step)
    copy = swap(x2F, e2, 3, 19, WIN)
    far = [
        send(x2F.at[17:18, :, WIN], x2F.at[1:2, :, WIN], peer(1, 0)),
        send(x2F.at[4:5, :, WIN], x2F.at[20:21, :, WIN], peer(-1, 0)),
    ]
    sweep_fine(rF, x2F, e2, 3, 19, INNER, residual)
    copy.wait()
    sweep_fine(rF, x2F, e2, 3, 19, OUTER, residual)

    @pl.loop(0, 10)
    def _(i):
        for k in range(4):
            t1[i, k, WIN, :] = 0.125 * (
                rF[2 * i, k, WIN, :]
                + 3.0 * (rF[2 * i + 1, k, WIN, :] + rF[2 * i + 2, k, WIN, :])
                + rF[2 * i + 3, k, WIN, :]
            )
            part = [t1[i, k, pl.ds(s, 16, stride=2), :] for s in (11, 12, 13, 14)]
            t2[i, k] = 0.125 * (part[0] + 3.0 * (part[1] + part[2]) + part[3])

    copy = send(t2.at[:, edge_phase], e3.at[:, core], sibling)
    copy.wait()
    lane16 = lanes(16)

    @pl.loop(0, 10)
    def _(i):
        p = [t2[i, k] for k in range(4)]
        before = roll_up(jnp.where(lane16 == 127, e3[i, 0], p[3]))
        after = roll_down(jnp.where(lane16 == 0, e3[i, 1], p[0]))
        b1[i + 5, 0, core, 16:32, :] = 0.125 * (before + 3.0 * (p[0] + p[1]) + p[2])
        b1[i + 5, 1, core, 16:32, :] = 0.125 * (p[1] + 3.0 * (p[2] + p[3]) + after)

    halo_b1 = []
    for dx, dy in peers14:
        if abs(dx) < 2:
            ys, yd = rows_of[dy]
            if dx == 0:
                halo_b1.append(send(b1.at[5:15, :, core, ys], b1.at[5:15, :, core, yd], peer(dx, dy)))
            else:
                xs, xd, near, side = (
                    (slice(9, 13), slice(1, 5), slice(13, 15), 0)
                    if dx == 1
                    else (slice(7, 11), slice(15, 19), slice(5, 7), 1)
                )
                halo_b1.append(send(b1.at[near, :, core, ys], stg.at[side, :, :, yd], peer(dx, dy)))
                halo_b1.append(send(b1.at[xs, :, core, ys], b1.at[xd, :, core, yd], peer(dx, dy)))

    for copy in halo_c1 + halo_c2:
        copy.wait()
    clear_planes(c1, 0, 6, gx == 0)
    clear_planes(c1, 14, 6, gx == nx - 1)
    clear_rows(c1, 8, 8, gy == 0)
    clear_rows(c1, 32, 8, gy == ny - 1)
    clear_planes(c2, 4, 4, gx == 0)
    clear_planes(c2, 0, 4, gx <= 1)
    clear_planes(c2, 12, 4, gx == nx - 1)
    clear_planes(c2, 16, 4, gx >= nx - 2)
    clear_rows(c2, 8, 8, gy == 0)
    clear_rows(c2, 24, 8, gy == ny - 1)
    hand = [
        send(c1.at[:, :, core, 8:40], c1.at[:, :, core, 8:40], sibling),
        send(c2.at[:, core, 8:32], c2.at[:, core, 8:32], sibling),
    ]
    for copy in hand:
        copy.wait()

    lane32, lane24 = lanes(32), lanes(24)
    WL, UL, DL = slice(8, 40), slice(7, 39), slice(9, 41)
    W2, U2, D2 = slice(8, 32), slice(7, 31), slice(9, 33)

    def before_pair(halves, lane):
        turned = [roll_up(half) for half in halves]
        return [jnp.where(lane == 0, 0.0, turned[0]), jnp.where(lane == 0, turned[0], turned[1])]

    def after_pair(halves, lane):
        turned = [roll_down(half) for half in halves]
        return [jnp.where(lane == 127, turned[1], turned[0]), jnp.where(lane == 127, 0.0, turned[1])]

    def z_mid(ref, x):
        p0 = [ref[x, 0, t, WL, :] for t in range(2)]
        p1 = [ref[x, 1, t, WL, :] for t in range(2)]
        return [(before_pair(p1, lane32), p1), (p0, after_pair(p0, lane32))]

    @pl.loop(1, 19)
    def _(x):
        z_list = z_mid(c1, x)
        for q in range(2):
            for t in range(2):
                beside = [
                    c1[x - 1, q, t, WL, :], c1[x + 1, q, t, WL, :], c1[x, q, t, UL, :], c1[x, q, t, DL, :],
                    z_list[q][0][t], z_list[q][1][t],
                ]
                weights, diagonal, inverse = operator_parts(c1[x, q, t, WL, :], beside)
                for n, weight in enumerate(weights):
                    gL[n, x - 1, q, t] = weight
                dL[x, q, t] = diagonal
                x0L[x, q, t, WL, :] = inverse * (1.0 / THETA)

    @pl.loop(1, 19)
    def _(x):
        halves = [c2[x, t, W2, :] for t in range(2)]
        low, high = before_pair(halves, lane24), after_pair(halves, lane24)
        for t in range(2):
            beside = [
                c2[x - 1, t, W2, :], c2[x + 1, t, W2, :], c2[x, t, U2, :], c2[x, t, D2, :], low[t], high[t],
            ]
            weights, _, inverse = operator_parts(halves[t], beside)
            for n, weight in enumerate(weights):
                g2[n, x - 1, t] = weight
            inv2[x, t] = inverse

    for copy in halo_b1:
        copy.wait()
    for side, at in ((0, 5), (1, 13)):

        @pl.when((gx > 0) if side == 0 else (gx < nx - 1))
        def _(side=side, at=at):
            for n in range(2):
                for q in range(2):
                    b1[at + n, q, core, WL, :] = b1[at + n, q, core, WL, :] + stg[side, n, q, WL, :]

    @pl.loop(1, 19)
    def _(x):
        for q in range(2):
            x1L[x, q, core, WL, :] = b1[x, q, core, WL, :] * x0L[x, q, core, WL, :]

    copy = send(x1L.at[1:19, :, core, 8:40], x1L.at[1:19, :, core, 8:40], sibling)
    copy.wait()

    def sum_mid(ref, x):
        z_list = z_mid(ref, x)
        return {
            (q, t): gL[0, x - 1, q, t] * ref[x - 1, q, t, WL, :]
            + gL[1, x - 1, q, t] * ref[x + 1, q, t, WL, :]
            + gL[2, x - 1, q, t] * ref[x, q, t, UL, :]
            + gL[3, x - 1, q, t] * ref[x, q, t, DL, :]
            + gL[4, x - 1, q, t] * z_list[q][0][t]
            + gL[5, x - 1, q, t] * z_list[q][1][t]
            for q in range(2)
            for t in range(2)
        }

    def sweep_mid(target, source, first, last, formula):
        def body(x):
            results = {at: formula(x, *at, total) for at, total in sum_mid(source, x).items()}

            def store_all():
                for (q, t), value in results.items():
                    target[x, q, t, WL, :] = value

            return store_all

        planes(first, last, 2, body)

    sweep_mid(
        x2L, x1L, 2, 18, lambda x, q, t, total: first * x1L[x, q, t, WL, :] + GAIN * total
    )
    sweep_mid(
        xpL, x2L, 5, 15,
        lambda x, q, t, total: dL[x, q, t] * (THETA * x1L[x, q, t, WL, :] - x2L[x, q, t, WL, :] + total),
    )

    lane8 = lanes(8)

    @pl.loop(0, 4)
    def _(i):
        coarse = []
        for q in range(2):
            halves = []
            for t in range(2):
                tL[0, q, t, WL, :] = 0.125 * (
                    xpL[2 * i + 5, q, t, WL, :]
                    + 3.0 * (xpL[2 * i + 6, q, t, WL, :] + xpL[2 * i + 7, q, t, WL, :])
                    + xpL[2 * i + 8, q, t, WL, :]
                )
                part = [tL[0, q, t, pl.ds(s, 8, stride=2), :] for s in (15, 16, 17, 18)]
                halves.append(0.125 * (part[0] + 3.0 * (part[1] + part[2]) + part[3]))
            coarse.append(halves)
        low, high = before_pair(coarse[1], lane8), after_pair(coarse[0], lane8)
        pair = [0.125 * (low[t] + 3.0 * (coarse[0][t] + coarse[1][t]) + high[t]) for t in range(2)]
        mine = jnp.where(core == 0, pair[0], pair[1])
        bd2[i + 8, core, 16:24, :] = mine * inv2[i + 8, core, 8:16, :]

    halo_b2 = [
        send(
            bd2.at[8:12, core, 16:24],
            bd2.at[8 - 4 * dx : 12 - 4 * dx, core, 16 - 8 * dy : 24 - 8 * dy],
            peer(dx, dy),
        )
        for dx, dy in peers14
    ]
    for copy in halo_b2:
        copy.wait()
    copy = send(bd2.at[:, core, 8:32], bd2.at[:, core, 8:32], sibling)
    copy.wait()

    @pl.loop(0, 20)
    def _(x):
        for t in range(2):
            scaled = jnp.where(c2[x, t, W2, :] > 0.0, bd2[x, t, W2, :], 0.0)
            bd2[x, t, W2, :] = scaled
            d2[x, t] = scaled * (1.0 / THETA_LOW)
            xa[x, t, W2, :] = scaled * (1.0 / THETA_LOW)

    now, later = xa, xb
    for number, (mom, gain) in enumerate(STEPS_LOW):

        def body(x, now=now, later=later, mom=mom, gain=gain):
            halves = [now[x, t, W2, :] for t in range(2)]
            low, high = before_pair(halves, lane24), after_pair(halves, lane24)
            steps = []
            for t in range(2):
                total = (
                    g2[0, x - 1, t] * now[x - 1, t, W2, :]
                    + g2[1, x - 1, t] * now[x + 1, t, W2, :]
                    + g2[2, x - 1, t] * now[x, t, U2, :]
                    + g2[3, x - 1, t] * now[x, t, D2, :]
                    + g2[4, x - 1, t] * low[t]
                    + g2[5, x - 1, t] * high[t]
                )
                steps.append(mom * d2[x, t] + gain * (bd2[x, t, W2, :] - halves[t] + total))

            def store_all():
                for t in range(2):
                    d2[x, t] = steps[t]
                    later[x, t, W2, :] = halves[t] + steps[t]

            return store_all

        planes(number + 1, 19 - number, 4, body)
        now, later = later, now
    bottom = now

    @pl.loop(0, 8)
    def _(i):
        for odd in range(2):
            x = 2 * i + 2 + odd
            mixed = [
                0.75 * bottom[i + 6, t, W2, :] + 0.25 * bottom[i + 5 + 2 * odd, t, W2, :]
                for t in range(2)
            ]
            low, high = before_pair(mixed, lane24), after_pair(mixed, lane24)
            for q, side in ((0, low), (1, high)):
                for t in range(2):
                    t3[q, t, W2, :] = 0.75 * mixed[t] + 0.25 * side[t]
                    centre = 0.75 * t3[q, t, 12:28, :]
                    x0L[x, q, t, pl.ds(8, 16, stride=2), :] = centre + 0.25 * t3[q, t, 11:27, :]
                    x0L[x, q, t, pl.ds(9, 16, stride=2), :] = centre + 0.25 * t3[q, t, 13:29, :]
                    x0L[x, q, t, WL, :] = jnp.where(
                        c1[x, q, t, WL, :] > 0.0, x2L[x, q, t, WL, :] + x0L[x, q, t, WL, :], 0.0
                    )

    def post_first(x, q, t, total):
        start = x0L[x, q, t, WL, :]
        return start + (THETA * x1L[x, q, t, WL, :] - start + total) * (1.0 / THETA)

    def post_second(x, q, t, total):
        here = xpL[x, q, t, WL, :]
        return (
            here
            + MOM * (here - x0L[x, q, t, WL, :])
            + GAIN * (THETA * x1L[x, q, t, WL, :] - here + total)
        )

    sweep_mid(xpL, x0L, 3, 17, post_first)
    sweep_mid(x2L, xpL, 4, 16, post_second)

    for copy in far:
        copy.wait()
    has_left = jnp.where(core == 1, 1.0, 0.0)
    has_right = jnp.where(core == 0, 1.0, 0.0)

    @pl.loop(0, 10)
    def _(i):
        for odd in range(2):
            x = 2 * i + 1 + odd

            def mixed(q, t):
                return 0.75 * x2L[i + 5, q, t, WL, :] + 0.25 * x2L[i + 4 + 2 * odd, q, t, WL, :]

            m0, m1 = mixed(0, core), mixed(1, core)
            before = roll_up(jnp.where(lane32 == 127, has_left * mixed(1, other), m1))
            after = roll_down(jnp.where(lane32 == 0, has_right * mixed(0, other), m0))
            fine = [
                0.75 * m0 + 0.25 * before, 0.75 * m0 + 0.25 * m1,
                0.75 * m1 + 0.25 * m0, 0.75 * m1 + 0.25 * after,
            ]
            for k in range(4):
                tL[0, k // 2, k % 2, WL, :] = fine[k]
                centre = 0.75 * tL[0, k // 2, k % 2, 14:34, :]
                cF[x, k, pl.ds(8, 20, stride=2), :] = centre + 0.25 * tL[0, k // 2, k % 2, 13:33, :]
                cF[x, k, pl.ds(9, 20, stride=2), :] = centre + 0.25 * tL[0, k // 2, k % 2, 15:35, :]
                cF[x, k, WIN, :] = cF[x, k, WIN, :] + x2F[x, k, WIN, :]

    def last_first(x, k, total):
        start = cF[x, k, WIN, :]
        return start + (THETA * xF[x, k, WIN, :] - start + total) * (1.0 / THETA)

    def last_second(x, k, total):
        here = rF[x, k, WIN, :]
        return (
            here
            + MOM * (here - cF[x, k, WIN, :])
            + GAIN * (THETA * xF[x, k, WIN, :] - here + total)
        )

    copy = swap(cF, e1, 2, 20, WIN)
    sweep_fine(rF, cF, e1, 2, 20, INNER, last_first)
    copy.wait()
    sweep_fine(rF, cF, e1, 2, 20, OUTER, last_first)
    copy = swap(rF, e2, 3, 19, WIN)
    sweep_fine(x2F, rF, e2, 3, 19, INNER, last_second)
    copy.wait()
    sweep_fine(x2F, rF, e2, 3, 19, OUTER, last_second)

    @pl.loop(0, 2)
    def _(half):
        total = None
        for k in range(4):
            rows = x2F[pl.ds(half * 8 + 3, 8), k, 12:44, :].reshape(256, 128)
            high = rows.astype(BF16)
            low = (rows - high.astype(F32)).astype(BF16)
            table = perm[:, k * 128 : (k + 1) * 128]
            for part in (high, low):
                product = lax.dot_general(part, table, (((1,), (1,)), ((), ())), preferred_element_type=F32)
                total = product if total is None else total + product
        out_vm[pl.ds(half * 8, 8)] = total.reshape(8, 32, 512)

    store = pltpu.make_async_copy(out_vm, out_hbm, local_sem.at[2])
    store.start()
    store.wait()


def local(right_side, coefficient):
    def vmem(*shape):
        return pltpu.VMEM(shape, F32)

    inputs, fine, mid, low = (22, 4, 48, 128), (22, 4, 56, 128), (20, 2, 2, 48, 128), (20, 2, 40, 128)
    edge = (22, 2, 48, 128)
    scratch = [
        vmem(16, 32, 512), vmem(16, 32, 512), vmem(16, 32, 512), pltpu.VMEM((512, 512), BF16),
        vmem(*fine), vmem(*inputs), vmem(*fine), vmem(*fine), vmem(22, 4, 40, 128), vmem(*fine), vmem(6, 20, 4, 40, 128),
        vmem(*edge), vmem(*edge), vmem(*edge),
        vmem(2, 16, 4, 8, 128), vmem(2, 22, 4, 8, 128),
        vmem(10, 4, 48, 128), vmem(10, 4, 16, 128), vmem(10, 2, 16, 128),
        vmem(*mid), vmem(*mid), vmem(*mid), vmem(*mid), vmem(*mid), vmem(*mid), vmem(20, 2, 2, 32, 128),
        vmem(6, 18, 2, 2, 32, 128), vmem(2, 2, 2, 48, 128), vmem(1, 2, 2, 48, 128),
        vmem(*low), vmem(*low), vmem(*low), vmem(*low), vmem(20, 2, 24, 128), vmem(20, 2, 24, 128),
        vmem(6, 18, 2, 24, 128), vmem(2, 2, 40, 128),
        pltpu.SemaphoreType.DMA((3,)), pltpu.SemaphoreType.DMA((80,)), pltpu.SemaphoreType.DMA((80,)),
    ]
    return pl.pallas_call(
        kernel,
        out_shape=jax.ShapeDtypeStruct((16, 32, 512), F32),
        in_specs=[pl.BlockSpec(memory_space=pl.ANY)] * 2,
        out_specs=pl.BlockSpec(memory_space=pl.ANY),
        scratch_shapes=scratch,
        compiler_params=pltpu.CompilerParams(
            collective_id=0, has_side_effects=True, vmem_limit_bytes=63 * 2**20
        ),
    )(right_side, coefficient)


def solution(mesh):
    return jax.shard_map(
        local,
        mesh=mesh,
        in_specs=(P("gx", "gy", "gz"), P("gx", "gy", "gz")),
        out_specs=P("gx", "gy", "gz"),
        check_vma=False,
    )
```

```python
import functools

import jax
import jax.numpy as jnp
from jax import lax
from jax.experimental import pallas as pl
from jax.experimental.pallas import tpu as pltpu
from jax.sharding import PartitionSpec as P

MESH = pl.DeviceIdType.MESH
F32 = jnp.float32
BF16 = jnp.bfloat16


def cheb_constants(sweeps, lower_edge, upper_edge):
    theta = 0.5 * (upper_edge + lower_edge)
    delta = 0.5 * (upper_edge - lower_edge)
    sigma = theta / delta
    rho = 1.0 / sigma
    steps = []
    for _ in range(1, sweeps):
        rho_next = 1.0 / (2.0 * sigma - rho)
        steps.append((rho_next * rho, 2.0 * rho_next / delta))
        rho = rho_next
    return theta, steps


THETA, ((MOM, GAIN),) = cheb_constants(2, 0.3, 2.0)
THETA_LOW, STEPS_LOW = cheb_constants(6, 0.05, 2.0)


def lanes(rows):
    return lax.broadcasted_iota(jnp.int32, (rows, 128), 1)


def roll_up(value):
    return pltpu.roll(value, 1, 1)


def roll_down(value):
    return pltpu.roll(value, 127, 1)


def operator_parts(centre, beside):
    faces = []
    diagonal = None
    for other in beside:
        face = jnp.where(other > 0.0, 0.5 * (centre + other), centre)
        diagonal = face if diagonal is None else diagonal + face
        faces.append(jnp.where(other > 0.0, face, 0.0))
    inside = centre > 0.0
    inverse = jnp.where(inside, 1.0 / diagonal, 0.0)
    diagonal = jnp.where(inside, diagonal, 0.0)
    return [face * inverse for face in faces], diagonal, inverse


def kernel(
    b_hbm, c_hbm, out_hbm,
    out_vm, b_in, c_in, perm,
    cF, bF, xF, x2F, dF, rF, gF, eC, e1, e2, face_c_in, face_b_in, pk_out, pk_in, pk,
    t1, t2, e3,
    c1, b1, x1L, x2L, x0L, xpL, dL, gL, stg, tL,
    c2, bd2, xa, xb, d2, inv2, g2, t3,
    local_sem, ss, rs,
):
    gx, gy, core = lax.axis_index("gx"), lax.axis_index("gy"), lax.axis_index("gz")
    nx, ny = lax.axis_size("gx"), lax.axis_size("gy")
    other = 1 - core
    sibling = (gx, gy, other)
    counter = [0]

    def peer(dx, dy):
        return (lax.rem(gx + dx + nx, nx), lax.rem(gy + dy + ny, ny), core)

    def send(src, dst, device):
        number = counter[0]
        counter[0] += 1
        copy = pltpu.make_async_remote_copy(
            src_ref=src, dst_ref=dst, send_sem=ss.at[number], recv_sem=rs.at[number],
            device_id=device, device_id_type=MESH,
        )
        copy.start()
        return copy

    peers14 = [(dx, dy) for dx in (-2, 2, -1, 1, 0) for dy in (-1, 1, 0) if (dx, dy) != (0, 0)]
    peers8 = [(dx, dy) for dx, dy in peers14 if abs(dx) < 2]
    barrier = pltpu.get_barrier_semaphore()
    for dx, dy in peers8:
        pl.semaphore_signal(barrier, inc=1, device_id=peer(dx, dy), device_id_type=MESH)
    pl.semaphore_signal(barrier, inc=1, device_id=sibling, device_id_type=MESH)
    load_c = pltpu.make_async_copy(c_hbm, c_in, local_sem.at[0])
    load_b = pltpu.make_async_copy(b_hbm, b_in, local_sem.at[1])
    load_c.start()
    load_b.start()
    pl.semaphore_wait(barrier, len(peers8) + 1)
    face_c = [
        send(c_hbm.at[0:3], face_c_in.at[1], peer(-1, 0)),
        send(c_hbm.at[13:16], face_c_in.at[0], peer(1, 0)),
    ]
    face_b = [
        send(b_hbm.at[0:2], face_b_in.at[1], peer(-1, 0)),
        send(b_hbm.at[14:16], face_b_in.at[0], peer(1, 0)),
    ]
    load_c.wait()
    load_b.wait()

    @pl.loop(0, 16)
    def _(x):
        for side, rows in ((0, slice(0, 4)), (1, slice(28, 32))):
            pk_out[side, x, 0:4, :] = c_in[x, rows, :]
            pk_out[side, x, 4:8, :] = b_in[x, rows, :]

    halo = [
        send(pk_out.at[0], pk_in.at[1, 3:19], peer(0, -1)),
        send(pk_out.at[1], pk_in.at[0, 3:19], peer(0, 1)),
        send(pk_out.at[0, 0:3], pk_in.at[1, 19:22], peer(-1, -1)),
        send(pk_out.at[0, 13:16], pk_in.at[1, 0:3], peer(1, -1)),
        send(pk_out.at[1, 0:3], pk_in.at[0, 19:22], peer(-1, 1)),
        send(pk_out.at[1, 13:16], pk_in.at[0, 0:3], peer(1, 1)),
    ]

    @pl.loop(0, 4)
    def _(j):
        z = lax.broadcasted_iota(jnp.int32, (128, 512), 0) + j * 128
        col = lax.broadcasted_iota(jnp.int32, (128, 512), 1)
        perm[pl.ds(pl.multiple_of(j * 128, 128), 128), :] = jnp.where(
            z == 4 * (col % 128) + col // 128, 1.0, 0.0
        ).astype(BF16)

    def spread(rows):
        high = rows.astype(BF16)
        low = (rows - high.astype(F32)).astype(BF16)
        table = perm[...]
        result = jnp.dot(high, table, preferred_element_type=F32) + jnp.dot(
            low, table, preferred_element_type=F32
        )
        return [result[:, k * 128 : (k + 1) * 128] for k in range(4)]

    for source, target in ((c_in, cF), (b_in, bF)):

        @pl.loop(0, 2)
        def _(half, source=source, target=target):
            for k, part in enumerate(spread(source[pl.ds(half * 8, 8)].reshape(256, 512))):
                target[pl.ds(half * 8 + 3, 8), k, 8:40, :] = part.reshape(8, 32, 128)

    @pl.loop(0, 22)
    def _(x):
        for ref in (e1, e2):
            ref[x, core] = jnp.zeros((48, 128), F32)

    @pl.loop(0, 10)
    def _(x):
        e3[x, core] = jnp.zeros((16, 128), F32)

    @pl.loop(0, 3)
    def _(x):
        rF[x, :, 8:48, :] = jnp.zeros((4, 40, 128), F32)
        rF[x + 19, :, 8:48, :] = jnp.zeros((4, 40, 128), F32)

    @pl.loop(0, 8)
    def _(i):
        for k in range(4):
            t1[0, k, 8:40, :] = cF[2 * i + 3, k, 8:40, :] + cF[2 * i + 4, k, 8:40, :]
        for q in range(2):
            total = None
            for k in (2 * q, 2 * q + 1):
                for start in (8, 9):
                    part = t1[0, k, pl.ds(start, 16, stride=2), :]
                    total = part if total is None else total + part
            c1[i + 4, q, core, 16:32, :] = total * (0.125 * 0.25)

    @pl.loop(0, 4)
    def _(i):
        total = None
        for q in range(2):
            tL[0, q, 0, 16:32, :] = c1[2 * i + 4, q, core, 16:32, :] + c1[2 * i + 5, q, core, 16:32, :]
            for start in (16, 17):
                part = tL[0, q, 0, pl.ds(start, 8, stride=2), :]
                total = part if total is None else total + part
        c2[i + 8, core, 16:24, :] = total * (0.125 * 0.25)

    def spread_faces(arrived, target, depth, low, high):
        for side, at in ((0, low), (1, high)):
            for k, part in enumerate(spread(arrived[side].reshape(depth * 32, 512))):
                target[at : at + depth, k, 8:40, :] = part.reshape(depth, 32, 128)

    for copy in face_c:
        copy.wait_recv()
    spread_faces(face_c_in, cF, 3, 0, 19)
    for copy in face_b:
        copy.wait_recv()
    spread_faces(face_b_in, bF, 2, 1, 19)
    for copy in halo:
        copy.wait_recv()
    for side in range(2):
        for k, part in enumerate(spread(pk_in[side].reshape(176, 512))):
            pk[side, :, k, :, :] = part.reshape(22, 8, 128)

    CWIN, CUP, CDOWN = slice(4, 44), slice(3, 43), slice(5, 45)
    WIN, UP, DOWN = slice(8, 48), slice(7, 47), slice(9, 49)

    @pl.loop(0, 22)
    def _(x):
        for k in range(4):
            cF[x, k, 4:8, :] = pk[0, x, k, 0:4, :]
            bF[x, k, 4:8, :] = pk[0, x, k, 4:8, :]
            cF[x, k, 40:44, :] = pk[1, x, k, 0:4, :]
            bF[x, k, 40:44, :] = pk[1, x, k, 4:8, :]

    def clear_planes(ref, first, count, condition):
        @pl.when(condition)
        def _():
            @pl.loop(first, first + count)
            def _(x):
                if ref.shape[1] == 4:
                    ref[x, :, 0:48, :] = jnp.zeros((4, 48, 128), F32)
                elif len(ref.shape) == 5:
                    for q in range(2):
                        ref[x, q, core] = jnp.zeros(ref.shape[3:], F32)
                else:
                    ref[x, core] = jnp.zeros(ref.shape[2:], F32)

    def clear_rows(ref, first, count, condition):
        zero = jnp.zeros((count, 128), F32)

        @pl.when(condition)
        def _():
            @pl.loop(0, ref.shape[0])
            def _(x):
                if ref.shape[1] == 4:
                    for k in range(4):
                        ref[x, k, first : first + count, :] = zero
                elif len(ref.shape) == 5:
                    for q in range(2):
                        ref[x, q, core, first : first + count, :] = zero
                else:
                    ref[x, core, first : first + count, :] = zero

    for ghost, cell, condition in ((2, 3, gx == 0), (19, 18, gx == nx - 1)):

        @pl.when(condition)
        def _(ghost=ghost, cell=cell):
            cF[ghost] = cF[cell]

    for ghost, cell, condition in ((7, 8, gy == 0), (40, 39, gy == ny - 1)):

        @pl.when(condition)
        def _(ghost=ghost, cell=cell):
            @pl.loop(0, 22)
            def _(x):
                for k in range(4):
                    cF[x, k, ghost : ghost + 1, :] = cF[x, k, cell : cell + 1, :]

    @pl.loop(1, 21)
    def _(x):
        low = roll_down(cF[x, 0, CWIN, :])
        high = roll_up(cF[x, 3, CWIN, :])
        eC[x, core, CWIN, :] = jnp.where(core == 0, low, high)

    edge_phase = 3 * other

    def swap(source, target, first, last, rows):
        return send(
            source.at[first:last, edge_phase, rows], target.at[first:last, core, rows], sibling
        )

    lane40 = lanes(40)

    def left_of(ref, edge, x, k, win):
        if k:
            return ref[x, k - 1, win, :]
        return roll_up(jnp.where(lane40 == 127, edge[x, 0, win, :], ref[x, 3, win, :]))

    def right_of(ref, edge, x, k, win):
        if k < 3:
            return ref[x, k + 1, win, :]
        return roll_down(jnp.where(lane40 == 0, edge[x, 1, win, :], ref[x, 0, win, :]))

    def planes(first, last, group, body):
        count = last - first

        @pl.loop(0, count // group)
        def _(j):
            for store_all in [body(first + j * group + u) for u in range(group)]:
                store_all()

        for store_all in [body(last - 1 - u) for u in range(count % group)]:
            store_all()

    INNER, OUTER = (1, 2), (0, 3)

    def setup_fine(phases):
        def body(x):
            results = []
            for k in phases:
                beside = [
                    cF[x - 1, k, CWIN, :], cF[x + 1, k, CWIN, :], cF[x, k, CUP, :], cF[x, k, CDOWN, :],
                    left_of(cF, eC, x, k, CWIN), right_of(cF, eC, x, k, CWIN),
                ]
                centre = cF[x, k, CWIN, :]
                pairs = [centre + value for value in beside]
                twice = ((pairs[0] + pairs[1]) + (pairs[2] + pairs[3])) + (pairs[4] + pairs[5])
                inverse = 1.0 / twice
                weights = [pair * inverse for pair in pairs]
                results.append((k, weights, 0.5 * twice, bF[x, k, CWIN, :] * inverse * (2.0 / THETA)))

            def store_all():
                for k, weights, diagonal, iterate in results:
                    for n, weight in enumerate(weights):
                        gF[n, x - 1, k] = weight
                    dF[x, k] = diagonal
                    xF[x, k, WIN, :] = iterate

            return store_all

        planes(1, 21, 2, body)

    def sum_fine(ref, edge, x, k):
        return (
            gF[0, x - 1, k] * ref[x - 1, k, WIN, :]
            + gF[1, x - 1, k] * ref[x + 1, k, WIN, :]
            + gF[2, x - 1, k] * ref[x, k, UP, :]
            + gF[3, x - 1, k] * ref[x, k, DOWN, :]
            + gF[4, x - 1, k] * left_of(ref, edge, x, k, WIN)
            + gF[5, x - 1, k] * right_of(ref, edge, x, k, WIN)
        )

    def sweep_fine(target, source, edge, first, last, phases, formula):
        def body(x):
            results = [(k, formula(x, k, sum_fine(source, edge, x, k))) for k in phases]

            def store_all():
                for k, value in results:
                    target[x, k, WIN, :] = value

            return store_all

        planes(first, last, 3, body)

    first = 1.0 + MOM + GAIN * (THETA - 1.0)

    def pre_step(x, k, total):
        return first * xF[x, k, WIN, :] + GAIN * total

    def residual(x, k, total):
        return dF[x, k] * (THETA * xF[x, k, WIN, :] - x2F[x, k, WIN, :] + total)

    copy = swap(cF, eC, 1, 21, slice(0, 48))
    rows_of = {0: (slice(16, 32), slice(16, 32)), -1: (slice(16, 24), slice(32, 40)), 1: (slice(24, 32), slice(8, 16))}
    planes_c1 = {0: (slice(4, 12), slice(4, 12)), -1: (slice(4, 8), slice(12, 16)), 1: (slice(8, 12), slice(0, 4))}
    halo_c1 = []
    for dx, dy in peers8:
        (xs, xd), (ys, yd) = planes_c1[dx], rows_of[dy]
        halo_c1.append(send(c1.at[xs, :, core, ys], c1.at[xd, :, core, yd], peer(dx, dy)))
    halo_c2 = [
        send(
            c2.at[8:12, core, 16:24],
            c2.at[8 - 4 * dx : 12 - 4 * dx, core, 16 - 8 * dy : 24 - 8 * dy],
            peer(dx, dy),
        )
        for dx, dy in peers14
    ]

    setup_fine(INNER)
    copy.wait()
    setup_fine(OUTER)
    for n, plane, condition in ((0, 2, gx == 0), (1, 17, gx == nx - 1)):

        @pl.when(condition)
        def _(n=n, plane=plane):
            gF[n, plane] = jnp.zeros((4, 40, 128), F32)

    for n, row, condition in ((2, 4, gy == 0), (3, 35, gy == ny - 1)):

        @pl.when(condition)
        def _(n=n, row=row):
            @pl.loop(1, 19)
            def _(x):
                for k in range(4):
                    gF[n, x, k, row : row + 1, :] = jnp.zeros((1, 128), F32)

    copy = swap(xF, e1, 2, 20, WIN)
    sweep_fine(x2F, xF, e1, 2, 20, INNER, pre_step)
    copy.wait()
    sweep_fine(x2F, xF, e1, 2, 20, OUTER, pre_step)
    copy = swap(x2F, e2, 3, 19, WIN)
    sweep_fine(rF, x2F, e2, 3, 19, INNER, residual)
    copy.wait()
    sweep_fine(rF, x2F, e2, 3, 19, OUTER, residual)

    for row, condition in ((8, gy == 0), (44, gy == ny - 1)):

        @pl.when(condition)
        def _(row=row):
            @pl.loop(3, 19)
            def _(x):
                for k in range(4):
                    rF[x, k, row : row + 4, :] = jnp.zeros((4, 128), F32)

    def restrict_x(i):
        results = [
            0.125
            * (
                rF[2 * i, k, WIN, :]
                + 3.0 * (rF[2 * i + 1, k, WIN, :] + rF[2 * i + 2, k, WIN, :])
                + rF[2 * i + 3, k, WIN, :]
            )
            for k in range(4)
        ]

        def store_all():
            for k in range(4):
                t1[i, k, WIN, :] = results[k]

        return store_all

    def restrict_y(i):
        results = []
        for k in range(4):
            part = [t1[i, k, pl.ds(s, 16, stride=2), :] for s in (11, 12, 13, 14)]
            results.append(0.125 * (part[0] + 3.0 * (part[1] + part[2]) + part[3]))

        def store_all():
            for k in range(4):
                t2[i, k] = results[k]

        return store_all

    planes(0, 10, 2, restrict_x)
    planes(0, 10, 2, restrict_y)

    copy = send(t2.at[:, edge_phase], e3.at[:, core], sibling)
    copy.wait()
    lane16 = lanes(16)

    @pl.loop(0, 10)
    def _(i):
        p = [t2[i, k] for k in range(4)]
        before = roll_up(jnp.where(lane16 == 127, e3[i, 0], p[3]))
        after = roll_down(jnp.where(lane16 == 0, e3[i, 1], p[0]))
        b1[i + 3, 0, core, 16:32, :] = 0.125 * (before + 3.0 * (p[0] + p[1]) + p[2])
        b1[i + 3, 1, core, 16:32, :] = 0.125 * (p[1] + 3.0 * (p[2] + p[3]) + after)

    halo_b1 = []
    for dx, dy in peers8:
        ys, yd = rows_of[dy]
        if dx == 0:
            halo_b1.append(send(b1.at[3:13, :, core, ys], b1.at[3:13, :, core, yd], peer(dx, dy)))
        else:
            xs, xd, near, side = (
                (slice(9, 11), slice(1, 3), slice(11, 13), 0)
                if dx == 1
                else (slice(5, 7), slice(13, 15), slice(3, 5), 1)
            )
            halo_b1.append(send(b1.at[near, :, core, ys], stg.at[side, :, :, yd], peer(dx, dy)))
            halo_b1.append(send(b1.at[xs, :, core, ys], b1.at[xd, :, core, yd], peer(dx, dy)))

    far = [
        send(x2F.at[17:18, :, WIN], x2F.at[1:2, :, WIN], peer(1, 0)),
        send(x2F.at[4:5, :, WIN], x2F.at[20:21, :, WIN], peer(-1, 0)),
    ]

    for copy in face_c + face_b + halo:
        copy.wait_send()
    for copy in halo_c1 + halo_c2:
        copy.wait()
    clear_planes(c1, 0, 4, gx == 0)
    clear_planes(c1, 12, 4, gx == nx - 1)
    clear_rows(c1, 8, 8, gy == 0)
    clear_rows(c1, 32, 8, gy == ny - 1)
    clear_planes(c2, 4, 4, gx == 0)
    clear_planes(c2, 0, 4, gx <= 1)
    clear_planes(c2, 12, 4, gx == nx - 1)
    clear_planes(c2, 16, 4, gx >= nx - 2)
    clear_rows(c2, 8, 8, gy == 0)
    clear_rows(c2, 24, 8, gy == ny - 1)
    hand = [
        send(c1.at[:, :, core, 8:40], c1.at[:, :, core, 8:40], sibling),
        send(c2.at[:, core, 8:32], c2.at[:, core, 8:32], sibling),
    ]
    for copy in hand:
        copy.wait()

    lane32, lane24 = lanes(32), lanes(24)
    WL, UL, DL = slice(8, 40), slice(7, 39), slice(9, 41)
    W2, U2, D2 = slice(8, 32), slice(7, 31), slice(9, 33)

    def before_pair(halves, lane):
        turned = [roll_up(half) for half in halves]
        return [jnp.where(lane == 0, 0.0, turned[0]), jnp.where(lane == 0, turned[0], turned[1])]

    def after_pair(halves, lane):
        turned = [roll_down(half) for half in halves]
        return [jnp.where(lane == 127, turned[1], turned[0]), jnp.where(lane == 127, 0.0, turned[1])]

    def z_mid(ref, x):
        p0 = [ref[x, 0, t, WL, :] for t in range(2)]
        p1 = [ref[x, 1, t, WL, :] for t in range(2)]
        return [(before_pair(p1, lane32), p1), (p0, after_pair(p0, lane32))]

    @pl.loop(1, 15)
    def _(x):
        z_list = z_mid(c1, x)
        for q in range(2):
            for t in range(2):
                beside = [
                    c1[x - 1, q, t, WL, :], c1[x + 1, q, t, WL, :], c1[x, q, t, UL, :], c1[x, q, t, DL, :],
                    z_list[q][0][t], z_list[q][1][t],
                ]
                weights, diagonal, inverse = operator_parts(c1[x, q, t, WL, :], beside)
                for n, weight in enumerate(weights):
                    gL[n, x - 1, q, t] = weight
                dL[x, q, t] = diagonal
                x0L[x, q, t, WL, :] = inverse * (1.0 / THETA)

    def setup_low(first, last):
        @pl.loop(first, last)
        def _(x):
            halves = [c2[x, t, W2, :] for t in range(2)]
            low, high = before_pair(halves, lane24), after_pair(halves, lane24)
            for t in range(2):
                beside = [
                    c2[x - 1, t, W2, :], c2[x + 1, t, W2, :], c2[x, t, U2, :], c2[x, t, D2, :], low[t], high[t],
                ]
                weights, _, inverse = operator_parts(halves[t], beside)
                for n, weight in enumerate(weights):
                    g2[n, x - 1, t] = weight
                inv2[x, t] = inverse

    setup_low(8, 12)

    def scale_mid(first, last):
        @pl.loop(first, last)
        def _(x):
            for q in range(2):
                x1L[x, q, core, WL, :] = b1[x, q, core, WL, :] * x0L[x, q, core, WL, :]

        return send(
            x1L.at[first:last, :, core, 8:40], x1L.at[first:last, :, core, 8:40], sibling
        )

    for copy in halo_b1[-2:]:
        copy.wait()
    handed = [scale_mid(5, 11)]
    for copy in halo_b1[:-2]:
        copy.wait()
    for side, at in ((0, 3), (1, 11)):

        @pl.when((gx > 0) if side == 0 else (gx < nx - 1))
        def _(side=side, at=at):
            for n in range(2):
                for q in range(2):
                    b1[at + n, q, core, WL, :] = b1[at + n, q, core, WL, :] + stg[side, n, q, WL, :]

    handed += [scale_mid(1, 5), scale_mid(11, 15)]
    for copy in handed:
        copy.wait()

    def sum_mid(ref, x):
        z_list = z_mid(ref, x)
        return {
            (q, t): gL[0, x - 1, q, t] * ref[x - 1, q, t, WL, :]
            + gL[1, x - 1, q, t] * ref[x + 1, q, t, WL, :]
            + gL[2, x - 1, q, t] * ref[x, q, t, UL, :]
            + gL[3, x - 1, q, t] * ref[x, q, t, DL, :]
            + gL[4, x - 1, q, t] * z_list[q][0][t]
            + gL[5, x - 1, q, t] * z_list[q][1][t]
            for q in range(2)
            for t in range(2)
        }

    def sweep_mid(target, source, first, last, formula):
        def body(x):
            results = {at: formula(x, *at, total) for at, total in sum_mid(source, x).items()}

            def store_all():
                for (q, t), value in results.items():
                    target[x, q, t, WL, :] = value

            return store_all

        planes(first, last, 2, body)

    sweep_mid(
        x2L, x1L, 2, 14, lambda x, q, t, total: first * x1L[x, q, t, WL, :] + GAIN * total
    )
    sweep_mid(
        xpL, x2L, 3, 13,
        lambda x, q, t, total: dL[x, q, t] * (THETA * x1L[x, q, t, WL, :] - x2L[x, q, t, WL, :] + total),
    )

    lane8 = lanes(8)

    @pl.loop(0, 4)
    def _(i):
        coarse = []
        for q in range(2):
            halves = []
            for t in range(2):
                tL[0, q, t, WL, :] = 0.125 * (
                    xpL[2 * i + 3, q, t, WL, :]
                    + 3.0 * (xpL[2 * i + 4, q, t, WL, :] + xpL[2 * i + 5, q, t, WL, :])
                    + xpL[2 * i + 6, q, t, WL, :]
                )
                part = [tL[0, q, t, pl.ds(s, 8, stride=2), :] for s in (15, 16, 17, 18)]
                halves.append(0.125 * (part[0] + 3.0 * (part[1] + part[2]) + part[3]))
            coarse.append(halves)
        low, high = before_pair(coarse[1], lane8), after_pair(coarse[0], lane8)
        pair = [0.125 * (low[t] + 3.0 * (coarse[0][t] + coarse[1][t]) + high[t]) for t in range(2)]
        mine = jnp.where(core == 0, pair[0], pair[1])
        bd2[i + 8, core, 16:24, :] = mine * inv2[i + 8, core, 8:16, :]

    halo_b2 = [
        send(
            bd2.at[8:12, core, 16:24],
            bd2.at[8 - 4 * dx : 12 - 4 * dx, core, 16 - 8 * dy : 24 - 8 * dy],
            peer(dx, dy),
        )
        for dx, dy in peers14
    ]
    far_mid = [
        send(x2L.at[8:10, :, :, 8:40], x2L.at[0:2, :, :, 8:40], peer(1, 0)),
        send(x2L.at[6:8, :, :, 8:40], x2L.at[14:16, :, :, 8:40], peer(-1, 0)),
    ]
    setup_low(1, 8)
    setup_low(12, 19)
    handed = []
    for group in (0, 1, 2):
        for (dx, dy), copy in zip(peers14, halo_b2):
            if abs(dx) == group:
                copy.wait()
        for at in sorted({8 - 4 * group, 8 + 4 * group}):
            block = bd2.at[at : at + 4, core, 8:32]
            handed.append(send(block, block, sibling))
    for copy in handed:
        copy.wait()

    @pl.loop(0, 20)
    def _(x):
        for t in range(2):
            scaled = jnp.where(c2[x, t, W2, :] > 0.0, bd2[x, t, W2, :], 0.0)
            bd2[x, t, W2, :] = scaled
            d2[x, t] = scaled * (1.0 / THETA_LOW)
            xa[x, t, W2, :] = scaled * (1.0 / THETA_LOW)

    now, later = xa, xb
    for number, (mom, gain) in enumerate(STEPS_LOW):

        def body(x, now=now, later=later, mom=mom, gain=gain):
            halves = [now[x, t, W2, :] for t in range(2)]
            low, high = before_pair(halves, lane24), after_pair(halves, lane24)
            steps = []
            for t in range(2):
                total = (
                    g2[0, x - 1, t] * now[x - 1, t, W2, :]
                    + g2[1, x - 1, t] * now[x + 1, t, W2, :]
                    + g2[2, x - 1, t] * now[x, t, U2, :]
                    + g2[3, x - 1, t] * now[x, t, D2, :]
                    + g2[4, x - 1, t] * low[t]
                    + g2[5, x - 1, t] * high[t]
                )
                steps.append(mom * d2[x, t] + gain * (bd2[x, t, W2, :] - halves[t] + total))

            def store_all():
                for t in range(2):
                    d2[x, t] = steps[t]
                    later[x, t, W2, :] = halves[t] + steps[t]

            return store_all

        planes(number + 1, 19 - number, 4, body)
        now, later = later, now
    bottom = now

    for copy in far_mid:
        copy.wait()

    @pl.loop(0, 8)
    def _(i):
        for odd in range(2):
            x = 2 * i + odd
            mixed = [
                0.75 * bottom[i + 6, t, W2, :] + 0.25 * bottom[i + 5 + 2 * odd, t, W2, :]
                for t in range(2)
            ]
            low, high = before_pair(mixed, lane24), after_pair(mixed, lane24)
            for q, side in ((0, low), (1, high)):
                for t in range(2):
                    t3[odd, q, t, W2, :] = 0.75 * mixed[t] + 0.25 * side[t]
                    centre = 0.75 * t3[odd, q, t, 12:28, :]
                    x0L[x, q, t, pl.ds(8, 16, stride=2), :] = centre + 0.25 * t3[odd, q, t, 11:27, :]
                    x0L[x, q, t, pl.ds(9, 16, stride=2), :] = centre + 0.25 * t3[odd, q, t, 13:29, :]
                    x0L[x, q, t, WL, :] = jnp.where(
                        c1[x, q, t, WL, :] > 0.0, x2L[x, q, t, WL, :] + x0L[x, q, t, WL, :], 0.0
                    )

    def post_first(x, q, t, total):
        start = x0L[x, q, t, WL, :]
        return start + (THETA * x1L[x, q, t, WL, :] - start + total) * (1.0 / THETA)

    def post_second(x, q, t, total):
        here = xpL[x, q, t, WL, :]
        return (
            here
            + MOM * (here - x0L[x, q, t, WL, :])
            + GAIN * (THETA * x1L[x, q, t, WL, :] - here + total)
        )

    sweep_mid(xpL, x0L, 1, 15, post_first)
    sweep_mid(x2L, xpL, 2, 14, post_second)

    for copy in far:
        copy.wait()
    has_left = jnp.where(core == 1, 1.0, 0.0)
    has_right = jnp.where(core == 0, 1.0, 0.0)

    @pl.loop(0, 10)
    def _(i):
        for odd in range(2):
            x = 2 * i + 1 + odd

            def mixed(q, t):
                return 0.75 * x2L[i + 3, q, t, WL, :] + 0.25 * x2L[i + 2 + 2 * odd, q, t, WL, :]

            m0, m1 = mixed(0, core), mixed(1, core)
            before = roll_up(jnp.where(lane32 == 127, has_left * mixed(1, other), m1))
            after = roll_down(jnp.where(lane32 == 0, has_right * mixed(0, other), m0))
            fine = [
                0.75 * m0 + 0.25 * before, 0.75 * m0 + 0.25 * m1,
                0.75 * m1 + 0.25 * m0, 0.75 * m1 + 0.25 * after,
            ]
            for k in range(4):
                tL[odd, k // 2, k % 2, WL, :] = fine[k]
                centre = 0.75 * tL[odd, k // 2, k % 2, 14:34, :]
                cF[x, k, pl.ds(8, 20, stride=2), :] = centre + 0.25 * tL[odd, k // 2, k % 2, 13:33, :]
                cF[x, k, pl.ds(9, 20, stride=2), :] = centre + 0.25 * tL[odd, k // 2, k % 2, 15:35, :]
                cF[x, k, WIN, :] = cF[x, k, WIN, :] + x2F[x, k, WIN, :]

    def last_first(x, k, total):
        start = cF[x, k, WIN, :]
        return start + (THETA * xF[x, k, WIN, :] - start + total) * (1.0 / THETA)

    def last_second(x, k, total):
        here = rF[x, k, WIN, :]
        return (
            here
            + MOM * (here - cF[x, k, WIN, :])
            + GAIN * (THETA * xF[x, k, WIN, :] - here + total)
        )

    copy = swap(cF, e1, 2, 20, WIN)
    sweep_fine(rF, cF, e1, 2, 20, INNER, last_first)
    copy.wait()
    sweep_fine(rF, cF, e1, 2, 20, OUTER, last_first)
    copy = swap(rF, e2, 3, 19, WIN)
    sweep_fine(x2F, rF, e2, 3, 19, INNER, last_second)
    copy.wait()
    sweep_fine(x2F, rF, e2, 3, 19, OUTER, last_second)

    def store(part):
        planes_of = pl.ds(part * 4, 4)
        return pltpu.make_async_copy(out_vm.at[planes_of], out_hbm.at[planes_of], local_sem.at[2 + part])

    for part in range(4):
        total = None
        for k in range(4):
            rows = x2F[part * 4 + 3 : part * 4 + 7, k, 12:44, :].reshape(128, 128)
            high = rows.astype(BF16)
            low = (rows - high.astype(F32)).astype(BF16)
            table = perm[:, k * 128 : (k + 1) * 128]
            for piece in (high, low):
                product = lax.dot_general(piece, table, (((1,), (1,)), ((), ())), preferred_element_type=F32)
                total = product if total is None else total + product
        out_vm[part * 4 : part * 4 + 4] = total.reshape(4, 32, 512)
        store(part).start()
    for part in range(4):
        store(part).wait()


def copy_kernel(source, target, buffer, read_sem, write_sem):
    reads, writes = [], []
    for n in range(8):
        part = pl.ds(2 * n, 2)
        reads.append(pltpu.make_async_copy(source.at[part], buffer.at[part], read_sem.at[n]))
        writes.append(pltpu.make_async_copy(buffer.at[part], target.at[part], write_sem.at[n]))
    for copy in reads:
        copy.start()
    for copy, after in zip(reads, writes):
        copy.wait()
        after.start()
    for copy in writes:
        copy.wait()


def local(right_side, coefficient):
    def vmem(*shape):
        return pltpu.VMEM(shape, F32)

    inputs, fine, mid, low = (22, 4, 48, 128), (22, 4, 56, 128), (16, 2, 2, 48, 128), (20, 2, 40, 128)
    edge = (22, 2, 48, 128)
    scratch = [
        vmem(16, 32, 512), vmem(16, 32, 512), vmem(16, 32, 512), pltpu.VMEM((512, 512), BF16),
        vmem(*fine), vmem(*inputs), vmem(*fine), vmem(*fine), vmem(22, 4, 40, 128), vmem(*fine), vmem(6, 20, 4, 40, 128),
        vmem(*edge), vmem(*edge), vmem(*edge),
        vmem(2, 3, 32, 512), vmem(2, 2, 32, 512), vmem(2, 16, 8, 512), vmem(2, 22, 8, 512), vmem(2, 22, 4, 8, 128),
        vmem(10, 4, 48, 128), vmem(10, 4, 16, 128), vmem(10, 2, 16, 128),
        vmem(*mid), vmem(*mid), vmem(*mid), vmem(*mid), vmem(*mid), vmem(*mid), vmem(16, 2, 2, 32, 128),
        vmem(6, 14, 2, 2, 32, 128), vmem(2, 2, 2, 48, 128), vmem(2, 2, 2, 48, 128),
        vmem(*low), vmem(*low), vmem(*low), vmem(*low), vmem(20, 2, 24, 128), vmem(20, 2, 24, 128),
        vmem(6, 18, 2, 24, 128), vmem(2, 2, 2, 40, 128),
        pltpu.SemaphoreType.DMA((6,)), pltpu.SemaphoreType.DMA((80,)), pltpu.SemaphoreType.DMA((80,)),
    ]
    result = pl.pallas_call(
        kernel,
        out_shape=jax.ShapeDtypeStruct((16, 32, 512), F32),
        in_specs=[pl.BlockSpec(memory_space=pl.ANY)] * 2,
        out_specs=pl.BlockSpec(memory_space=pl.ANY),
        scratch_shapes=scratch,
        compiler_params=pltpu.CompilerParams(
            collective_id=0, has_side_effects=True, vmem_limit_bytes=63 * 2**20
        ),
    )(right_side, coefficient)
    return pl.pallas_call(
        copy_kernel,
        out_shape=jax.ShapeDtypeStruct((16, 32, 512), F32),
        in_specs=[pl.BlockSpec(memory_space=pl.ANY)],
        out_specs=pl.BlockSpec(memory_space=pl.ANY),
        scratch_shapes=[vmem(16, 32, 512), pltpu.SemaphoreType.DMA((8,)), pltpu.SemaphoreType.DMA((8,))],
    )(result)


def solution(mesh):
    return jax.shard_map(
        local,
        mesh=mesh,
        in_specs=(P("gx", "gy", "gz"), P("gx", "gy", "gz")),
        out_specs=P("gx", "gy", "gz"),
        check_vma=False,
    )
```

```python
import functools

import jax
import jax.numpy as jnp
from jax import lax
from jax.experimental import pallas as pl
from jax.experimental.pallas import tpu as pltpu
from jax.sharding import PartitionSpec as P

MESH = pl.DeviceIdType.MESH
F32 = jnp.float32
BF16 = jnp.bfloat16


def cheb_constants(sweeps, lower_edge, upper_edge):
    theta = 0.5 * (upper_edge + lower_edge)
    delta = 0.5 * (upper_edge - lower_edge)
    sigma = theta / delta
    rho = 1.0 / sigma
    steps = []
    for _ in range(1, sweeps):
        rho_next = 1.0 / (2.0 * sigma - rho)
        steps.append((rho_next * rho, 2.0 * rho_next / delta))
        rho = rho_next
    return theta, steps


THETA, ((MOM, GAIN),) = cheb_constants(2, 0.3, 2.0)
THETA_LOW, STEPS_LOW = cheb_constants(6, 0.05, 2.0)


def lanes(rows):
    return lax.broadcasted_iota(jnp.int32, (rows, 128), 1)


def roll_up(value):
    return pltpu.roll(value, 1, 1)


def roll_down(value):
    return pltpu.roll(value, 127, 1)


def operator_parts(centre, beside):
    faces = []
    diagonal = None
    for other in beside:
        face = jnp.where(other > 0.0, 0.5 * (centre + other), centre)
        diagonal = face if diagonal is None else diagonal + face
        faces.append(jnp.where(other > 0.0, face, 0.0))
    inside = centre > 0.0
    inverse = jnp.where(inside, 1.0 / diagonal, 0.0)
    diagonal = jnp.where(inside, diagonal, 0.0)
    return [face * inverse for face in faces], diagonal, inverse


def kernel(
    b_hbm, c_hbm, out_hbm,
    out_vm, b_in, c_in, perm,
    cF, bF, xF, x2F, dF, rF, gF, eC, e1, e2, face_c_in, face_b_in, pk_out, pk_in, pk,
    t1, t2, e3,
    c1, b1, x1L, x2L, x0L, xpL, dL, gL, stg, tL,
    c2, bd2, xa, xb, d2, inv2, g2, t3,
    local_sem, ss, rs,
):
    gx, gy, core = lax.axis_index("gx"), lax.axis_index("gy"), lax.axis_index("gz")
    nx, ny = lax.axis_size("gx"), lax.axis_size("gy")
    other = 1 - core
    sibling = (gx, gy, other)
    counter = [0]

    def peer(dx, dy):
        return (lax.rem(gx + dx + nx, nx), lax.rem(gy + dy + ny, ny), core)

    def send(src, dst, device):
        number = counter[0]
        counter[0] += 1
        copy = pltpu.make_async_remote_copy(
            src_ref=src, dst_ref=dst, send_sem=ss.at[number], recv_sem=rs.at[number],
            device_id=device, device_id_type=MESH,
        )
        copy.start()
        return copy

    peers14 = [(dx, dy) for dx in (-2, 2, -1, 1, 0) for dy in (-1, 1, 0) if (dx, dy) != (0, 0)]
    peers8 = [(dx, dy) for dx, dy in peers14 if abs(dx) < 2]
    barrier = pltpu.get_barrier_semaphore()
    for dx, dy in peers8:
        pl.semaphore_signal(barrier, inc=1, device_id=peer(dx, dy), device_id_type=MESH)
    pl.semaphore_signal(barrier, inc=1, device_id=sibling, device_id_type=MESH)
    load_c = pltpu.make_async_copy(c_hbm, c_in, local_sem.at[0])
    load_b = pltpu.make_async_copy(b_hbm, b_in, local_sem.at[1])
    load_c.start()
    load_b.start()
    pl.semaphore_wait(barrier, len(peers8) + 1)
    face_c = [
        send(c_hbm.at[0:3], face_c_in.at[1], peer(-1, 0)),
        send(c_hbm.at[13:16], face_c_in.at[0], peer(1, 0)),
    ]
    face_b = [
        send(b_hbm.at[0:2], face_b_in.at[1], peer(-1, 0)),
        send(b_hbm.at[14:16], face_b_in.at[0], peer(1, 0)),
    ]
    load_c.wait()
    load_b.wait()

    @pl.loop(0, 16)
    def _(x):
        for side, rows in ((0, slice(0, 4)), (1, slice(28, 32))):
            pk_out[side, x, 0:4, :] = c_in[x, rows, :]
            pk_out[side, x, 4:8, :] = b_in[x, rows, :]

    halo = [
        send(pk_out.at[0], pk_in.at[1, 3:19], peer(0, -1)),
        send(pk_out.at[1], pk_in.at[0, 3:19], peer(0, 1)),
        send(pk_out.at[0, 0:3], pk_in.at[1, 19:22], peer(-1, -1)),
        send(pk_out.at[0, 13:16], pk_in.at[1, 0:3], peer(1, -1)),
        send(pk_out.at[1, 0:3], pk_in.at[0, 19:22], peer(-1, 1)),
        send(pk_out.at[1, 13:16], pk_in.at[0, 0:3], peer(1, 1)),
    ]

    @pl.loop(0, 4)
    def _(j):
        z = lax.broadcasted_iota(jnp.int32, (128, 512), 0) + j * 128
        col = lax.broadcasted_iota(jnp.int32, (128, 512), 1)
        perm[pl.ds(pl.multiple_of(j * 128, 128), 128), :] = jnp.where(
            z == 4 * (col % 128) + col // 128, 1.0, 0.0
        ).astype(BF16)

    def spread(rows):
        high = rows.astype(BF16)
        low = (rows - high.astype(F32)).astype(BF16)
        table = perm[...]
        result = jnp.dot(high, table, preferred_element_type=F32) + jnp.dot(
            low, table, preferred_element_type=F32
        )
        return [result[:, k * 128 : (k + 1) * 128] for k in range(4)]

    for source, target in ((c_in, cF), (b_in, bF)):

        @pl.loop(0, 2)
        def _(half, source=source, target=target):
            for k, part in enumerate(spread(source[pl.ds(half * 8, 8)].reshape(256, 512))):
                target[pl.ds(half * 8 + 3, 8), k, 8:40, :] = part.reshape(8, 32, 128)

    @pl.loop(0, 22)
    def _(x):
        for ref in (e1, e2):
            ref[x, core] = jnp.zeros((48, 128), F32)

    @pl.loop(0, 10)
    def _(x):
        e3[x, core] = jnp.zeros((16, 128), F32)

    @pl.loop(0, 3)
    def _(x):
        rF[x, :, 8:48, :] = jnp.zeros((4, 40, 128), F32)
        rF[x + 19, :, 8:48, :] = jnp.zeros((4, 40, 128), F32)

    @pl.loop(0, 8)
    def _(i):
        for k in range(4):
            t1[0, k, 8:40, :] = cF[2 * i + 3, k, 8:40, :] + cF[2 * i + 4, k, 8:40, :]
        for q in range(2):
            total = None
            for k in (2 * q, 2 * q + 1):
                for start in (8, 9):
                    part = t1[0, k, pl.ds(start, 16, stride=2), :]
                    total = part if total is None else total + part
            c1[i + 4, q, core, 16:32, :] = total * (0.125 * 0.25)

    @pl.loop(0, 4)
    def _(i):
        total = None
        for q in range(2):
            tL[0, q, 0, 16:32, :] = c1[2 * i + 4, q, core, 16:32, :] + c1[2 * i + 5, q, core, 16:32, :]
            for start in (16, 17):
                part = tL[0, q, 0, pl.ds(start, 8, stride=2), :]
                total = part if total is None else total + part
        c2[i + 8, core, 16:24, :] = total * (0.125 * 0.25)

    def spread_faces(arrived, target, depth, low, high):
        for side, at in ((0, low), (1, high)):
            for k, part in enumerate(spread(arrived[side].reshape(depth * 32, 512))):
                target[at : at + depth, k, 8:40, :] = part.reshape(depth, 32, 128)

    for copy in face_c:
        copy.wait_recv()
    spread_faces(face_c_in, cF, 3, 0, 19)
    for copy in face_b:
        copy.wait_recv()
    spread_faces(face_b_in, bF, 2, 1, 19)
    for copy in halo:
        copy.wait_recv()
    for side in range(2):
        for k, part in enumerate(spread(pk_in[side].reshape(176, 512))):
            pk[side, :, k, :, :] = part.reshape(22, 8, 128)

    CWIN, CUP, CDOWN = slice(4, 44), slice(3, 43), slice(5, 45)
    WIN, UP, DOWN = slice(8, 48), slice(7, 47), slice(9, 49)

    @pl.loop(0, 22)
    def _(x):
        for k in range(4):
            cF[x, k, 4:8, :] = pk[0, x, k, 0:4, :]
            bF[x, k, 4:8, :] = pk[0, x, k, 4:8, :]
            cF[x, k, 40:44, :] = pk[1, x, k, 0:4, :]
            bF[x, k, 40:44, :] = pk[1, x, k, 4:8, :]

    def clear_planes(ref, first, count, condition):
        @pl.when(condition)
        def _():
            @pl.loop(first, first + count)
            def _(x):
                if ref.shape[1] == 4:
                    ref[x, :, 0:48, :] = jnp.zeros((4, 48, 128), F32)
                elif len(ref.shape) == 5:
                    for q in range(2):
                        ref[x, q, core] = jnp.zeros(ref.shape[3:], F32)
                else:
                    ref[x, core] = jnp.zeros(ref.shape[2:], F32)

    def clear_rows(ref, first, count, condition):
        zero = jnp.zeros((count, 128), F32)

        @pl.when(condition)
        def _():
            @pl.loop(0, ref.shape[0])
            def _(x):
                if ref.shape[1] == 4:
                    for k in range(4):
                        ref[x, k, first : first + count, :] = zero
                elif len(ref.shape) == 5:
                    for q in range(2):
                        ref[x, q, core, first : first + count, :] = zero
                else:
                    ref[x, core, first : first + count, :] = zero

    for ghost, cell, condition in ((2, 3, gx == 0), (19, 18, gx == nx - 1)):

        @pl.when(condition)
        def _(ghost=ghost, cell=cell):
            cF[ghost] = cF[cell]

    for ghost, cell, condition in ((7, 8, gy == 0), (40, 39, gy == ny - 1)):

        @pl.when(condition)
        def _(ghost=ghost, cell=cell):
            @pl.loop(0, 22)
            def _(x):
                for k in range(4):
                    cF[x, k, ghost : ghost + 1, :] = cF[x, k, cell : cell + 1, :]

    @pl.loop(1, 21)
    def _(x):
        low = roll_down(cF[x, 0, CWIN, :])
        high = roll_up(cF[x, 3, CWIN, :])
        eC[x, core, CWIN, :] = jnp.where(core == 0, low, high)

    edge_phase = 3 * other

    def swap(source, target, first, last, rows):
        return send(
            source.at[first:last, edge_phase, rows], target.at[first:last, core, rows], sibling
        )

    lane40 = lanes(40)

    def left_of(ref, edge, x, k, win):
        if k:
            return ref[x, k - 1, win, :]
        return roll_up(jnp.where(lane40 == 127, edge[x, 0, win, :], ref[x, 3, win, :]))

    def right_of(ref, edge, x, k, win):
        if k < 3:
            return ref[x, k + 1, win, :]
        return roll_down(jnp.where(lane40 == 0, edge[x, 1, win, :], ref[x, 0, win, :]))

    def planes(first, last, group, body):
        count = last - first

        @pl.loop(0, count // group)
        def _(j):
            for store_all in [body(first + j * group + u) for u in range(group)]:
                store_all()

        for store_all in [body(last - 1 - u) for u in range(count % group)]:
            store_all()

    INNER, OUTER = (1, 2), (0, 3)

    def setup_fine(phases):
        def body(x):
            results = []
            for k in phases:
                beside = [
                    cF[x - 1, k, CWIN, :], cF[x + 1, k, CWIN, :], cF[x, k, CUP, :], cF[x, k, CDOWN, :],
                    left_of(cF, eC, x, k, CWIN), right_of(cF, eC, x, k, CWIN),
                ]
                centre = cF[x, k, CWIN, :]
                pairs = [centre + value for value in beside]
                twice = ((pairs[0] + pairs[1]) + (pairs[2] + pairs[3])) + (pairs[4] + pairs[5])
                inverse = 1.0 / twice
                weights = [pair * inverse for pair in pairs]
                results.append((k, weights, 0.5 * twice, bF[x, k, CWIN, :] * inverse * (2.0 / THETA)))

            def store_all():
                for k, weights, diagonal, iterate in results:
                    for n, weight in enumerate(weights):
                        gF[n, x - 1, k] = weight
                    dF[x, k] = diagonal
                    xF[x, k, WIN, :] = iterate

            return store_all

        planes(1, 21, 4 // len(phases), body)

    def sum_fine(ref, edge, x, k):
        return (
            gF[0, x - 1, k] * ref[x - 1, k, WIN, :]
            + gF[1, x - 1, k] * ref[x + 1, k, WIN, :]
            + gF[2, x - 1, k] * ref[x, k, UP, :]
            + gF[3, x - 1, k] * ref[x, k, DOWN, :]
            + gF[4, x - 1, k] * left_of(ref, edge, x, k, WIN)
            + gF[5, x - 1, k] * right_of(ref, edge, x, k, WIN)
        )

    def sweep_fine(target, source, edge, first, last, phases, formula):
        def body(x):
            results = [(k, formula(x, k, sum_fine(source, edge, x, k))) for k in phases]

            def store_all():
                for k, value in results:
                    target[x, k, WIN, :] = value

            return store_all

        planes(first, last, 6 // len(phases), body)

    def edge_first(run, begin_swap):
        for position, phase in ((0, 3), (1, 0)):

            @pl.when(core == position)
            def _(phase=phase):
                run((phase,))

        copy = begin_swap()
        for position, phase in ((0, 0), (1, 3)):

            @pl.when(core == position)
            def _(phase=phase):
                run((phase,))

        return copy

    first = 1.0 + MOM + GAIN * (THETA - 1.0)

    def pre_step(x, k, total):
        return first * xF[x, k, WIN, :] + GAIN * total

    def residual(x, k, total):
        return dF[x, k] * (THETA * xF[x, k, WIN, :] - x2F[x, k, WIN, :] + total)

    copy = swap(cF, eC, 1, 21, slice(0, 48))
    rows_of = {0: (slice(16, 32), slice(16, 32)), -1: (slice(16, 24), slice(32, 40)), 1: (slice(24, 32), slice(8, 16))}
    planes_c1 = {0: (slice(4, 12), slice(4, 12)), -1: (slice(4, 8), slice(12, 16)), 1: (slice(8, 12), slice(0, 4))}
    halo_c1 = []
    for dx, dy in peers8:
        (xs, xd), (ys, yd) = planes_c1[dx], rows_of[dy]
        halo_c1.append(send(c1.at[xs, :, core, ys], c1.at[xd, :, core, yd], peer(dx, dy)))
    halo_c2 = [
        send(
            c2.at[8:12, core, 16:24],
            c2.at[8 - 4 * dx : 12 - 4 * dx, core, 16 - 8 * dy : 24 - 8 * dy],
            peer(dx, dy),
        )
        for dx, dy in peers14
    ]

    setup_fine(INNER)
    copy.wait()
    copy = edge_first(setup_fine, lambda: swap(xF, e1, 2, 20, WIN))
    for n, plane, condition in ((0, 2, gx == 0), (1, 17, gx == nx - 1)):

        @pl.when(condition)
        def _(n=n, plane=plane):
            gF[n, plane] = jnp.zeros((4, 40, 128), F32)

    for n, row, condition in ((2, 4, gy == 0), (3, 35, gy == ny - 1)):

        @pl.when(condition)
        def _(n=n, row=row):
            @pl.loop(1, 19)
            def _(x):
                for k in range(4):
                    gF[n, x, k, row : row + 1, :] = jnp.zeros((1, 128), F32)

    sweep_fine(x2F, xF, e1, 2, 20, INNER, pre_step)
    copy.wait()
    copy = edge_first(
        lambda phases: sweep_fine(x2F, xF, e1, 2, 20, phases, pre_step),
        lambda: swap(x2F, e2, 3, 19, WIN),
    )
    sweep_fine(rF, x2F, e2, 3, 19, INNER, residual)
    copy.wait()
    sweep_fine(rF, x2F, e2, 3, 19, OUTER, residual)

    for row, condition in ((8, gy == 0), (44, gy == ny - 1)):

        @pl.when(condition)
        def _(row=row):
            @pl.loop(3, 19)
            def _(x):
                for k in range(4):
                    rF[x, k, row : row + 4, :] = jnp.zeros((4, 128), F32)

    def restrict_xy(phases):
        def restrict_x(i):
            results = [
                0.125
                * (
                    rF[2 * i, k, WIN, :]
                    + 3.0 * (rF[2 * i + 1, k, WIN, :] + rF[2 * i + 2, k, WIN, :])
                    + rF[2 * i + 3, k, WIN, :]
                )
                for k in phases
            ]

            def store_all():
                for k, value in zip(phases, results):
                    t1[i, k, WIN, :] = value

            return store_all

        def restrict_y(i):
            results = []
            for k in phases:
                part = [t1[i, k, pl.ds(s, 16, stride=2), :] for s in (11, 12, 13, 14)]
                results.append(0.125 * (part[0] + 3.0 * (part[1] + part[2]) + part[3]))

            def store_all():
                for k, value in zip(phases, results):
                    t2[i, k] = value

            return store_all

        planes(0, 10, 5, restrict_x)
        planes(0, 10, 5, restrict_y)

    restrict_xy(OUTER)
    copy = send(t2.at[:, edge_phase], e3.at[:, core], sibling)
    restrict_xy(INNER)
    copy.wait()
    lane16 = lanes(16)

    @pl.loop(0, 10)
    def _(i):
        p = [t2[i, k] for k in range(4)]
        before = roll_up(jnp.where(lane16 == 127, e3[i, 0], p[3]))
        after = roll_down(jnp.where(lane16 == 0, e3[i, 1], p[0]))
        b1[i + 3, 0, core, 16:32, :] = 0.125 * (before + 3.0 * (p[0] + p[1]) + p[2])
        b1[i + 3, 1, core, 16:32, :] = 0.125 * (p[1] + 3.0 * (p[2] + p[3]) + after)

    halo_b1 = []
    for dx, dy in peers8:
        ys, yd = rows_of[dy]
        if dx == 0:
            halo_b1.append(send(b1.at[3:13, :, core, ys], b1.at[3:13, :, core, yd], peer(dx, dy)))
        else:
            xs, xd, near, side = (
                (slice(9, 11), slice(1, 3), slice(11, 13), 0)
                if dx == 1
                else (slice(5, 7), slice(13, 15), slice(3, 5), 1)
            )
            halo_b1.append(send(b1.at[near, :, core, ys], stg.at[side, :, :, yd], peer(dx, dy)))
            halo_b1.append(send(b1.at[xs, :, core, ys], b1.at[xd, :, core, yd], peer(dx, dy)))

    far = [
        send(x2F.at[17:18, :, WIN], x2F.at[1:2, :, WIN], peer(1, 0)),
        send(x2F.at[4:5, :, WIN], x2F.at[20:21, :, WIN], peer(-1, 0)),
    ]

    for copy in face_c + face_b + halo:
        copy.wait_send()
    for copy in halo_c1 + halo_c2:
        copy.wait()
    clear_planes(c1, 0, 4, gx == 0)
    clear_planes(c1, 12, 4, gx == nx - 1)
    clear_rows(c1, 8, 8, gy == 0)
    clear_rows(c1, 32, 8, gy == ny - 1)
    clear_planes(c2, 4, 4, gx == 0)
    clear_planes(c2, 0, 4, gx <= 1)
    clear_planes(c2, 12, 4, gx == nx - 1)
    clear_planes(c2, 16, 4, gx >= nx - 2)
    clear_rows(c2, 8, 8, gy == 0)
    clear_rows(c2, 24, 8, gy == ny - 1)
    hand = [
        send(c1.at[:, :, core, 8:40], c1.at[:, :, core, 8:40], sibling),
        send(c2.at[:, core, 8:32], c2.at[:, core, 8:32], sibling),
    ]
    for copy in hand:
        copy.wait()

    lane32, lane24 = lanes(32), lanes(24)
    WL, UL, DL = slice(8, 40), slice(7, 39), slice(9, 41)
    W2, U2, D2 = slice(8, 32), slice(7, 31), slice(9, 33)

    def before_pair(halves, lane):
        turned = [roll_up(half) for half in halves]
        return [jnp.where(lane == 0, 0.0, turned[0]), jnp.where(lane == 0, turned[0], turned[1])]

    def after_pair(halves, lane):
        turned = [roll_down(half) for half in halves]
        return [jnp.where(lane == 127, turned[1], turned[0]), jnp.where(lane == 127, 0.0, turned[1])]

    def z_mid(ref, x):
        p0 = [ref[x, 0, t, WL, :] for t in range(2)]
        p1 = [ref[x, 1, t, WL, :] for t in range(2)]
        return [(before_pair(p1, lane32), p1), (p0, after_pair(p0, lane32))]

    @pl.loop(1, 15)
    def _(x):
        z_list = z_mid(c1, x)
        for q in range(2):
            for t in range(2):
                beside = [
                    c1[x - 1, q, t, WL, :], c1[x + 1, q, t, WL, :], c1[x, q, t, UL, :], c1[x, q, t, DL, :],
                    z_list[q][0][t], z_list[q][1][t],
                ]
                weights, diagonal, inverse = operator_parts(c1[x, q, t, WL, :], beside)
                for n, weight in enumerate(weights):
                    gL[n, x - 1, q, t] = weight
                dL[x, q, t] = diagonal
                x0L[x, q, t, WL, :] = inverse * (1.0 / THETA)

    def setup_low(first, last):
        @pl.loop(first, last)
        def _(x):
            halves = [c2[x, t, W2, :] for t in range(2)]
            low, high = before_pair(halves, lane24), after_pair(halves, lane24)
            for t in range(2):
                beside = [
                    c2[x - 1, t, W2, :], c2[x + 1, t, W2, :], c2[x, t, U2, :], c2[x, t, D2, :], low[t], high[t],
                ]
                weights, _, inverse = operator_parts(halves[t], beside)
                for n, weight in enumerate(weights):
                    g2[n, x - 1, t] = weight
                inv2[x, t] = inverse

    setup_low(8, 12)

    def scale_mid(first, last):
        @pl.loop(first, last)
        def _(x):
            for q in range(2):
                x1L[x, q, core, WL, :] = b1[x, q, core, WL, :] * x0L[x, q, core, WL, :]

        return send(
            x1L.at[first:last, :, core, 8:40], x1L.at[first:last, :, core, 8:40], sibling
        )

    for copy in halo_b1[-2:]:
        copy.wait()
    handed = [scale_mid(5, 11)]
    for copy in halo_b1[:-2]:
        copy.wait()
    for side, at in ((0, 3), (1, 11)):

        @pl.when((gx > 0) if side == 0 else (gx < nx - 1))
        def _(side=side, at=at):
            for n in range(2):
                for q in range(2):
                    b1[at + n, q, core, WL, :] = b1[at + n, q, core, WL, :] + stg[side, n, q, WL, :]

    handed += [scale_mid(1, 5), scale_mid(11, 15)]
    for copy in handed:
        copy.wait()

    def sum_mid(ref, x):
        z_list = z_mid(ref, x)
        return {
            (q, t): gL[0, x - 1, q, t] * ref[x - 1, q, t, WL, :]
            + gL[1, x - 1, q, t] * ref[x + 1, q, t, WL, :]
            + gL[2, x - 1, q, t] * ref[x, q, t, UL, :]
            + gL[3, x - 1, q, t] * ref[x, q, t, DL, :]
            + gL[4, x - 1, q, t] * z_list[q][0][t]
            + gL[5, x - 1, q, t] * z_list[q][1][t]
            for q in range(2)
            for t in range(2)
        }

    def sweep_mid(target, source, first, last, formula):
        def body(x):
            results = {at: formula(x, *at, total) for at, total in sum_mid(source, x).items()}

            def store_all():
                for (q, t), value in results.items():
                    target[x, q, t, WL, :] = value

            return store_all

        planes(first, last, 2, body)

    sweep_mid(
        x2L, x1L, 2, 14, lambda x, q, t, total: first * x1L[x, q, t, WL, :] + GAIN * total
    )
    sweep_mid(
        xpL, x2L, 3, 13,
        lambda x, q, t, total: dL[x, q, t] * (THETA * x1L[x, q, t, WL, :] - x2L[x, q, t, WL, :] + total),
    )

    lane8 = lanes(8)

    @pl.loop(0, 4)
    def _(i):
        coarse = []
        for q in range(2):
            halves = []
            for t in range(2):
                tL[0, q, t, WL, :] = 0.125 * (
                    xpL[2 * i + 3, q, t, WL, :]
                    + 3.0 * (xpL[2 * i + 4, q, t, WL, :] + xpL[2 * i + 5, q, t, WL, :])
                    + xpL[2 * i + 6, q, t, WL, :]
                )
                part = [tL[0, q, t, pl.ds(s, 8, stride=2), :] for s in (15, 16, 17, 18)]
                halves.append(0.125 * (part[0] + 3.0 * (part[1] + part[2]) + part[3]))
            coarse.append(halves)
        low, high = before_pair(coarse[1], lane8), after_pair(coarse[0], lane8)
        pair = [0.125 * (low[t] + 3.0 * (coarse[0][t] + coarse[1][t]) + high[t]) for t in range(2)]
        mine = jnp.where(core == 0, pair[0], pair[1])
        bd2[i + 8, core, 16:24, :] = mine * inv2[i + 8, core, 8:16, :]

    halo_b2 = [
        send(
            bd2.at[8:12, core, 16:24],
            bd2.at[8 - 4 * dx : 12 - 4 * dx, core, 16 - 8 * dy : 24 - 8 * dy],
            peer(dx, dy),
        )
        for dx, dy in peers14
    ]
    far_mid = [
        send(x2L.at[8:10, :, :, 8:40], x2L.at[0:2, :, :, 8:40], peer(1, 0)),
        send(x2L.at[6:8, :, :, 8:40], x2L.at[14:16, :, :, 8:40], peer(-1, 0)),
    ]
    setup_low(1, 8)
    setup_low(12, 19)
    handed = []
    for group in (0, 1, 2):
        for (dx, dy), copy in zip(peers14, halo_b2):
            if abs(dx) == group:
                copy.wait()
        for at in sorted({8 - 4 * group, 8 + 4 * group}):
            block = bd2.at[at : at + 4, core, 8:32]
            handed.append(send(block, block, sibling))
    for copy in handed:
        copy.wait()

    @pl.loop(0, 20)
    def _(x):
        for t in range(2):
            scaled = jnp.where(c2[x, t, W2, :] > 0.0, bd2[x, t, W2, :], 0.0)
            bd2[x, t, W2, :] = scaled
            d2[x, t] = scaled * (1.0 / THETA_LOW)
            xa[x, t, W2, :] = scaled * (1.0 / THETA_LOW)

    now, later = xa, xb
    for number, (mom, gain) in enumerate(STEPS_LOW):

        def body(x, now=now, later=later, mom=mom, gain=gain):
            halves = [now[x, t, W2, :] for t in range(2)]
            low, high = before_pair(halves, lane24), after_pair(halves, lane24)
            steps = []
            for t in range(2):
                total = (
                    g2[0, x - 1, t] * now[x - 1, t, W2, :]
                    + g2[1, x - 1, t] * now[x + 1, t, W2, :]
                    + g2[2, x - 1, t] * now[x, t, U2, :]
                    + g2[3, x - 1, t] * now[x, t, D2, :]
                    + g2[4, x - 1, t] * low[t]
                    + g2[5, x - 1, t] * high[t]
                )
                steps.append(mom * d2[x, t] + gain * (bd2[x, t, W2, :] - halves[t] + total))

            def store_all():
                for t in range(2):
                    d2[x, t] = steps[t]
                    later[x, t, W2, :] = halves[t] + steps[t]

            return store_all

        planes(number + 1, 19 - number, 6, body)
        now, later = later, now
    bottom = now

    for copy in far_mid:
        copy.wait()

    @pl.loop(0, 8)
    def _(i):
        for odd in range(2):
            x = 2 * i + odd
            mixed = [
                0.75 * bottom[i + 6, t, W2, :] + 0.25 * bottom[i + 5 + 2 * odd, t, W2, :]
                for t in range(2)
            ]
            low, high = before_pair(mixed, lane24), after_pair(mixed, lane24)
            for q, side in ((0, low), (1, high)):
                for t in range(2):
                    t3[odd, q, t, W2, :] = 0.75 * mixed[t] + 0.25 * side[t]
                    centre = 0.75 * t3[odd, q, t, 12:28, :]
                    x0L[x, q, t, pl.ds(8, 16, stride=2), :] = centre + 0.25 * t3[odd, q, t, 11:27, :]
                    x0L[x, q, t, pl.ds(9, 16, stride=2), :] = centre + 0.25 * t3[odd, q, t, 13:29, :]
                    x0L[x, q, t, WL, :] = jnp.where(
                        c1[x, q, t, WL, :] > 0.0, x2L[x, q, t, WL, :] + x0L[x, q, t, WL, :], 0.0
                    )

    def post_first(x, q, t, total):
        start = x0L[x, q, t, WL, :]
        return start + (THETA * x1L[x, q, t, WL, :] - start + total) * (1.0 / THETA)

    def post_second(x, q, t, total):
        here = xpL[x, q, t, WL, :]
        return (
            here
            + MOM * (here - x0L[x, q, t, WL, :])
            + GAIN * (THETA * x1L[x, q, t, WL, :] - here + total)
        )

    sweep_mid(xpL, x0L, 1, 15, post_first)
    sweep_mid(x2L, xpL, 2, 14, post_second)

    for copy in far:
        copy.wait()
    has_left = jnp.where(core == 1, 1.0, 0.0)
    has_right = jnp.where(core == 0, 1.0, 0.0)

    @pl.loop(0, 10)
    def _(i):
        for odd in range(2):
            x = 2 * i + 1 + odd

            def mixed(q, t):
                return 0.75 * x2L[i + 3, q, t, WL, :] + 0.25 * x2L[i + 2 + 2 * odd, q, t, WL, :]

            m0, m1 = mixed(0, core), mixed(1, core)
            before = roll_up(jnp.where(lane32 == 127, has_left * mixed(1, other), m1))
            after = roll_down(jnp.where(lane32 == 0, has_right * mixed(0, other), m0))
            fine = [
                0.75 * m0 + 0.25 * before, 0.75 * m0 + 0.25 * m1,
                0.75 * m1 + 0.25 * m0, 0.75 * m1 + 0.25 * after,
            ]
            for k in range(4):
                tL[odd, k // 2, k % 2, WL, :] = fine[k]
                centre = 0.75 * tL[odd, k // 2, k % 2, 14:34, :]
                cF[x, k, pl.ds(8, 20, stride=2), :] = centre + 0.25 * tL[odd, k // 2, k % 2, 13:33, :]
                cF[x, k, pl.ds(9, 20, stride=2), :] = centre + 0.25 * tL[odd, k // 2, k % 2, 15:35, :]
                cF[x, k, WIN, :] = cF[x, k, WIN, :] + x2F[x, k, WIN, :]

    def last_first(x, k, total):
        start = cF[x, k, WIN, :]
        return start + (THETA * xF[x, k, WIN, :] - start + total) * (1.0 / THETA)

    def last_second(x, k, total):
        here = rF[x, k, WIN, :]
        return (
            here
            + MOM * (here - cF[x, k, WIN, :])
            + GAIN * (THETA * xF[x, k, WIN, :] - here + total)
        )

    copy = swap(cF, e1, 2, 20, WIN)
    sweep_fine(rF, cF, e1, 2, 20, INNER, last_first)
    copy.wait()
    copy = edge_first(
        lambda phases: sweep_fine(rF, cF, e1, 2, 20, phases, last_first),
        lambda: swap(rF, e2, 3, 19, WIN),
    )
    sweep_fine(x2F, rF, e2, 3, 19, INNER, last_second)
    copy.wait()
    sweep_fine(x2F, rF, e2, 3, 19, OUTER, last_second)

    def store(part):
        planes_of = pl.ds(part * 4, 4)
        return pltpu.make_async_copy(out_vm.at[planes_of], out_hbm.at[planes_of], local_sem.at[2 + part])

    for part in range(4):
        total = None
        for k in range(4):
            rows = x2F[part * 4 + 3 : part * 4 + 7, k, 12:44, :].reshape(128, 128)
            high = rows.astype(BF16)
            low = (rows - high.astype(F32)).astype(BF16)
            table = perm[:, k * 128 : (k + 1) * 128]
            for piece in (high, low):
                product = lax.dot_general(piece, table, (((1,), (1,)), ((), ())), preferred_element_type=F32)
                total = product if total is None else total + product
        out_vm[part * 4 : part * 4 + 4] = total.reshape(4, 32, 512)
        store(part).start()
    for part in range(4):
        store(part).wait()


def copy_kernel(source, target, buffer, read_sem, write_sem):
    reads, writes = [], []
    for n in range(8):
        part = pl.ds(2 * n, 2)
        reads.append(pltpu.make_async_copy(source.at[part], buffer.at[part], read_sem.at[n]))
        writes.append(pltpu.make_async_copy(buffer.at[part], target.at[part], write_sem.at[n]))
    for copy in reads:
        copy.start()
    for copy, after in zip(reads, writes):
        copy.wait()
        after.start()
    for copy in writes:
        copy.wait()


def local(right_side, coefficient):
    def vmem(*shape):
        return pltpu.VMEM(shape, F32)

    inputs, fine, mid, low = (22, 4, 48, 128), (22, 4, 56, 128), (16, 2, 2, 48, 128), (20, 2, 40, 128)
    edge = (22, 2, 48, 128)
    scratch = [
        vmem(16, 32, 512), vmem(16, 32, 512), vmem(16, 32, 512), pltpu.VMEM((512, 512), BF16),
        vmem(*fine), vmem(*inputs), vmem(*fine), vmem(*fine), vmem(22, 4, 40, 128), vmem(*fine), vmem(6, 20, 4, 40, 128),
        vmem(*edge), vmem(*edge), vmem(*edge),
        vmem(2, 3, 32, 512), vmem(2, 2, 32, 512), vmem(2, 16, 8, 512), vmem(2, 22, 8, 512), vmem(2, 22, 4, 8, 128),
        vmem(10, 4, 48, 128), vmem(10, 4, 16, 128), vmem(10, 2, 16, 128),
        vmem(*mid), vmem(*mid), vmem(*mid), vmem(*mid), vmem(*mid), vmem(*mid), vmem(16, 2, 2, 32, 128),
        vmem(6, 14, 2, 2, 32, 128), vmem(2, 2, 2, 48, 128), vmem(2, 2, 2, 48, 128),
        vmem(*low), vmem(*low), vmem(*low), vmem(*low), vmem(20, 2, 24, 128), vmem(20, 2, 24, 128),
        vmem(6, 18, 2, 24, 128), vmem(2, 2, 2, 40, 128),
        pltpu.SemaphoreType.DMA((6,)), pltpu.SemaphoreType.DMA((80,)), pltpu.SemaphoreType.DMA((80,)),
    ]
    result = pl.pallas_call(
        kernel,
        out_shape=jax.ShapeDtypeStruct((16, 32, 512), F32),
        in_specs=[pl.BlockSpec(memory_space=pl.ANY)] * 2,
        out_specs=pl.BlockSpec(memory_space=pl.ANY),
        scratch_shapes=scratch,
        compiler_params=pltpu.CompilerParams(
            collective_id=0, has_side_effects=True, vmem_limit_bytes=63 * 2**20
        ),
    )(right_side, coefficient)
    return pl.pallas_call(
        copy_kernel,
        out_shape=jax.ShapeDtypeStruct((16, 32, 512), F32),
        in_specs=[pl.BlockSpec(memory_space=pl.ANY)],
        out_specs=pl.BlockSpec(memory_space=pl.ANY),
        scratch_shapes=[vmem(16, 32, 512), pltpu.SemaphoreType.DMA((8,)), pltpu.SemaphoreType.DMA((8,))],
    )(result)


def solution(mesh):
    return jax.shard_map(
        local,
        mesh=mesh,
        in_specs=(P("gx", "gy", "gz"), P("gx", "gy", "gz")),
        out_specs=P("gx", "gy", "gz"),
        check_vma=False,
    )
```

```python
import functools

import jax
import jax.numpy as jnp
from jax import lax
from jax.experimental import pallas as pl
from jax.experimental.pallas import tpu as pltpu
from jax.sharding import PartitionSpec as P

MESH = pl.DeviceIdType.MESH
F32 = jnp.float32
BF16 = jnp.bfloat16


def cheb_constants(sweeps, lower_edge, upper_edge):
    theta = 0.5 * (upper_edge + lower_edge)
    delta = 0.5 * (upper_edge - lower_edge)
    sigma = theta / delta
    rho = 1.0 / sigma
    steps = []
    for _ in range(1, sweeps):
        rho_next = 1.0 / (2.0 * sigma - rho)
        steps.append((rho_next * rho, 2.0 * rho_next / delta))
        rho = rho_next
    return theta, steps


THETA, ((MOM, GAIN),) = cheb_constants(2, 0.3, 2.0)
THETA_LOW, STEPS_LOW = cheb_constants(6, 0.05, 2.0)


def lanes(rows):
    return lax.broadcasted_iota(jnp.int32, (rows, 128), 1)


def roll_up(value):
    return pltpu.roll(value, 1, 1)


def roll_down(value):
    return pltpu.roll(value, 127, 1)


def operator_parts(centre, beside):
    faces = []
    diagonal = None
    for other in beside:
        face = jnp.where(other > 0.0, 0.5 * (centre + other), centre)
        diagonal = face if diagonal is None else diagonal + face
        faces.append(jnp.where(other > 0.0, face, 0.0))
    inside = centre > 0.0
    inverse = jnp.where(inside, 1.0 / diagonal, 0.0)
    diagonal = jnp.where(inside, diagonal, 0.0)
    return [face * inverse for face in faces], diagonal, inverse


def kernel(
    b_hbm, c_hbm, out_hbm,
    out_vm, b_in, c_in, perm,
    cF, bF, xF, x2F, dF, rF, gF, eC, e1, e2, face_c_in, face_b_in, pk_out, pk_in, pk,
    t1, t2, e3,
    c1, b1, x1L, x2L, x0L, xpL, dL, gL, stg, tL,
    c2, bd2, xa, xb, d2, inv2, g2, t3,
    local_sem, ss, rs,
):
    gx, gy, core = lax.axis_index("gx"), lax.axis_index("gy"), lax.axis_index("gz")
    nx, ny = lax.axis_size("gx"), lax.axis_size("gy")
    other = 1 - core
    sibling = (gx, gy, other)
    counter = [0]

    def peer(dx, dy):
        return (lax.rem(gx + dx + nx, nx), lax.rem(gy + dy + ny, ny), core)

    def send(src, dst, device):
        number = counter[0]
        counter[0] += 1
        copy = pltpu.make_async_remote_copy(
            src_ref=src, dst_ref=dst, send_sem=ss.at[number], recv_sem=rs.at[number],
            device_id=device, device_id_type=MESH,
        )
        copy.start()
        return copy

    peers14 = [(dx, dy) for dx in (-2, 2, -1, 1, 0) for dy in (-1, 1, 0) if (dx, dy) != (0, 0)]
    peers8 = [(dx, dy) for dx, dy in peers14 if abs(dx) < 2]
    barrier = pltpu.get_barrier_semaphore()
    for dx, dy in peers8:
        pl.semaphore_signal(barrier, inc=1, device_id=peer(dx, dy), device_id_type=MESH)
    pl.semaphore_signal(barrier, inc=1, device_id=sibling, device_id_type=MESH)
    load_c = pltpu.make_async_copy(c_hbm, c_in, local_sem.at[0])
    load_b = pltpu.make_async_copy(b_hbm, b_in, local_sem.at[1])
    load_c.start()
    load_b.start()
    pl.semaphore_wait(barrier, len(peers8) + 1)
    face_c = [
        send(c_hbm.at[0:3], face_c_in.at[1], peer(-1, 0)),
        send(c_hbm.at[13:16], face_c_in.at[0], peer(1, 0)),
    ]
    face_b = [
        send(b_hbm.at[0:2], face_b_in.at[1], peer(-1, 0)),
        send(b_hbm.at[14:16], face_b_in.at[0], peer(1, 0)),
    ]
    load_c.wait()
    load_b.wait()

    @pl.loop(0, 16)
    def _(x):
        for side, rows in ((0, slice(0, 4)), (1, slice(28, 32))):
            pk_out[side, x, 0:4, :] = c_in[x, rows, :]
            pk_out[side, x, 4:8, :] = b_in[x, rows, :]

    halo = [
        send(pk_out.at[0], pk_in.at[1, 3:19], peer(0, -1)),
        send(pk_out.at[1], pk_in.at[0, 3:19], peer(0, 1)),
        send(pk_out.at[0, 0:3], pk_in.at[1, 19:22], peer(-1, -1)),
        send(pk_out.at[0, 13:16], pk_in.at[1, 0:3], peer(1, -1)),
        send(pk_out.at[1, 0:3], pk_in.at[0, 19:22], peer(-1, 1)),
        send(pk_out.at[1, 13:16], pk_in.at[0, 0:3], peer(1, 1)),
    ]

    @pl.loop(0, 4)
    def _(j):
        z = lax.broadcasted_iota(jnp.int32, (128, 512), 0) + j * 128
        col = lax.broadcasted_iota(jnp.int32, (128, 512), 1)
        perm[pl.ds(pl.multiple_of(j * 128, 128), 128), :] = jnp.where(
            z == 4 * (col % 128) + col // 128, 1.0, 0.0
        ).astype(BF16)

    def spread(rows):
        high = rows.astype(BF16)
        low = (rows - high.astype(F32)).astype(BF16)
        table = perm[...]
        result = jnp.dot(high, table, preferred_element_type=F32) + jnp.dot(
            low, table, preferred_element_type=F32
        )
        return [result[:, k * 128 : (k + 1) * 128] for k in range(4)]

    for source, target in ((c_in, cF), (b_in, bF)):

        @pl.loop(0, 2)
        def _(half, source=source, target=target):
            for k, part in enumerate(spread(source[pl.ds(half * 8, 8)].reshape(256, 512))):
                target[pl.ds(half * 8 + 3, 8), k, 8:40, :] = part.reshape(8, 32, 128)

    @pl.loop(0, 22)
    def _(x):
        for ref in (e1, e2):
            ref[x, core] = jnp.zeros((48, 128), F32)

    @pl.loop(0, 10)
    def _(x):
        e3[x, core] = jnp.zeros((16, 128), F32)

    @pl.loop(0, 3)
    def _(x):
        rF[x, :, 8:48, :] = jnp.zeros((4, 40, 128), F32)
        rF[x + 19, :, 8:48, :] = jnp.zeros((4, 40, 128), F32)

    @pl.loop(0, 8)
    def _(i):
        for k in range(4):
            t1[0, k, 8:40, :] = cF[2 * i + 3, k, 8:40, :] + cF[2 * i + 4, k, 8:40, :]
        for q in range(2):
            total = None
            for k in (2 * q, 2 * q + 1):
                for start in (8, 9):
                    part = t1[0, k, pl.ds(start, 16, stride=2), :]
                    total = part if total is None else total + part
            c1[i + 4, q, core, 16:32, :] = total * (0.125 * 0.25)

    @pl.loop(0, 4)
    def _(i):
        total = None
        for q in range(2):
            tL[0, q, 0, 16:32, :] = c1[2 * i + 4, q, core, 16:32, :] + c1[2 * i + 5, q, core, 16:32, :]
            for start in (16, 17):
                part = tL[0, q, 0, pl.ds(start, 8, stride=2), :]
                total = part if total is None else total + part
        c2[i + 8, core, 16:24, :] = total * (0.125 * 0.25)

    def spread_faces(arrived, target, depth, low, high):
        for side, at in ((0, low), (1, high)):
            for k, part in enumerate(spread(arrived[side].reshape(depth * 32, 512))):
                target[at : at + depth, k, 8:40, :] = part.reshape(depth, 32, 128)

    for copy in face_c:
        copy.wait_recv()
    spread_faces(face_c_in, cF, 3, 0, 19)
    for copy in face_b:
        copy.wait_recv()
    spread_faces(face_b_in, bF, 2, 1, 19)
    for copy in halo:
        copy.wait_recv()
    for side in range(2):
        for k, part in enumerate(spread(pk_in[side].reshape(176, 512))):
            pk[side, :, k, :, :] = part.reshape(22, 8, 128)

    CWIN, CUP, CDOWN = slice(4, 44), slice(3, 43), slice(5, 45)
    WIN, UP, DOWN = slice(8, 48), slice(7, 47), slice(9, 49)

    @pl.loop(0, 22)
    def _(x):
        for k in range(4):
            cF[x, k, 4:8, :] = pk[0, x, k, 0:4, :]
            bF[x, k, 4:8, :] = pk[0, x, k, 4:8, :]
            cF[x, k, 40:44, :] = pk[1, x, k, 0:4, :]
            bF[x, k, 40:44, :] = pk[1, x, k, 4:8, :]

    def clear_planes(ref, first, count, condition):
        @pl.when(condition)
        def _():
            @pl.loop(first, first + count)
            def _(x):
                if ref.shape[1] == 4:
                    ref[x, :, 0:48, :] = jnp.zeros((4, 48, 128), F32)
                elif len(ref.shape) == 5:
                    for q in range(2):
                        ref[x, q, core] = jnp.zeros(ref.shape[3:], F32)
                else:
                    ref[x, core] = jnp.zeros(ref.shape[2:], F32)

    def clear_rows(ref, first, count, condition):
        zero = jnp.zeros((count, 128), F32)

        @pl.when(condition)
        def _():
            @pl.loop(0, ref.shape[0])
            def _(x):
                if ref.shape[1] == 4:
                    for k in range(4):
                        ref[x, k, first : first + count, :] = zero
                elif len(ref.shape) == 5:
                    for q in range(2):
                        ref[x, q, core, first : first + count, :] = zero
                else:
                    ref[x, core, first : first + count, :] = zero

    for ghost, cell, condition in ((2, 3, gx == 0), (19, 18, gx == nx - 1)):

        @pl.when(condition)
        def _(ghost=ghost, cell=cell):
            cF[ghost] = cF[cell]

    for ghost, cell, condition in ((7, 8, gy == 0), (40, 39, gy == ny - 1)):

        @pl.when(condition)
        def _(ghost=ghost, cell=cell):
            @pl.loop(0, 22)
            def _(x):
                for k in range(4):
                    cF[x, k, ghost : ghost + 1, :] = cF[x, k, cell : cell + 1, :]

    @pl.loop(1, 21)
    def _(x):
        low = roll_down(cF[x, 0, CWIN, :])
        high = roll_up(cF[x, 3, CWIN, :])
        eC[x, core, CWIN, :] = jnp.where(core == 0, low, high)

    edge_phase = 3 * other

    def swap(source, target, first, last, rows):
        return send(
            source.at[first:last, edge_phase, rows], target.at[first:last, core, rows], sibling
        )

    lane40 = lanes(40)

    def left_of(ref, edge, x, k, win):
        if k:
            return ref[x, k - 1, win, :]
        return roll_up(jnp.where(lane40 == 127, edge[x, 0, win, :], ref[x, 3, win, :]))

    def right_of(ref, edge, x, k, win):
        if k < 3:
            return ref[x, k + 1, win, :]
        return roll_down(jnp.where(lane40 == 0, edge[x, 1, win, :], ref[x, 0, win, :]))

    def planes(first, last, group, body):
        count = last - first

        @pl.loop(0, count // group)
        def _(j):
            for store_all in [body(first + j * group + u) for u in range(group)]:
                store_all()

        for store_all in [body(last - 1 - u) for u in range(count % group)]:
            store_all()

    INNER, OUTER = (1, 2), (0, 3)

    def setup_fine(phases):
        def body(x):
            results = []
            for k in phases:
                beside = [
                    cF[x - 1, k, CWIN, :], cF[x + 1, k, CWIN, :], cF[x, k, CUP, :], cF[x, k, CDOWN, :],
                    left_of(cF, eC, x, k, CWIN), right_of(cF, eC, x, k, CWIN),
                ]
                centre = cF[x, k, CWIN, :]
                pairs = [centre + value for value in beside]
                twice = ((pairs[0] + pairs[1]) + (pairs[2] + pairs[3])) + (pairs[4] + pairs[5])
                inverse = 1.0 / twice
                weights = [pair * inverse for pair in pairs]
                results.append((k, weights, 0.5 * twice, bF[x, k, CWIN, :] * inverse * (2.0 / THETA)))

            def store_all():
                for k, weights, diagonal, iterate in results:
                    for n, weight in enumerate(weights):
                        gF[n, x - 1, k] = weight
                    dF[x, k] = diagonal
                    xF[x, k, WIN, :] = iterate

            return store_all

        planes(1, 21, 4 // len(phases), body)

    def sum_fine(ref, edge, x, k):
        return (
            gF[0, x - 1, k] * ref[x - 1, k, WIN, :]
            + gF[1, x - 1, k] * ref[x + 1, k, WIN, :]
            + gF[2, x - 1, k] * ref[x, k, UP, :]
            + gF[3, x - 1, k] * ref[x, k, DOWN, :]
            + gF[4, x - 1, k] * left_of(ref, edge, x, k, WIN)
            + gF[5, x - 1, k] * right_of(ref, edge, x, k, WIN)
        )

    def sweep_fine(target, source, edge, first, last, phases, formula):
        def body(x):
            results = [(k, formula(x, k, sum_fine(source, edge, x, k))) for k in phases]

            def store_all():
                for k, value in results:
                    target[x, k, WIN, :] = value

            return store_all

        planes(first, last, 6 // len(phases), body)

    def edge_first(run, begin_swap):
        for position, phase in ((0, 3), (1, 0)):

            @pl.when(core == position)
            def _(phase=phase):
                run((phase,))

        copy = begin_swap()
        for position, phase in ((0, 0), (1, 3)):

            @pl.when(core == position)
            def _(phase=phase):
                run((phase,))

        return copy

    first = 1.0 + MOM + GAIN * (THETA - 1.0)

    def pre_step(x, k, total):
        return first * xF[x, k, WIN, :] + GAIN * total

    def residual(x, k, total):
        return dF[x, k] * (THETA * xF[x, k, WIN, :] - x2F[x, k, WIN, :] + total)

    copy = swap(cF, eC, 1, 21, slice(0, 48))
    rows_of = {0: (slice(16, 32), slice(16, 32)), -1: (slice(16, 24), slice(32, 40)), 1: (slice(24, 32), slice(8, 16))}
    planes_c1 = {0: (slice(4, 12), slice(4, 12)), -1: (slice(4, 8), slice(12, 16)), 1: (slice(8, 12), slice(0, 4))}
    halo_c1 = []
    for dx, dy in peers8:
        (xs, xd), (ys, yd) = planes_c1[dx], rows_of[dy]
        halo_c1.append(send(c1.at[xs, :, core, ys], c1.at[xd, :, core, yd], peer(dx, dy)))
    halo_c2 = [
        send(
            c2.at[8:12, core, 16:24],
            c2.at[8 - 4 * dx : 12 - 4 * dx, core, 16 - 8 * dy : 24 - 8 * dy],
            peer(dx, dy),
        )
        for dx, dy in peers14
    ]

    setup_fine(INNER)
    copy.wait()
    copy = edge_first(setup_fine, lambda: swap(xF, e1, 2, 20, WIN))
    for n, plane, condition in ((0, 2, gx == 0), (1, 17, gx == nx - 1)):

        @pl.when(condition)
        def _(n=n, plane=plane):
            gF[n, plane] = jnp.zeros((4, 40, 128), F32)

    for n, row, condition in ((2, 4, gy == 0), (3, 35, gy == ny - 1)):

        @pl.when(condition)
        def _(n=n, row=row):
            @pl.loop(1, 19)
            def _(x):
                for k in range(4):
                    gF[n, x, k, row : row + 1, :] = jnp.zeros((1, 128), F32)

    sweep_fine(x2F, xF, e1, 2, 20, INNER, pre_step)
    copy.wait()
    copy = edge_first(
        lambda phases: sweep_fine(x2F, xF, e1, 2, 20, phases, pre_step),
        lambda: swap(x2F, e2, 3, 19, WIN),
    )
    sweep_fine(rF, x2F, e2, 3, 19, INNER, residual)
    copy.wait()
    sweep_fine(rF, x2F, e2, 3, 19, OUTER, residual)

    for row, condition in ((8, gy == 0), (44, gy == ny - 1)):

        @pl.when(condition)
        def _(row=row):
            @pl.loop(3, 19)
            def _(x):
                for k in range(4):
                    rF[x, k, row : row + 4, :] = jnp.zeros((4, 128), F32)

    def restrict_xy(phases):
        def restrict_x(i):
            results = [
                0.125
                * (
                    rF[2 * i, k, WIN, :]
                    + 3.0 * (rF[2 * i + 1, k, WIN, :] + rF[2 * i + 2, k, WIN, :])
                    + rF[2 * i + 3, k, WIN, :]
                )
                for k in phases
            ]

            def store_all():
                for k, value in zip(phases, results):
                    t1[i, k, WIN, :] = value

            return store_all

        def restrict_y(i):
            results = []
            for k in phases:
                part = [t1[i, k, pl.ds(s, 16, stride=2), :] for s in (11, 12, 13, 14)]
                results.append(0.125 * (part[0] + 3.0 * (part[1] + part[2]) + part[3]))

            def store_all():
                for k, value in zip(phases, results):
                    t2[i, k] = value

            return store_all

        planes(0, 10, 5, restrict_x)
        planes(0, 10, 5, restrict_y)

    restrict_xy(OUTER)
    copy = send(t2.at[:, edge_phase], e3.at[:, core], sibling)
    restrict_xy(INNER)
    copy.wait()
    lane16 = lanes(16)

    def restrict_z(i):
        p = [t2[i, k] for k in range(4)]
        before = roll_up(jnp.where(lane16 == 127, e3[i, 0], p[3]))
        after = roll_down(jnp.where(lane16 == 0, e3[i, 1], p[0]))
        even = 0.125 * (before + 3.0 * (p[0] + p[1]) + p[2])
        odd = 0.125 * (p[1] + 3.0 * (p[2] + p[3]) + after)

        def store_all():
            b1[i + 3, 0, core, 16:32, :] = even
            b1[i + 3, 1, core, 16:32, :] = odd

        return store_all

    planes(0, 10, 5, restrict_z)

    halo_b1 = []
    for dx, dy in peers8:
        ys, yd = rows_of[dy]
        if dx == 0:
            halo_b1.append(send(b1.at[3:13, :, core, ys], b1.at[3:13, :, core, yd], peer(dx, dy)))
        else:
            xs, xd, near, side = (
                (slice(9, 11), slice(1, 3), slice(11, 13), 0)
                if dx == 1
                else (slice(5, 7), slice(13, 15), slice(3, 5), 1)
            )
            halo_b1.append(send(b1.at[near, :, core, ys], stg.at[side, :, :, yd], peer(dx, dy)))
            halo_b1.append(send(b1.at[xs, :, core, ys], b1.at[xd, :, core, yd], peer(dx, dy)))

    far = [
        send(x2F.at[17:18, :, WIN], x2F.at[1:2, :, WIN], peer(1, 0)),
        send(x2F.at[4:5, :, WIN], x2F.at[20:21, :, WIN], peer(-1, 0)),
    ]

    for copy in face_c + face_b + halo:
        copy.wait_send()
    for copy in halo_c1 + halo_c2:
        copy.wait()
    clear_planes(c1, 0, 4, gx == 0)
    clear_planes(c1, 12, 4, gx == nx - 1)
    clear_rows(c1, 8, 8, gy == 0)
    clear_rows(c1, 32, 8, gy == ny - 1)
    clear_planes(c2, 4, 4, gx == 0)
    clear_planes(c2, 0, 4, gx <= 1)
    clear_planes(c2, 12, 4, gx == nx - 1)
    clear_planes(c2, 16, 4, gx >= nx - 2)
    clear_rows(c2, 8, 8, gy == 0)
    clear_rows(c2, 24, 8, gy == ny - 1)
    hand = [
        send(c1.at[:, :, core, 8:40], c1.at[:, :, core, 8:40], sibling),
        send(c2.at[:, core, 8:32], c2.at[:, core, 8:32], sibling),
    ]
    for copy in hand:
        copy.wait()

    lane32, lane24 = lanes(32), lanes(24)
    WL, UL, DL = slice(8, 40), slice(7, 39), slice(9, 41)
    W2, U2, D2 = slice(8, 32), slice(7, 31), slice(9, 33)

    def before_pair(halves, lane):
        turned = [roll_up(half) for half in halves]
        return [jnp.where(lane == 0, 0.0, turned[0]), jnp.where(lane == 0, turned[0], turned[1])]

    def after_pair(halves, lane):
        turned = [roll_down(half) for half in halves]
        return [jnp.where(lane == 127, turned[1], turned[0]), jnp.where(lane == 127, 0.0, turned[1])]

    def z_mid(ref, x):
        p0 = [ref[x, 0, t, WL, :] for t in range(2)]
        p1 = [ref[x, 1, t, WL, :] for t in range(2)]
        return [(before_pair(p1, lane32), p1), (p0, after_pair(p0, lane32))]

    @pl.loop(1, 15)
    def _(x):
        z_list = z_mid(c1, x)
        for q in range(2):
            for t in range(2):
                beside = [
                    c1[x - 1, q, t, WL, :], c1[x + 1, q, t, WL, :], c1[x, q, t, UL, :], c1[x, q, t, DL, :],
                    z_list[q][0][t], z_list[q][1][t],
                ]
                weights, diagonal, inverse = operator_parts(c1[x, q, t, WL, :], beside)
                for n, weight in enumerate(weights):
                    gL[n, x - 1, q, t] = weight
                dL[x, q, t] = diagonal
                x0L[x, q, t, WL, :] = inverse * (1.0 / THETA)

    def setup_low(first, last):
        @pl.loop(first, last)
        def _(x):
            halves = [c2[x, t, W2, :] for t in range(2)]
            low, high = before_pair(halves, lane24), after_pair(halves, lane24)
            for t in range(2):
                beside = [
                    c2[x - 1, t, W2, :], c2[x + 1, t, W2, :], c2[x, t, U2, :], c2[x, t, D2, :], low[t], high[t],
                ]
                weights, _, inverse = operator_parts(halves[t], beside)
                for n, weight in enumerate(weights):
                    g2[n, x - 1, t] = weight
                inv2[x, t] = inverse

    setup_low(8, 12)

    def scale_mid(first, last):
        @pl.loop(first, last)
        def _(x):
            for q in range(2):
                x1L[x, q, core, WL, :] = b1[x, q, core, WL, :] * x0L[x, q, core, WL, :]

        return send(
            x1L.at[first:last, :, core, 8:40], x1L.at[first:last, :, core, 8:40], sibling
        )

    for copy in halo_b1[-2:]:
        copy.wait()
    handed = [scale_mid(5, 11)]
    for copy in halo_b1[:-2]:
        copy.wait()
    for side, at in ((0, 3), (1, 11)):

        @pl.when((gx > 0) if side == 0 else (gx < nx - 1))
        def _(side=side, at=at):
            for n in range(2):
                for q in range(2):
                    b1[at + n, q, core, WL, :] = b1[at + n, q, core, WL, :] + stg[side, n, q, WL, :]

    handed += [scale_mid(1, 5), scale_mid(11, 15)]
    for copy in handed:
        copy.wait()

    def sum_mid(ref, x):
        z_list = z_mid(ref, x)
        return {
            (q, t): gL[0, x - 1, q, t] * ref[x - 1, q, t, WL, :]
            + gL[1, x - 1, q, t] * ref[x + 1, q, t, WL, :]
            + gL[2, x - 1, q, t] * ref[x, q, t, UL, :]
            + gL[3, x - 1, q, t] * ref[x, q, t, DL, :]
            + gL[4, x - 1, q, t] * z_list[q][0][t]
            + gL[5, x - 1, q, t] * z_list[q][1][t]
            for q in range(2)
            for t in range(2)
        }

    def sweep_mid(target, source, first, last, formula):
        def body(x):
            results = {at: formula(x, *at, total) for at, total in sum_mid(source, x).items()}

            def store_all():
                for (q, t), value in results.items():
                    target[x, q, t, WL, :] = value

            return store_all

        planes(first, last, 2, body)

    sweep_mid(
        x2L, x1L, 2, 14, lambda x, q, t, total: first * x1L[x, q, t, WL, :] + GAIN * total
    )
    sweep_mid(
        xpL, x2L, 3, 13,
        lambda x, q, t, total: dL[x, q, t] * (THETA * x1L[x, q, t, WL, :] - x2L[x, q, t, WL, :] + total),
    )

    lane8 = lanes(8)

    for i in range(4):
        for q in range(2):
            for t in range(2):
                t1[i, 2 * q + t, WL, :] = 0.125 * (
                    xpL[2 * i + 3, q, t, WL, :]
                    + 3.0 * (xpL[2 * i + 4, q, t, WL, :] + xpL[2 * i + 5, q, t, WL, :])
                    + xpL[2 * i + 6, q, t, WL, :]
                )
    for i in range(4):
        coarse = []
        for q in range(2):
            halves = []
            for t in range(2):
                part = [t1[i, 2 * q + t, pl.ds(s, 8, stride=2), :] for s in (15, 16, 17, 18)]
                halves.append(0.125 * (part[0] + 3.0 * (part[1] + part[2]) + part[3]))
            coarse.append(halves)
        low, high = before_pair(coarse[1], lane8), after_pair(coarse[0], lane8)
        pair = [0.125 * (low[t] + 3.0 * (coarse[0][t] + coarse[1][t]) + high[t]) for t in range(2)]
        mine = jnp.where(core == 0, pair[0], pair[1])
        bd2[i + 8, core, 16:24, :] = mine * inv2[i + 8, core, 8:16, :]

    halo_b2 = [
        send(
            bd2.at[8:12, core, 16:24],
            bd2.at[8 - 4 * dx : 12 - 4 * dx, core, 16 - 8 * dy : 24 - 8 * dy],
            peer(dx, dy),
        )
        for dx, dy in peers14
    ]
    far_mid = [
        send(x2L.at[8:10, :, :, 8:40], x2L.at[0:2, :, :, 8:40], peer(1, 0)),
        send(x2L.at[6:8, :, :, 8:40], x2L.at[14:16, :, :, 8:40], peer(-1, 0)),
    ]
    setup_low(1, 8)
    setup_low(12, 19)
    handed = []
    for group in (0, 1, 2):
        for (dx, dy), copy in zip(peers14, halo_b2):
            if abs(dx) == group:
                copy.wait()
        for at in sorted({8 - 4 * group, 8 + 4 * group}):
            block = bd2.at[at : at + 4, core, 8:32]
            handed.append(send(block, block, sibling))
    for copy in handed:
        copy.wait()

    def begin_low(x):
        scaled = [jnp.where(c2[x, t, W2, :] > 0.0, bd2[x, t, W2, :], 0.0) for t in range(2)]

        def store_all():
            for t in range(2):
                bd2[x, t, W2, :] = scaled[t]
                d2[x, t] = scaled[t] * (1.0 / THETA_LOW)
                xa[x, t, W2, :] = scaled[t] * (1.0 / THETA_LOW)

        return store_all

    planes(0, 20, 5, begin_low)

    now, later = xa, xb
    for number, (mom, gain) in enumerate(STEPS_LOW):

        def body(x, now=now, later=later, mom=mom, gain=gain):
            halves = [now[x, t, W2, :] for t in range(2)]
            low, high = before_pair(halves, lane24), after_pair(halves, lane24)
            steps = []
            for t in range(2):
                total = (
                    g2[0, x - 1, t] * now[x - 1, t, W2, :]
                    + g2[1, x - 1, t] * now[x + 1, t, W2, :]
                    + g2[2, x - 1, t] * now[x, t, U2, :]
                    + g2[3, x - 1, t] * now[x, t, D2, :]
                    + g2[4, x - 1, t] * low[t]
                    + g2[5, x - 1, t] * high[t]
                )
                steps.append(mom * d2[x, t] + gain * (bd2[x, t, W2, :] - halves[t] + total))

            def store_all():
                for t in range(2):
                    d2[x, t] = steps[t]
                    later[x, t, W2, :] = halves[t] + steps[t]

            return store_all

        planes(number + 1, 19 - number, 6, body)
        now, later = later, now
    bottom = now

    for copy in far_mid:
        copy.wait()

    def prolong_mid(i):
        results = []
        for odd in range(2):
            mixed = [
                0.75 * bottom[i + 6, t, W2, :] + 0.25 * bottom[i + 5 + 2 * odd, t, W2, :]
                for t in range(2)
            ]
            low, high = before_pair(mixed, lane24), after_pair(mixed, lane24)
            for q, side in ((0, low), (1, high)):
                for t in range(2):
                    results.append((odd, 2 * q + t, 0.75 * mixed[t] + 0.25 * side[t]))

        def store_all():
            for odd, slot, value in results:
                bF[2 * i + odd, slot, W2, :] = value

        return store_all

    def prolong_mid_rows(x):
        results = []
        for slot in range(4):
            centre = 0.75 * bF[x, slot, 12:28, :]
            results.append(
                (centre + 0.25 * bF[x, slot, 11:27, :], centre + 0.25 * bF[x, slot, 13:29, :])
            )

        def store_all():
            for slot, (even, odd) in enumerate(results):
                x0L[x, slot // 2, slot % 2, pl.ds(8, 16, stride=2), :] = even
                x0L[x, slot // 2, slot % 2, pl.ds(9, 16, stride=2), :] = odd

        return store_all

    def correct_mid(x):
        results = [
            (q, t, jnp.where(c1[x, q, t, WL, :] > 0.0, x2L[x, q, t, WL, :] + x0L[x, q, t, WL, :], 0.0))
            for q in range(2)
            for t in range(2)
        ]

        def store_all():
            for q, t, value in results:
                x0L[x, q, t, WL, :] = value

        return store_all

    planes(0, 8, 2, prolong_mid)
    planes(0, 16, 4, prolong_mid_rows)
    planes(0, 16, 2, correct_mid)

    def post_first(x, q, t, total):
        start = x0L[x, q, t, WL, :]
        return start + (THETA * x1L[x, q, t, WL, :] - start + total) * (1.0 / THETA)

    def post_second(x, q, t, total):
        here = xpL[x, q, t, WL, :]
        return (
            here
            + MOM * (here - x0L[x, q, t, WL, :])
            + GAIN * (THETA * x1L[x, q, t, WL, :] - here + total)
        )

    sweep_mid(xpL, x0L, 1, 15, post_first)
    sweep_mid(x2L, xpL, 2, 14, post_second)

    for copy in far:
        copy.wait()
    has_left = jnp.where(core == 1, 1.0, 0.0)
    has_right = jnp.where(core == 0, 1.0, 0.0)

    def prolong_fine(i):
        results = []
        for odd in range(2):

            def mixed(q, t):
                return 0.75 * x2L[i + 3, q, t, WL, :] + 0.25 * x2L[i + 2 + 2 * odd, q, t, WL, :]

            m0, m1 = mixed(0, core), mixed(1, core)
            before = roll_up(jnp.where(lane32 == 127, has_left * mixed(1, other), m1))
            after = roll_down(jnp.where(lane32 == 0, has_right * mixed(0, other), m0))
            results.append(
                (
                    0.75 * m0 + 0.25 * before, 0.75 * m0 + 0.25 * m1,
                    0.75 * m1 + 0.25 * m0, 0.75 * m1 + 0.25 * after,
                )
            )

        def store_all():
            for odd in range(2):
                for k in range(4):
                    bF[2 * i + 1 + odd, k, WL, :] = results[odd][k]

        return store_all

    def prolong_fine_rows(x):
        results = []
        for k in range(4):
            centre = 0.75 * bF[x, k, 14:34, :]
            results.append((centre + 0.25 * bF[x, k, 13:33, :], centre + 0.25 * bF[x, k, 15:35, :]))

        def store_all():
            for k, (even, odd) in enumerate(results):
                cF[x, k, pl.ds(8, 20, stride=2), :] = even
                cF[x, k, pl.ds(9, 20, stride=2), :] = odd

        return store_all

    def correct_fine(x):
        results = [cF[x, k, WIN, :] + x2F[x, k, WIN, :] for k in range(4)]

        def store_all():
            for k in range(4):
                cF[x, k, WIN, :] = results[k]

        return store_all

    planes(0, 10, 1, prolong_fine)
    planes(1, 21, 2, prolong_fine_rows)
    planes(1, 21, 2, correct_fine)

    def last_first(x, k, total):
        start = cF[x, k, WIN, :]
        return start + (THETA * xF[x, k, WIN, :] - start + total) * (1.0 / THETA)

    def last_second(x, k, total):
        here = rF[x, k, WIN, :]
        return (
            here
            + MOM * (here - cF[x, k, WIN, :])
            + GAIN * (THETA * xF[x, k, WIN, :] - here + total)
        )

    copy = swap(cF, e1, 2, 20, WIN)
    sweep_fine(rF, cF, e1, 2, 20, INNER, last_first)
    copy.wait()
    copy = edge_first(
        lambda phases: sweep_fine(rF, cF, e1, 2, 20, phases, last_first),
        lambda: swap(rF, e2, 3, 19, WIN),
    )
    sweep_fine(x2F, rF, e2, 3, 19, INNER, last_second)
    copy.wait()
    sweep_fine(x2F, rF, e2, 3, 19, OUTER, last_second)

    def store(part):
        planes_of = pl.ds(part * 4, 4)
        return pltpu.make_async_copy(out_vm.at[planes_of], out_hbm.at[planes_of], local_sem.at[2 + part])

    for part in range(4):
        total = None
        for k in range(4):
            rows = x2F[part * 4 + 3 : part * 4 + 7, k, 12:44, :].reshape(128, 128)
            high = rows.astype(BF16)
            low = (rows - high.astype(F32)).astype(BF16)
            table = perm[:, k * 128 : (k + 1) * 128]
            for piece in (high, low):
                product = lax.dot_general(piece, table, (((1,), (1,)), ((), ())), preferred_element_type=F32)
                total = product if total is None else total + product
        out_vm[part * 4 : part * 4 + 4] = total.reshape(4, 32, 512)
        store(part).start()
    for part in range(4):
        store(part).wait()


def copy_kernel(source, target, buffer, read_sem, write_sem):
    reads, writes = [], []
    for n in range(8):
        part = pl.ds(2 * n, 2)
        reads.append(pltpu.make_async_copy(source.at[part], buffer.at[part], read_sem.at[n]))
        writes.append(pltpu.make_async_copy(buffer.at[part], target.at[part], write_sem.at[n]))
    for copy in reads:
        copy.start()
    for copy, after in zip(reads, writes):
        copy.wait()
        after.start()
    for copy in writes:
        copy.wait()


def local(right_side, coefficient):
    def vmem(*shape):
        return pltpu.VMEM(shape, F32)

    inputs, fine, mid, low = (22, 4, 48, 128), (22, 4, 56, 128), (16, 2, 2, 48, 128), (20, 2, 40, 128)
    edge = (22, 2, 48, 128)
    scratch = [
        vmem(16, 32, 512), vmem(16, 32, 512), vmem(16, 32, 512), pltpu.VMEM((512, 512), BF16),
        vmem(*fine), vmem(*inputs), vmem(*fine), vmem(*fine), vmem(22, 4, 40, 128), vmem(*fine), vmem(6, 20, 4, 40, 128),
        vmem(*edge), vmem(*edge), vmem(*edge),
        vmem(2, 3, 32, 512), vmem(2, 2, 32, 512), vmem(2, 16, 8, 512), vmem(2, 22, 8, 512), vmem(2, 22, 4, 8, 128),
        vmem(10, 4, 48, 128), vmem(10, 4, 16, 128), vmem(10, 2, 16, 128),
        vmem(*mid), vmem(*mid), vmem(*mid), vmem(*mid), vmem(*mid), vmem(*mid), vmem(16, 2, 2, 32, 128),
        vmem(6, 14, 2, 2, 32, 128), vmem(2, 2, 2, 48, 128), vmem(2, 2, 2, 48, 128),
        vmem(*low), vmem(*low), vmem(*low), vmem(*low), vmem(20, 2, 24, 128), vmem(20, 2, 24, 128),
        vmem(6, 18, 2, 24, 128), vmem(2, 2, 2, 40, 128),
        pltpu.SemaphoreType.DMA((6,)), pltpu.SemaphoreType.DMA((80,)), pltpu.SemaphoreType.DMA((80,)),
    ]
    result = pl.pallas_call(
        kernel,
        out_shape=jax.ShapeDtypeStruct((16, 32, 512), F32),
        in_specs=[pl.BlockSpec(memory_space=pl.ANY)] * 2,
        out_specs=pl.BlockSpec(memory_space=pl.ANY),
        scratch_shapes=scratch,
        compiler_params=pltpu.CompilerParams(
            collective_id=0, has_side_effects=True, vmem_limit_bytes=63 * 2**20
        ),
    )(right_side, coefficient)
    return pl.pallas_call(
        copy_kernel,
        out_shape=jax.ShapeDtypeStruct((16, 32, 512), F32),
        in_specs=[pl.BlockSpec(memory_space=pl.ANY)],
        out_specs=pl.BlockSpec(memory_space=pl.ANY),
        scratch_shapes=[vmem(16, 32, 512), pltpu.SemaphoreType.DMA((8,)), pltpu.SemaphoreType.DMA((8,))],
    )(result)


def solution(mesh):
    return jax.shard_map(
        local,
        mesh=mesh,
        in_specs=(P("gx", "gy", "gz"), P("gx", "gy", "gz")),
        out_specs=P("gx", "gy", "gz"),
        check_vma=False,
    )
```

```python
import functools

import jax
import jax.numpy as jnp
from jax import lax
from jax.experimental import pallas as pl
from jax.experimental.pallas import tpu as pltpu
from jax.sharding import PartitionSpec as P

MESH = pl.DeviceIdType.MESH
F32 = jnp.float32
BF16 = jnp.bfloat16


def cheb_constants(sweeps, lower_edge, upper_edge):
    theta = 0.5 * (upper_edge + lower_edge)
    delta = 0.5 * (upper_edge - lower_edge)
    sigma = theta / delta
    rho = 1.0 / sigma
    steps = []
    for _ in range(1, sweeps):
        rho_next = 1.0 / (2.0 * sigma - rho)
        steps.append((rho_next * rho, 2.0 * rho_next / delta))
        rho = rho_next
    return theta, steps


THETA, ((MOM, GAIN),) = cheb_constants(2, 0.3, 2.0)
THETA_LOW, STEPS_LOW = cheb_constants(6, 0.05, 2.0)


def lanes(rows):
    return lax.broadcasted_iota(jnp.int32, (rows, 128), 1)


def roll_up(value):
    return pltpu.roll(value, 1, 1)


def roll_down(value):
    return pltpu.roll(value, 127, 1)


def operator_parts(centre, beside):
    faces = []
    diagonal = None
    for other in beside:
        face = jnp.where(other > 0.0, 0.5 * (centre + other), centre)
        diagonal = face if diagonal is None else diagonal + face
        faces.append(jnp.where(other > 0.0, face, 0.0))
    inside = centre > 0.0
    inverse = jnp.where(inside, 1.0 / diagonal, 0.0)
    diagonal = jnp.where(inside, diagonal, 0.0)
    return [face * inverse for face in faces], diagonal, inverse


def kernel(
    b_hbm, c_hbm, out_hbm,
    out_vm, b_in, c_in, perm,
    cF, bF, xF, x2F, dF, rF, gF, eC, e1, e2, face_c_in, face_b_in, pk_out, pk_in, pk,
    t1, t2, e3,
    c1, b1, x1L, x2L, x0L, xpL, dL, gL, stg, tL,
    c2, bd2, xa, xb, d2, inv2, g2, t3,
    local_sem, ss, rs,
):
    gx, gy, core = lax.axis_index("gx"), lax.axis_index("gy"), lax.axis_index("gz")
    nx, ny = lax.axis_size("gx"), lax.axis_size("gy")
    other = 1 - core
    sibling = (gx, gy, other)
    counter = [0]

    def peer(dx, dy):
        return (lax.rem(gx + dx + nx, nx), lax.rem(gy + dy + ny, ny), core)

    def send(src, dst, device):
        number = counter[0]
        counter[0] += 1
        copy = pltpu.make_async_remote_copy(
            src_ref=src, dst_ref=dst, send_sem=ss.at[number], recv_sem=rs.at[number],
            device_id=device, device_id_type=MESH,
        )
        copy.start()
        return copy

    peers14 = [(dx, dy) for dx in (-2, 2, -1, 1, 0) for dy in (-1, 1, 0) if (dx, dy) != (0, 0)]
    peers8 = [(dx, dy) for dx, dy in peers14 if abs(dx) < 2]
    barrier = pltpu.get_barrier_semaphore()
    for dx, dy in peers8:
        pl.semaphore_signal(barrier, inc=1, device_id=peer(dx, dy), device_id_type=MESH)
    pl.semaphore_signal(barrier, inc=1, device_id=sibling, device_id_type=MESH)
    load_c = pltpu.make_async_copy(c_hbm, c_in, local_sem.at[0])
    load_b = pltpu.make_async_copy(b_hbm, b_in, local_sem.at[1])
    load_c.start()
    load_b.start()
    pl.semaphore_wait(barrier, len(peers8) + 1)
    face_c = [
        send(c_hbm.at[0:3], face_c_in.at[1], peer(-1, 0)),
        send(c_hbm.at[13:16], face_c_in.at[0], peer(1, 0)),
    ]
    face_b = [
        send(b_hbm.at[0:2], face_b_in.at[1], peer(-1, 0)),
        send(b_hbm.at[14:16], face_b_in.at[0], peer(1, 0)),
    ]
    load_c.wait()
    load_b.wait()

    @pl.loop(0, 16)
    def _(x):
        for side, rows in ((0, slice(0, 4)), (1, slice(28, 32))):
            pk_out[side, x, 0:4, :] = c_in[x, rows, :]
            pk_out[side, x, 4:8, :] = b_in[x, rows, :]

    halo = [
        send(pk_out.at[0], pk_in.at[1, 3:19], peer(0, -1)),
        send(pk_out.at[1], pk_in.at[0, 3:19], peer(0, 1)),
        send(pk_out.at[0, 0:3], pk_in.at[1, 19:22], peer(-1, -1)),
        send(pk_out.at[0, 13:16], pk_in.at[1, 0:3], peer(1, -1)),
        send(pk_out.at[1, 0:3], pk_in.at[0, 19:22], peer(-1, 1)),
        send(pk_out.at[1, 13:16], pk_in.at[0, 0:3], peer(1, 1)),
    ]

    @pl.loop(0, 4)
    def _(j):
        z = lax.broadcasted_iota(jnp.int32, (128, 512), 0) + j * 128
        col = lax.broadcasted_iota(jnp.int32, (128, 512), 1)
        perm[pl.ds(pl.multiple_of(j * 128, 128), 128), :] = jnp.where(
            z == 4 * (col % 128) + col // 128, 1.0, 0.0
        ).astype(BF16)

    def spread(rows):
        high = rows.astype(BF16)
        low = (rows - high.astype(F32)).astype(BF16)
        table = perm[...]
        result = jnp.dot(high, table, preferred_element_type=F32) + jnp.dot(
            low, table, preferred_element_type=F32
        )
        return [result[:, k * 128 : (k + 1) * 128] for k in range(4)]

    for source, target in ((c_in, cF), (b_in, bF)):

        @pl.loop(0, 2)
        def _(half, source=source, target=target):
            for k, part in enumerate(spread(source[pl.ds(half * 8, 8)].reshape(256, 512))):
                target[pl.ds(half * 8 + 3, 8), k, 8:40, :] = part.reshape(8, 32, 128)

    @pl.loop(0, 22)
    def _(x):
        for ref in (e1, e2):
            ref[x, core] = jnp.zeros((48, 128), F32)

    @pl.loop(0, 10)
    def _(x):
        e3[x, core] = jnp.zeros((16, 128), F32)

    @pl.loop(0, 3)
    def _(x):
        rF[x, :, 8:48, :] = jnp.zeros((4, 40, 128), F32)
        rF[x + 19, :, 8:48, :] = jnp.zeros((4, 40, 128), F32)

    @pl.loop(0, 8)
    def _(i):
        for k in range(4):
            t1[0, k, 8:40, :] = cF[2 * i + 3, k, 8:40, :] + cF[2 * i + 4, k, 8:40, :]
        for q in range(2):
            total = None
            for k in (2 * q, 2 * q + 1):
                for start in (8, 9):
                    part = t1[0, k, pl.ds(start, 16, stride=2), :]
                    total = part if total is None else total + part
            c1[i + 4, q, core, 16:32, :] = total * (0.125 * 0.25)

    @pl.loop(0, 4)
    def _(i):
        total = None
        for q in range(2):
            tL[0, q, 0, 16:32, :] = c1[2 * i + 4, q, core, 16:32, :] + c1[2 * i + 5, q, core, 16:32, :]
            for start in (16, 17):
                part = tL[0, q, 0, pl.ds(start, 8, stride=2), :]
                total = part if total is None else total + part
        c2[i + 8, core, 16:24, :] = total * (0.125 * 0.25)

    def spread_faces(arrived, target, depth, low, high):
        for side, at in ((0, low), (1, high)):
            for k, part in enumerate(spread(arrived[side].reshape(depth * 32, 512))):
                target[at : at + depth, k, 8:40, :] = part.reshape(depth, 32, 128)

    for copy in face_c:
        copy.wait_recv()
    spread_faces(face_c_in, cF, 3, 0, 19)
    for copy in face_b:
        copy.wait_recv()
    spread_faces(face_b_in, bF, 2, 1, 19)
    for copy in halo:
        copy.wait_recv()
    for side in range(2):
        for k, part in enumerate(spread(pk_in[side].reshape(176, 512))):
            pk[side, :, k, :, :] = part.reshape(22, 8, 128)

    CWIN, CUP, CDOWN = slice(4, 44), slice(3, 43), slice(5, 45)
    WIN, UP, DOWN = slice(8, 48), slice(7, 47), slice(9, 49)

    @pl.loop(0, 22)
    def _(x):
        for k in range(4):
            cF[x, k, 4:8, :] = pk[0, x, k, 0:4, :]
            bF[x, k, 4:8, :] = pk[0, x, k, 4:8, :]
            cF[x, k, 40:44, :] = pk[1, x, k, 0:4, :]
            bF[x, k, 40:44, :] = pk[1, x, k, 4:8, :]

    def clear_planes(ref, first, count, condition):
        @pl.when(condition)
        def _():
            @pl.loop(first, first + count)
            def _(x):
                if ref.shape[1] == 4:
                    ref[x, :, 0:48, :] = jnp.zeros((4, 48, 128), F32)
                elif len(ref.shape) == 5:
                    for q in range(2):
                        ref[x, q, core] = jnp.zeros(ref.shape[3:], F32)
                else:
                    ref[x, core] = jnp.zeros(ref.shape[2:], F32)

    def clear_rows(ref, first, count, condition):
        zero = jnp.zeros((count, 128), F32)

        @pl.when(condition)
        def _():
            @pl.loop(0, ref.shape[0])
            def _(x):
                if ref.shape[1] == 4:
                    for k in range(4):
                        ref[x, k, first : first + count, :] = zero
                elif len(ref.shape) == 5:
                    for q in range(2):
                        ref[x, q, core, first : first + count, :] = zero
                else:
                    ref[x, core, first : first + count, :] = zero

    for ghost, cell, condition in ((2, 3, gx == 0), (19, 18, gx == nx - 1)):

        @pl.when(condition)
        def _(ghost=ghost, cell=cell):
            cF[ghost] = cF[cell]

    for ghost, cell, condition in ((7, 8, gy == 0), (40, 39, gy == ny - 1)):

        @pl.when(condition)
        def _(ghost=ghost, cell=cell):
            @pl.loop(0, 22)
            def _(x):
                for k in range(4):
                    cF[x, k, ghost : ghost + 1, :] = cF[x, k, cell : cell + 1, :]

    @pl.loop(1, 21)
    def _(x):
        low = roll_down(cF[x, 0, CWIN, :])
        high = roll_up(cF[x, 3, CWIN, :])
        eC[x, core, CWIN, :] = jnp.where(core == 0, low, high)

    edge_phase = 3 * other

    def swap(source, target, first, last, rows):
        return send(
            source.at[first:last, edge_phase, rows], target.at[first:last, core, rows], sibling
        )

    lane40 = lanes(40)

    def left_of(ref, edge, x, k, win):
        if k:
            return ref[x, k - 1, win, :]
        return roll_up(jnp.where(lane40 == 127, edge[x, 0, win, :], ref[x, 3, win, :]))

    def right_of(ref, edge, x, k, win):
        if k < 3:
            return ref[x, k + 1, win, :]
        return roll_down(jnp.where(lane40 == 0, edge[x, 1, win, :], ref[x, 0, win, :]))

    def planes(first, last, group, body):
        count = last - first

        @pl.loop(0, count // group)
        def _(j):
            for store_all in [body(first + j * group + u) for u in range(group)]:
                store_all()

        for store_all in [body(last - 1 - u) for u in range(count % group)]:
            store_all()

    INNER, OUTER = (1, 2), (0, 3)

    def setup_fine(phases):
        def body(x):
            results = []
            for k in phases:
                beside = [
                    cF[x - 1, k, CWIN, :], cF[x + 1, k, CWIN, :], cF[x, k, CUP, :], cF[x, k, CDOWN, :],
                    left_of(cF, eC, x, k, CWIN), right_of(cF, eC, x, k, CWIN),
                ]
                centre = cF[x, k, CWIN, :]
                pairs = [centre + value for value in beside]
                twice = ((pairs[0] + pairs[1]) + (pairs[2] + pairs[3])) + (pairs[4] + pairs[5])
                inverse = 1.0 / twice
                weights = [pair * inverse for pair in pairs]
                results.append((k, weights, 0.5 * twice, bF[x, k, CWIN, :] * inverse * (2.0 / THETA)))

            def store_all():
                for k, weights, diagonal, iterate in results:
                    for n, weight in enumerate(weights):
                        gF[n, x - 1, k] = weight
                    dF[x, k] = diagonal
                    xF[x, k, WIN, :] = iterate

            return store_all

        planes(1, 21, 4 // len(phases), body)

    def sum_fine(ref, edge, x, k):
        return (
            gF[0, x - 1, k] * ref[x - 1, k, WIN, :]
            + gF[1, x - 1, k] * ref[x + 1, k, WIN, :]
            + gF[2, x - 1, k] * ref[x, k, UP, :]
            + gF[3, x - 1, k] * ref[x, k, DOWN, :]
            + gF[4, x - 1, k] * left_of(ref, edge, x, k, WIN)
            + gF[5, x - 1, k] * right_of(ref, edge, x, k, WIN)
        )

    def sweep_fine(target, source, edge, first, last, phases, formula):
        def body(x):
            results = [(k, formula(x, k, sum_fine(source, edge, x, k))) for k in phases]

            def store_all():
                for k, value in results:
                    target[x, k, WIN, :] = value

            return store_all

        planes(first, last, (8 if (last - first) % 8 == 0 else 6) // len(phases), body)

    def edge_first(run, begin_swap):
        for position, phase in ((0, 3), (1, 0)):

            @pl.when(core == position)
            def _(phase=phase):
                run((phase,))

        copy = begin_swap()
        for position, phase in ((0, 0), (1, 3)):

            @pl.when(core == position)
            def _(phase=phase):
                run((phase,))

        return copy

    first = 1.0 + MOM + GAIN * (THETA - 1.0)

    def pre_step(x, k, total):
        return first * xF[x, k, WIN, :] + GAIN * total

    def residual(x, k, total):
        return dF[x, k] * (THETA * xF[x, k, WIN, :] - x2F[x, k, WIN, :] + total)

    copy = swap(cF, eC, 1, 21, slice(0, 48))
    rows_of = {0: (slice(16, 32), slice(16, 32)), -1: (slice(16, 24), slice(32, 40)), 1: (slice(24, 32), slice(8, 16))}
    planes_c1 = {0: (slice(4, 12), slice(4, 12)), -1: (slice(4, 8), slice(12, 16)), 1: (slice(8, 12), slice(0, 4))}
    halo_c1 = []
    for dx, dy in peers8:
        (xs, xd), (ys, yd) = planes_c1[dx], rows_of[dy]
        halo_c1.append(send(c1.at[xs, :, core, ys], c1.at[xd, :, core, yd], peer(dx, dy)))
    halo_c2 = [
        send(
            c2.at[8:12, core, 16:24],
            c2.at[8 - 4 * dx : 12 - 4 * dx, core, 16 - 8 * dy : 24 - 8 * dy],
            peer(dx, dy),
        )
        for dx, dy in peers14
    ]

    setup_fine(INNER)
    copy.wait()
    copy = edge_first(setup_fine, lambda: swap(xF, e1, 2, 20, WIN))
    for n, plane, condition in ((0, 2, gx == 0), (1, 17, gx == nx - 1)):

        @pl.when(condition)
        def _(n=n, plane=plane):
            gF[n, plane] = jnp.zeros((4, 40, 128), F32)

    for n, row, condition in ((2, 4, gy == 0), (3, 35, gy == ny - 1)):

        @pl.when(condition)
        def _(n=n, row=row):
            @pl.loop(1, 19)
            def _(x):
                for k in range(4):
                    gF[n, x, k, row : row + 1, :] = jnp.zeros((1, 128), F32)

    sweep_fine(x2F, xF, e1, 2, 20, INNER, pre_step)
    copy.wait()
    copy = edge_first(
        lambda phases: sweep_fine(x2F, xF, e1, 2, 20, phases, pre_step),
        lambda: swap(x2F, e2, 3, 19, WIN),
    )
    sweep_fine(rF, x2F, e2, 3, 19, INNER, residual)
    copy.wait()
    sweep_fine(rF, x2F, e2, 3, 19, OUTER, residual)

    for row, condition in ((8, gy == 0), (44, gy == ny - 1)):

        @pl.when(condition)
        def _(row=row):
            @pl.loop(3, 19)
            def _(x):
                for k in range(4):
                    rF[x, k, row : row + 4, :] = jnp.zeros((4, 128), F32)

    def restrict_xy(phases):
        def restrict_x(i):
            results = [
                0.125
                * (
                    rF[2 * i, k, WIN, :]
                    + 3.0 * (rF[2 * i + 1, k, WIN, :] + rF[2 * i + 2, k, WIN, :])
                    + rF[2 * i + 3, k, WIN, :]
                )
                for k in phases
            ]

            def store_all():
                for k, value in zip(phases, results):
                    t1[i, k, WIN, :] = value

            return store_all

        def restrict_y(i):
            results = []
            for k in phases:
                part = [t1[i, k, pl.ds(s, 16, stride=2), :] for s in (11, 12, 13, 14)]
                results.append(0.125 * (part[0] + 3.0 * (part[1] + part[2]) + part[3]))

            def store_all():
                for k, value in zip(phases, results):
                    t2[i, k] = value

            return store_all

        planes(0, 10, 5, restrict_x)
        planes(0, 10, 5, restrict_y)

    restrict_xy(OUTER)
    copy = send(t2.at[:, edge_phase], e3.at[:, core], sibling)
    restrict_xy(INNER)
    copy.wait()
    lane16 = lanes(16)

    def restrict_z(i):
        p = [t2[i, k] for k in range(4)]
        before = roll_up(jnp.where(lane16 == 127, e3[i, 0], p[3]))
        after = roll_down(jnp.where(lane16 == 0, e3[i, 1], p[0]))
        even = 0.125 * (before + 3.0 * (p[0] + p[1]) + p[2])
        odd = 0.125 * (p[1] + 3.0 * (p[2] + p[3]) + after)

        def store_all():
            b1[i + 3, 0, core, 16:32, :] = even
            b1[i + 3, 1, core, 16:32, :] = odd

        return store_all

    planes(0, 10, 5, restrict_z)

    halo_b1 = []
    for dx, dy in peers8:
        ys, yd = rows_of[dy]
        if dx == 0:
            halo_b1.append(send(b1.at[3:13, :, core, ys], b1.at[3:13, :, core, yd], peer(dx, dy)))
        else:
            xs, xd, near, side = (
                (slice(9, 11), slice(1, 3), slice(11, 13), 0)
                if dx == 1
                else (slice(5, 7), slice(13, 15), slice(3, 5), 1)
            )
            halo_b1.append(send(b1.at[near, :, core, ys], stg.at[side, :, :, yd], peer(dx, dy)))
            halo_b1.append(send(b1.at[xs, :, core, ys], b1.at[xd, :, core, yd], peer(dx, dy)))

    far = [
        send(x2F.at[17:18, :, WIN], x2F.at[1:2, :, WIN], peer(1, 0)),
        send(x2F.at[4:5, :, WIN], x2F.at[20:21, :, WIN], peer(-1, 0)),
    ]

    for copy in face_c + face_b + halo:
        copy.wait_send()
    for copy in halo_c1 + halo_c2:
        copy.wait()
    clear_planes(c1, 0, 4, gx == 0)
    clear_planes(c1, 12, 4, gx == nx - 1)
    clear_rows(c1, 8, 8, gy == 0)
    clear_rows(c1, 32, 8, gy == ny - 1)
    clear_planes(c2, 4, 4, gx == 0)
    clear_planes(c2, 0, 4, gx <= 1)
    clear_planes(c2, 12, 4, gx == nx - 1)
    clear_planes(c2, 16, 4, gx >= nx - 2)
    clear_rows(c2, 8, 8, gy == 0)
    clear_rows(c2, 24, 8, gy == ny - 1)
    hand = [
        send(c1.at[:, :, core, 8:40], c1.at[:, :, core, 8:40], sibling),
        send(c2.at[:, core, 8:32], c2.at[:, core, 8:32], sibling),
    ]
    for copy in hand:
        copy.wait()

    lane32, lane24 = lanes(32), lanes(24)
    WL, UL, DL = slice(8, 40), slice(7, 39), slice(9, 41)
    W2, U2, D2 = slice(8, 32), slice(7, 31), slice(9, 33)

    def before_pair(halves, lane):
        turned = [roll_up(half) for half in halves]
        return [jnp.where(lane == 0, 0.0, turned[0]), jnp.where(lane == 0, turned[0], turned[1])]

    def after_pair(halves, lane):
        turned = [roll_down(half) for half in halves]
        return [jnp.where(lane == 127, turned[1], turned[0]), jnp.where(lane == 127, 0.0, turned[1])]

    def z_mid(ref, x):
        p0 = [ref[x, 0, t, WL, :] for t in range(2)]
        p1 = [ref[x, 1, t, WL, :] for t in range(2)]
        return [(before_pair(p1, lane32), p1), (p0, after_pair(p0, lane32))]

    @pl.loop(1, 15)
    def _(x):
        z_list = z_mid(c1, x)
        for q in range(2):
            for t in range(2):
                beside = [
                    c1[x - 1, q, t, WL, :], c1[x + 1, q, t, WL, :], c1[x, q, t, UL, :], c1[x, q, t, DL, :],
                    z_list[q][0][t], z_list[q][1][t],
                ]
                weights, diagonal, inverse = operator_parts(c1[x, q, t, WL, :], beside)
                for n, weight in enumerate(weights):
                    gL[n, x - 1, q, t] = weight
                dL[x, q, t] = diagonal
                x0L[x, q, t, WL, :] = inverse * (1.0 / THETA)

    def setup_low(first, last):
        @pl.loop(first, last)
        def _(x):
            halves = [c2[x, t, W2, :] for t in range(2)]
            low, high = before_pair(halves, lane24), after_pair(halves, lane24)
            for t in range(2):
                beside = [
                    c2[x - 1, t, W2, :], c2[x + 1, t, W2, :], c2[x, t, U2, :], c2[x, t, D2, :], low[t], high[t],
                ]
                weights, _, inverse = operator_parts(halves[t], beside)
                for n, weight in enumerate(weights):
                    g2[n, x - 1, t] = weight
                inv2[x, t] = inverse

    setup_low(8, 12)

    def scale_mid(first, last):
        def body(x):
            results = [b1[x, q, core, WL, :] * x0L[x, q, core, WL, :] for q in range(2)]

            def store_all():
                for q in range(2):
                    x1L[x, q, core, WL, :] = results[q]

            return store_all

        planes(first, last, 2, body)

        return send(
            x1L.at[first:last, :, core, 8:40], x1L.at[first:last, :, core, 8:40], sibling
        )

    for copy in halo_b1[-2:]:
        copy.wait()
    handed = [scale_mid(5, 11)]
    for copy in halo_b1[:-2]:
        copy.wait()
    for side, at in ((0, 3), (1, 11)):

        @pl.when((gx > 0) if side == 0 else (gx < nx - 1))
        def _(side=side, at=at):
            for n in range(2):
                for q in range(2):
                    b1[at + n, q, core, WL, :] = b1[at + n, q, core, WL, :] + stg[side, n, q, WL, :]

    handed += [scale_mid(1, 5), scale_mid(11, 15)]
    for copy in handed:
        copy.wait()

    def sum_mid(ref, x):
        z_list = z_mid(ref, x)
        return {
            (q, t): gL[0, x - 1, q, t] * ref[x - 1, q, t, WL, :]
            + gL[1, x - 1, q, t] * ref[x + 1, q, t, WL, :]
            + gL[2, x - 1, q, t] * ref[x, q, t, UL, :]
            + gL[3, x - 1, q, t] * ref[x, q, t, DL, :]
            + gL[4, x - 1, q, t] * z_list[q][0][t]
            + gL[5, x - 1, q, t] * z_list[q][1][t]
            for q in range(2)
            for t in range(2)
        }

    def sweep_mid(target, source, first, last, formula):
        def body(x):
            results = {at: formula(x, *at, total) for at, total in sum_mid(source, x).items()}

            def store_all():
                for (q, t), value in results.items():
                    target[x, q, t, WL, :] = value

            return store_all

        planes(first, last, 2, body)

    sweep_mid(
        x2L, x1L, 2, 14, lambda x, q, t, total: first * x1L[x, q, t, WL, :] + GAIN * total
    )
    sweep_mid(
        xpL, x2L, 3, 13,
        lambda x, q, t, total: dL[x, q, t] * (THETA * x1L[x, q, t, WL, :] - x2L[x, q, t, WL, :] + total),
    )

    lane8 = lanes(8)

    for i in range(4):
        for q in range(2):
            for t in range(2):
                t1[i, 2 * q + t, WL, :] = 0.125 * (
                    xpL[2 * i + 3, q, t, WL, :]
                    + 3.0 * (xpL[2 * i + 4, q, t, WL, :] + xpL[2 * i + 5, q, t, WL, :])
                    + xpL[2 * i + 6, q, t, WL, :]
                )
    for i in range(4):
        coarse = []
        for q in range(2):
            halves = []
            for t in range(2):
                part = [t1[i, 2 * q + t, pl.ds(s, 8, stride=2), :] for s in (15, 16, 17, 18)]
                halves.append(0.125 * (part[0] + 3.0 * (part[1] + part[2]) + part[3]))
            coarse.append(halves)
        low, high = before_pair(coarse[1], lane8), after_pair(coarse[0], lane8)
        pair = [0.125 * (low[t] + 3.0 * (coarse[0][t] + coarse[1][t]) + high[t]) for t in range(2)]
        mine = jnp.where(core == 0, pair[0], pair[1])
        bd2[i + 8, core, 16:24, :] = mine * inv2[i + 8, core, 8:16, :]

    halo_b2 = [
        send(
            bd2.at[8:12, core, 16:24],
            bd2.at[8 - 4 * dx : 12 - 4 * dx, core, 16 - 8 * dy : 24 - 8 * dy],
            peer(dx, dy),
        )
        for dx, dy in peers14
    ]
    far_mid = [
        send(x2L.at[8:10, :, :, 8:40], x2L.at[0:2, :, :, 8:40], peer(1, 0)),
        send(x2L.at[6:8, :, :, 8:40], x2L.at[14:16, :, :, 8:40], peer(-1, 0)),
    ]
    setup_low(1, 8)
    setup_low(12, 19)
    handed = []
    for group in (0, 1, 2):
        for (dx, dy), copy in zip(peers14, halo_b2):
            if abs(dx) == group:
                copy.wait()
        for at in sorted({8 - 4 * group, 8 + 4 * group}):
            block = bd2.at[at : at + 4, core, 8:32]
            handed.append(send(block, block, sibling))
    for copy in handed:
        copy.wait()

    def begin_low(x):
        scaled = [jnp.where(c2[x, t, W2, :] > 0.0, bd2[x, t, W2, :], 0.0) for t in range(2)]

        def store_all():
            for t in range(2):
                bd2[x, t, W2, :] = scaled[t]
                d2[x, t] = scaled[t] * (1.0 / THETA_LOW)
                xa[x, t, W2, :] = scaled[t] * (1.0 / THETA_LOW)

        return store_all

    planes(0, 20, 5, begin_low)

    now, later = xa, xb
    for number, (mom, gain) in enumerate(STEPS_LOW):

        def body(x, now=now, later=later, mom=mom, gain=gain):
            halves = [now[x, t, W2, :] for t in range(2)]
            low, high = before_pair(halves, lane24), after_pair(halves, lane24)
            steps = []
            for t in range(2):
                total = (
                    g2[0, x - 1, t] * now[x - 1, t, W2, :]
                    + g2[1, x - 1, t] * now[x + 1, t, W2, :]
                    + g2[2, x - 1, t] * now[x, t, U2, :]
                    + g2[3, x - 1, t] * now[x, t, D2, :]
                    + g2[4, x - 1, t] * low[t]
                    + g2[5, x - 1, t] * high[t]
                )
                steps.append(mom * d2[x, t] + gain * (bd2[x, t, W2, :] - halves[t] + total))

            def store_all():
                for t in range(2):
                    d2[x, t] = steps[t]
                    later[x, t, W2, :] = halves[t] + steps[t]

            return store_all

        planes(number + 1, 19 - number, 6, body)
        now, later = later, now
    bottom = now

    for copy in far_mid:
        copy.wait()

    def prolong_mid(i):
        results = []
        for odd in range(2):
            mixed = [
                0.75 * bottom[i + 6, t, W2, :] + 0.25 * bottom[i + 5 + 2 * odd, t, W2, :]
                for t in range(2)
            ]
            low, high = before_pair(mixed, lane24), after_pair(mixed, lane24)
            for q, side in ((0, low), (1, high)):
                for t in range(2):
                    results.append((odd, 2 * q + t, 0.75 * mixed[t] + 0.25 * side[t]))

        def store_all():
            for odd, slot, value in results:
                bF[2 * i + odd, slot, W2, :] = value

        return store_all

    def prolong_mid_rows(x):
        results = []
        for slot in range(4):
            centre = 0.75 * bF[x, slot, 12:28, :]
            results.append(
                (centre + 0.25 * bF[x, slot, 11:27, :], centre + 0.25 * bF[x, slot, 13:29, :])
            )

        def store_all():
            for slot, (even, odd) in enumerate(results):
                x0L[x, slot // 2, slot % 2, pl.ds(8, 16, stride=2), :] = even
                x0L[x, slot // 2, slot % 2, pl.ds(9, 16, stride=2), :] = odd

        return store_all

    def correct_mid(x):
        results = [
            (q, t, jnp.where(c1[x, q, t, WL, :] > 0.0, x2L[x, q, t, WL, :] + x0L[x, q, t, WL, :], 0.0))
            for q in range(2)
            for t in range(2)
        ]

        def store_all():
            for q, t, value in results:
                x0L[x, q, t, WL, :] = value

        return store_all

    planes(0, 8, 2, prolong_mid)
    planes(0, 16, 4, prolong_mid_rows)
    planes(0, 16, 2, correct_mid)

    def post_first(x, q, t, total):
        start = x0L[x, q, t, WL, :]
        return start + (THETA * x1L[x, q, t, WL, :] - start + total) * (1.0 / THETA)

    def post_second(x, q, t, total):
        here = xpL[x, q, t, WL, :]
        return (
            here
            + MOM * (here - x0L[x, q, t, WL, :])
            + GAIN * (THETA * x1L[x, q, t, WL, :] - here + total)
        )

    sweep_mid(xpL, x0L, 1, 15, post_first)
    sweep_mid(x2L, xpL, 2, 14, post_second)

    for copy in far:
        copy.wait()
    has_left = jnp.where(core == 1, 1.0, 0.0)
    has_right = jnp.where(core == 0, 1.0, 0.0)

    def prolong_fine(i):
        results = []
        for odd in range(2):

            def mixed(q, t):
                return 0.75 * x2L[i + 3, q, t, WL, :] + 0.25 * x2L[i + 2 + 2 * odd, q, t, WL, :]

            m0, m1 = mixed(0, core), mixed(1, core)
            before = roll_up(jnp.where(lane32 == 127, has_left * mixed(1, other), m1))
            after = roll_down(jnp.where(lane32 == 0, has_right * mixed(0, other), m0))
            results.append(
                (
                    0.75 * m0 + 0.25 * before, 0.75 * m0 + 0.25 * m1,
                    0.75 * m1 + 0.25 * m0, 0.75 * m1 + 0.25 * after,
                )
            )

        def store_all():
            for odd in range(2):
                for k in range(4):
                    bF[2 * i + 1 + odd, k, WL, :] = results[odd][k]

        return store_all

    def prolong_fine_rows(x):
        results = []
        for k in range(4):
            centre = 0.75 * bF[x, k, 14:34, :]
            results.append((centre + 0.25 * bF[x, k, 13:33, :], centre + 0.25 * bF[x, k, 15:35, :]))

        def store_all():
            for k, (even, odd) in enumerate(results):
                cF[x, k, pl.ds(8, 20, stride=2), :] = even
                cF[x, k, pl.ds(9, 20, stride=2), :] = odd

        return store_all

    def correct_fine(x):
        results = [cF[x, k, WIN, :] + x2F[x, k, WIN, :] for k in range(4)]

        def store_all():
            for k in range(4):
                cF[x, k, WIN, :] = results[k]

        return store_all

    planes(0, 10, 1, prolong_fine)
    planes(1, 21, 2, prolong_fine_rows)
    planes(1, 21, 2, correct_fine)

    def last_first(x, k, total):
        start = cF[x, k, WIN, :]
        return start + (THETA * xF[x, k, WIN, :] - start + total) * (1.0 / THETA)

    def last_second(x, k, total):
        here = rF[x, k, WIN, :]
        return (
            here
            + MOM * (here - cF[x, k, WIN, :])
            + GAIN * (THETA * xF[x, k, WIN, :] - here + total)
        )

    copy = swap(cF, e1, 2, 20, WIN)
    sweep_fine(rF, cF, e1, 2, 20, INNER, last_first)
    copy.wait()
    copy = edge_first(
        lambda phases: sweep_fine(rF, cF, e1, 2, 20, phases, last_first),
        lambda: swap(rF, e2, 3, 19, WIN),
    )
    sweep_fine(x2F, rF, e2, 3, 19, INNER, last_second)
    copy.wait()
    sweep_fine(x2F, rF, e2, 3, 19, OUTER, last_second)

    def store(part):
        planes_of = pl.ds(part * 4, 4)
        return pltpu.make_async_copy(out_vm.at[planes_of], out_hbm.at[planes_of], local_sem.at[2 + part])

    for part in range(4):
        total = None
        for k in range(4):
            rows = x2F[part * 4 + 3 : part * 4 + 7, k, 12:44, :].reshape(128, 128)
            high = rows.astype(BF16)
            low = (rows - high.astype(F32)).astype(BF16)
            table = perm[:, k * 128 : (k + 1) * 128]
            for piece in (high, low):
                product = lax.dot_general(piece, table, (((1,), (1,)), ((), ())), preferred_element_type=F32)
                total = product if total is None else total + product
        out_vm[part * 4 : part * 4 + 4] = total.reshape(4, 32, 512)
        store(part).start()
    for part in range(4):
        store(part).wait()


def copy_kernel(source, target, buffer, read_sem, write_sem):
    reads, writes = [], []
    for n in range(8):
        part = pl.ds(2 * n, 2)
        reads.append(pltpu.make_async_copy(source.at[part], buffer.at[part], read_sem.at[n]))
        writes.append(pltpu.make_async_copy(buffer.at[part], target.at[part], write_sem.at[n]))
    for copy in reads:
        copy.start()
    for copy, after in zip(reads, writes):
        copy.wait()
        after.start()
    for copy in writes:
        copy.wait()


def local(right_side, coefficient):
    def vmem(*shape):
        return pltpu.VMEM(shape, F32)

    inputs, fine, mid, low = (22, 4, 48, 128), (22, 4, 56, 128), (16, 2, 2, 48, 128), (20, 2, 40, 128)
    edge = (22, 2, 48, 128)
    scratch = [
        vmem(16, 32, 512), vmem(16, 32, 512), vmem(16, 32, 512), pltpu.VMEM((512, 512), BF16),
        vmem(*fine), vmem(*inputs), vmem(*fine), vmem(*fine), vmem(22, 4, 40, 128), vmem(*fine), vmem(6, 20, 4, 40, 128),
        vmem(*edge), vmem(*edge), vmem(*edge),
        vmem(2, 3, 32, 512), vmem(2, 2, 32, 512), vmem(2, 16, 8, 512), vmem(2, 22, 8, 512), vmem(2, 22, 4, 8, 128),
        vmem(10, 4, 48, 128), vmem(10, 4, 16, 128), vmem(10, 2, 16, 128),
        vmem(*mid), vmem(*mid), vmem(*mid), vmem(*mid), vmem(*mid), vmem(*mid), vmem(16, 2, 2, 32, 128),
        vmem(6, 14, 2, 2, 32, 128), vmem(2, 2, 2, 48, 128), vmem(2, 2, 2, 48, 128),
        vmem(*low), vmem(*low), vmem(*low), vmem(*low), vmem(20, 2, 24, 128), vmem(20, 2, 24, 128),
        vmem(6, 18, 2, 24, 128), vmem(2, 2, 2, 40, 128),
        pltpu.SemaphoreType.DMA((6,)), pltpu.SemaphoreType.DMA((80,)), pltpu.SemaphoreType.DMA((80,)),
    ]
    result = pl.pallas_call(
        kernel,
        out_shape=jax.ShapeDtypeStruct((16, 32, 512), F32),
        in_specs=[pl.BlockSpec(memory_space=pl.ANY)] * 2,
        out_specs=pl.BlockSpec(memory_space=pl.ANY),
        scratch_shapes=scratch,
        compiler_params=pltpu.CompilerParams(
            collective_id=0, has_side_effects=True, vmem_limit_bytes=63 * 2**20
        ),
    )(right_side, coefficient)
    return pl.pallas_call(
        copy_kernel,
        out_shape=jax.ShapeDtypeStruct((16, 32, 512), F32),
        in_specs=[pl.BlockSpec(memory_space=pl.ANY)],
        out_specs=pl.BlockSpec(memory_space=pl.ANY),
        scratch_shapes=[vmem(16, 32, 512), pltpu.SemaphoreType.DMA((8,)), pltpu.SemaphoreType.DMA((8,))],
    )(result)


def solution(mesh):
    return jax.shard_map(
        local,
        mesh=mesh,
        in_specs=(P("gx", "gy", "gz"), P("gx", "gy", "gz")),
        out_specs=P("gx", "gy", "gz"),
        check_vma=False,
    )
```

```python
import functools

import jax
import jax.numpy as jnp
from jax import lax
from jax.experimental import pallas as pl
from jax.experimental.pallas import tpu as pltpu
from jax.sharding import PartitionSpec as P

MESH = pl.DeviceIdType.MESH
F32 = jnp.float32
BF16 = jnp.bfloat16


def cheb_constants(sweeps, lower_edge, upper_edge):
    theta = 0.5 * (upper_edge + lower_edge)
    delta = 0.5 * (upper_edge - lower_edge)
    sigma = theta / delta
    rho = 1.0 / sigma
    steps = []
    for _ in range(1, sweeps):
        rho_next = 1.0 / (2.0 * sigma - rho)
        steps.append((rho_next * rho, 2.0 * rho_next / delta))
        rho = rho_next
    return theta, steps


THETA, ((MOM, GAIN),) = cheb_constants(2, 0.3, 2.0)
THETA_LOW, STEPS_LOW = cheb_constants(6, 0.05, 2.0)


def lanes(rows):
    return lax.broadcasted_iota(jnp.int32, (rows, 128), 1)


def roll_up(value):
    return pltpu.roll(value, 1, 1)


def roll_down(value):
    return pltpu.roll(value, 127, 1)


def operator_parts(centre, beside):
    faces = []
    diagonal = None
    for other in beside:
        face = jnp.where(other > 0.0, 0.5 * (centre + other), centre)
        diagonal = face if diagonal is None else diagonal + face
        faces.append(jnp.where(other > 0.0, face, 0.0))
    inside = centre > 0.0
    inverse = jnp.where(inside, 1.0 / diagonal, 0.0)
    diagonal = jnp.where(inside, diagonal, 0.0)
    return [face * inverse for face in faces], diagonal, inverse


def kernel(
    b_hbm, c_hbm, out_hbm,
    out_vm, b_in, c_in, perm,
    cF, bF, xF, x2F, dF, rF, gF, eC, e1, e2, face_c_in, face_b_in, pk_out, pk_in, pk,
    t1, t2, e3,
    c1, b1, x1L, x2L, x0L, xpL, dL, gL, stg, tL,
    c2, bd2, xa, xb, d2, inv2, g2, t3,
    local_sem, ss, rs,
):
    gx, gy, core = lax.axis_index("gx"), lax.axis_index("gy"), lax.axis_index("gz")
    nx, ny = lax.axis_size("gx"), lax.axis_size("gy")
    other = 1 - core
    sibling = (gx, gy, other)
    counter = [0]

    def peer(dx, dy):
        return (lax.rem(gx + dx + nx, nx), lax.rem(gy + dy + ny, ny), core)

    def send(src, dst, device):
        number = counter[0]
        counter[0] += 1
        copy = pltpu.make_async_remote_copy(
            src_ref=src, dst_ref=dst, send_sem=ss.at[number], recv_sem=rs.at[number],
            device_id=device, device_id_type=MESH,
        )
        copy.start()
        return copy

    peers14 = [(dx, dy) for dx in (-2, 2, -1, 1, 0) for dy in (-1, 1, 0) if (dx, dy) != (0, 0)]
    peers8 = [(dx, dy) for dx, dy in peers14 if abs(dx) < 2]
    barrier = pltpu.get_barrier_semaphore()
    for dx, dy in peers8:
        pl.semaphore_signal(barrier, inc=1, device_id=peer(dx, dy), device_id_type=MESH)
    pl.semaphore_signal(barrier, inc=1, device_id=sibling, device_id_type=MESH)
    load_c = pltpu.make_async_copy(c_hbm, c_in, local_sem.at[0])
    load_b = pltpu.make_async_copy(b_hbm, b_in, local_sem.at[1])
    load_c.start()
    load_b.start()
    pl.semaphore_wait(barrier, len(peers8) + 1)
    face_c = [
        send(c_hbm.at[0:3], face_c_in.at[1], peer(-1, 0)),
        send(c_hbm.at[13:16], face_c_in.at[0], peer(1, 0)),
    ]
    load_c.wait()
    load_b.wait()

    @pl.loop(0, 16)
    def _(x):
        for side, rows in ((0, slice(0, 4)), (1, slice(28, 32))):
            pk_out[side, x, 0:4, :] = c_in[x, rows, :]
            pk_out[side, x, 4:8, :] = b_in[x, rows, :]

    halo = [
        send(pk_out.at[0], pk_in.at[1, 3:19], peer(0, -1)),
        send(pk_out.at[1], pk_in.at[0, 3:19], peer(0, 1)),
        send(pk_out.at[0, 0:3], pk_in.at[1, 19:22], peer(-1, -1)),
        send(pk_out.at[0, 13:16], pk_in.at[1, 0:3], peer(1, -1)),
        send(pk_out.at[1, 0:3], pk_in.at[0, 19:22], peer(-1, 1)),
        send(pk_out.at[1, 13:16], pk_in.at[0, 0:3], peer(1, 1)),
    ]
    face_b = [
        send(b_hbm.at[0:2], face_b_in.at[1], peer(-1, 0)),
        send(b_hbm.at[14:16], face_b_in.at[0], peer(1, 0)),
    ]

    @pl.loop(0, 4)
    def _(j):
        z = lax.broadcasted_iota(jnp.int32, (128, 512), 0) + j * 128
        col = lax.broadcasted_iota(jnp.int32, (128, 512), 1)
        perm[pl.ds(pl.multiple_of(j * 128, 128), 128), :] = jnp.where(
            z == 4 * (col % 128) + col // 128, 1.0, 0.0
        ).astype(BF16)

    def spread(rows):
        high = rows.astype(BF16)
        low = (rows - high.astype(F32)).astype(BF16)
        table = perm[...]
        result = jnp.dot(high, table, preferred_element_type=F32) + jnp.dot(
            low, table, preferred_element_type=F32
        )
        return [result[:, k * 128 : (k + 1) * 128] for k in range(4)]

    for source, target in ((c_in, cF), (b_in, bF)):

        @pl.loop(0, 2)
        def _(half, source=source, target=target):
            for k, part in enumerate(spread(source[pl.ds(half * 8, 8)].reshape(256, 512))):
                target[pl.ds(half * 8 + 3, 8), k, 8:40, :] = part.reshape(8, 32, 128)

    @pl.loop(0, 22)
    def _(x):
        for ref in (e1, e2):
            ref[x, core] = jnp.zeros((48, 128), F32)

    @pl.loop(0, 10)
    def _(x):
        e3[x, core] = jnp.zeros((16, 128), F32)

    @pl.loop(0, 3)
    def _(x):
        rF[x, :, 8:48, :] = jnp.zeros((4, 40, 128), F32)
        rF[x + 19, :, 8:48, :] = jnp.zeros((4, 40, 128), F32)

    @pl.loop(0, 8)
    def _(i):
        for k in range(4):
            t1[0, k, 8:40, :] = cF[2 * i + 3, k, 8:40, :] + cF[2 * i + 4, k, 8:40, :]
        for q in range(2):
            total = None
            for k in (2 * q, 2 * q + 1):
                for start in (8, 9):
                    part = t1[0, k, pl.ds(start, 16, stride=2), :]
                    total = part if total is None else total + part
            c1[i + 4, q, core, 16:32, :] = total * (0.125 * 0.25)

    @pl.loop(0, 4)
    def _(i):
        total = None
        for q in range(2):
            tL[0, q, 0, 16:32, :] = c1[2 * i + 4, q, core, 16:32, :] + c1[2 * i + 5, q, core, 16:32, :]
            for start in (16, 17):
                part = tL[0, q, 0, pl.ds(start, 8, stride=2), :]
                total = part if total is None else total + part
        c2[i + 8, core, 16:24, :] = total * (0.125 * 0.25)

    def spread_faces(arrived, target, depth, low, high):
        for side, at in ((0, low), (1, high)):
            for k, part in enumerate(spread(arrived[side].reshape(depth * 32, 512))):
                target[at : at + depth, k, 8:40, :] = part.reshape(depth, 32, 128)

    for copy in face_c:
        copy.wait_recv()
    spread_faces(face_c_in, cF, 3, 0, 19)
    for copy in halo:
        copy.wait_recv()
    for side in range(2):
        for k, part in enumerate(spread(pk_in[side].reshape(176, 512))):
            pk[side, :, k, :, :] = part.reshape(22, 8, 128)

    CWIN, CUP, CDOWN = slice(4, 44), slice(3, 43), slice(5, 45)
    WIN, UP, DOWN = slice(8, 48), slice(7, 47), slice(9, 49)

    @pl.loop(0, 22)
    def _(x):
        for k in range(4):
            cF[x, k, 4:8, :] = pk[0, x, k, 0:4, :]
            bF[x, k, 4:8, :] = pk[0, x, k, 4:8, :]
            cF[x, k, 40:44, :] = pk[1, x, k, 0:4, :]
            bF[x, k, 40:44, :] = pk[1, x, k, 4:8, :]

    def clear_planes(ref, first, count, condition):
        @pl.when(condition)
        def _():
            @pl.loop(first, first + count)
            def _(x):
                if ref.shape[1] == 4:
                    ref[x, :, 0:48, :] = jnp.zeros((4, 48, 128), F32)
                elif len(ref.shape) == 5:
                    for q in range(2):
                        ref[x, q, core] = jnp.zeros(ref.shape[3:], F32)
                else:
                    ref[x, core] = jnp.zeros(ref.shape[2:], F32)

    def clear_rows(ref, first, count, condition):
        zero = jnp.zeros((count, 128), F32)

        @pl.when(condition)
        def _():
            @pl.loop(0, ref.shape[0])
            def _(x):
                if ref.shape[1] == 4:
                    for k in range(4):
                        ref[x, k, first : first + count, :] = zero
                elif len(ref.shape) == 5:
                    for q in range(2):
                        ref[x, q, core, first : first + count, :] = zero
                else:
                    ref[x, core, first : first + count, :] = zero

    for ghost, cell, condition in ((2, 3, gx == 0), (19, 18, gx == nx - 1)):

        @pl.when(condition)
        def _(ghost=ghost, cell=cell):
            cF[ghost] = cF[cell]

    for ghost, cell, condition in ((7, 8, gy == 0), (40, 39, gy == ny - 1)):

        @pl.when(condition)
        def _(ghost=ghost, cell=cell):
            @pl.loop(0, 22)
            def _(x):
                for k in range(4):
                    cF[x, k, ghost : ghost + 1, :] = cF[x, k, cell : cell + 1, :]

    @pl.loop(1, 21)
    def _(x):
        low = roll_down(cF[x, 0, CWIN, :])
        high = roll_up(cF[x, 3, CWIN, :])
        eC[x, core, CWIN, :] = jnp.where(core == 0, low, high)

    edge_phase = 3 * other

    def swap(source, target, first, last, rows):
        return send(
            source.at[first:last, edge_phase, rows], target.at[first:last, core, rows], sibling
        )

    lane40 = lanes(40)

    def left_of(ref, edge, x, k, win):
        if k:
            return ref[x, k - 1, win, :]
        return roll_up(jnp.where(lane40 == 127, edge[x, 0, win, :], ref[x, 3, win, :]))

    def right_of(ref, edge, x, k, win):
        if k < 3:
            return ref[x, k + 1, win, :]
        return roll_down(jnp.where(lane40 == 0, edge[x, 1, win, :], ref[x, 0, win, :]))

    def planes(first, last, group, body):
        count = last - first

        @pl.loop(0, count // group)
        def _(j):
            for store_all in [body(first + j * group + u) for u in range(group)]:
                store_all()

        for store_all in [body(last - 1 - u) for u in range(count % group)]:
            store_all()

    INNER, OUTER = (1, 2), (0, 3)

    def setup_fine(phases):
        def body(x):
            results = []
            for k in phases:
                beside = [
                    cF[x - 1, k, CWIN, :], cF[x + 1, k, CWIN, :], cF[x, k, CUP, :], cF[x, k, CDOWN, :],
                    left_of(cF, eC, x, k, CWIN), right_of(cF, eC, x, k, CWIN),
                ]
                centre = cF[x, k, CWIN, :]
                pairs = [centre + value for value in beside]
                twice = ((pairs[0] + pairs[1]) + (pairs[2] + pairs[3])) + (pairs[4] + pairs[5])
                inverse = 1.0 / twice
                weights = [pair * inverse for pair in pairs]
                results.append((k, weights, 0.5 * twice, bF[x, k, CWIN, :] * inverse * (2.0 / THETA)))

            def store_all():
                for k, weights, diagonal, iterate in results:
                    for n, weight in enumerate(weights):
                        gF[n, x - 1, k] = weight
                    dF[x, k] = diagonal
                    xF[x, k, WIN, :] = iterate

            return store_all

        planes(1, 21, 4 // len(phases), body)

    def sum_fine(ref, edge, x, k):
        return (
            gF[0, x - 1, k] * ref[x - 1, k, WIN, :]
            + gF[1, x - 1, k] * ref[x + 1, k, WIN, :]
            + gF[2, x - 1, k] * ref[x, k, UP, :]
            + gF[3, x - 1, k] * ref[x, k, DOWN, :]
            + gF[4, x - 1, k] * left_of(ref, edge, x, k, WIN)
            + gF[5, x - 1, k] * right_of(ref, edge, x, k, WIN)
        )

    def sweep_fine(target, source, edge, first, last, phases, formula):
        def body(x):
            results = [(k, formula(x, k, sum_fine(source, edge, x, k))) for k in phases]

            def store_all():
                for k, value in results:
                    target[x, k, WIN, :] = value

            return store_all

        planes(first, last, 6 // len(phases), body)

    def edge_first(run, begin_swap):
        for position, phase in ((0, 3), (1, 0)):

            @pl.when(core == position)
            def _(phase=phase):
                run((phase,))

        copy = begin_swap()
        for position, phase in ((0, 0), (1, 3)):

            @pl.when(core == position)
            def _(phase=phase):
                run((phase,))

        return copy

    first = 1.0 + MOM + GAIN * (THETA - 1.0)

    def pre_step(x, k, total):
        return first * xF[x, k, WIN, :] + GAIN * total

    def residual(x, k, total):
        return dF[x, k] * (THETA * xF[x, k, WIN, :] - x2F[x, k, WIN, :] + total)

    copy = swap(cF, eC, 1, 21, slice(0, 48))
    rows_of = {0: (slice(16, 32), slice(16, 32)), -1: (slice(16, 24), slice(32, 40)), 1: (slice(24, 32), slice(8, 16))}
    planes_c1 = {0: (slice(4, 12), slice(4, 12)), -1: (slice(4, 8), slice(12, 16)), 1: (slice(8, 12), slice(0, 4))}
    halo_c1 = []
    for dx, dy in peers8:
        (xs, xd), (ys, yd) = planes_c1[dx], rows_of[dy]
        halo_c1.append(send(c1.at[xs, :, core, ys], c1.at[xd, :, core, yd], peer(dx, dy)))
    halo_c2 = [
        send(
            c2.at[8:12, core, 16:24],
            c2.at[8 - 4 * dx : 12 - 4 * dx, core, 16 - 8 * dy : 24 - 8 * dy],
            peer(dx, dy),
        )
        for dx, dy in peers14
    ]

    for face in face_b:
        face.wait_recv()
    spread_faces(face_b_in, bF, 2, 1, 19)
    setup_fine(INNER)
    copy.wait()
    copy = edge_first(setup_fine, lambda: swap(xF, e1, 2, 20, WIN))
    for n, plane, condition in ((0, 2, gx == 0), (1, 17, gx == nx - 1)):

        @pl.when(condition)
        def _(n=n, plane=plane):
            gF[n, plane] = jnp.zeros((4, 40, 128), F32)

    for n, row, condition in ((2, 4, gy == 0), (3, 35, gy == ny - 1)):

        @pl.when(condition)
        def _(n=n, row=row):
            @pl.loop(1, 19)
            def _(x):
                for k in range(4):
                    gF[n, x, k, row : row + 1, :] = jnp.zeros((1, 128), F32)

    sweep_fine(x2F, xF, e1, 2, 20, INNER, pre_step)
    copy.wait()
    copy = edge_first(
        lambda phases: sweep_fine(x2F, xF, e1, 2, 20, phases, pre_step),
        lambda: swap(x2F, e2, 3, 19, WIN),
    )
    sweep_fine(rF, x2F, e2, 3, 19, INNER, residual)
    copy.wait()
    sweep_fine(rF, x2F, e2, 3, 19, OUTER, residual)

    for row, condition in ((8, gy == 0), (44, gy == ny - 1)):

        @pl.when(condition)
        def _(row=row):
            @pl.loop(3, 19)
            def _(x):
                for k in range(4):
                    rF[x, k, row : row + 4, :] = jnp.zeros((4, 128), F32)

    def restrict_xy(phases):
        def restrict_x(i):
            results = [
                0.125
                * (
                    rF[2 * i, k, WIN, :]
                    + 3.0 * (rF[2 * i + 1, k, WIN, :] + rF[2 * i + 2, k, WIN, :])
                    + rF[2 * i + 3, k, WIN, :]
                )
                for k in phases
            ]

            def store_all():
                for k, value in zip(phases, results):
                    t1[i, k, WIN, :] = value

            return store_all

        def restrict_y(i):
            results = []
            for k in phases:
                part = [t1[i, k, pl.ds(s, 16, stride=2), :] for s in (11, 12, 13, 14)]
                results.append(0.125 * (part[0] + 3.0 * (part[1] + part[2]) + part[3]))

            def store_all():
                for k, value in zip(phases, results):
                    t2[i, k] = value

            return store_all

        planes(0, 10, 5, restrict_x)
        planes(0, 10, 5, restrict_y)

    restrict_xy(OUTER)
    copy = send(t2.at[:, edge_phase], e3.at[:, core], sibling)
    restrict_xy(INNER)
    copy.wait()
    lane16 = lanes(16)

    def restrict_z(i):
        p = [t2[i, k] for k in range(4)]
        before = roll_up(jnp.where(lane16 == 127, e3[i, 0], p[3]))
        after = roll_down(jnp.where(lane16 == 0, e3[i, 1], p[0]))
        even = 0.125 * (before + 3.0 * (p[0] + p[1]) + p[2])
        odd = 0.125 * (p[1] + 3.0 * (p[2] + p[3]) + after)

        def store_all():
            b1[i + 3, 0, core, 16:32, :] = even
            b1[i + 3, 1, core, 16:32, :] = odd

        return store_all

    planes(0, 10, 5, restrict_z)

    halo_b1 = []
    for dx, dy in peers8:
        ys, yd = rows_of[dy]
        if dx == 0:
            halo_b1.append(send(b1.at[3:13, :, core, ys], b1.at[3:13, :, core, yd], peer(dx, dy)))
        else:
            xs, xd, near, side = (
                (slice(9, 11), slice(1, 3), slice(11, 13), 0)
                if dx == 1
                else (slice(5, 7), slice(13, 15), slice(3, 5), 1)
            )
            halo_b1.append(send(b1.at[near, :, core, ys], stg.at[side, :, :, yd], peer(dx, dy)))
            halo_b1.append(send(b1.at[xs, :, core, ys], b1.at[xd, :, core, yd], peer(dx, dy)))

    far = [
        send(x2F.at[17:18, :, WIN], x2F.at[1:2, :, WIN], peer(1, 0)),
        send(x2F.at[4:5, :, WIN], x2F.at[20:21, :, WIN], peer(-1, 0)),
    ]

    for copy in face_c + face_b + halo:
        copy.wait_send()
    for copy in halo_c1 + halo_c2:
        copy.wait()
    clear_planes(c1, 0, 4, gx == 0)
    clear_planes(c1, 12, 4, gx == nx - 1)
    clear_rows(c1, 8, 8, gy == 0)
    clear_rows(c1, 32, 8, gy == ny - 1)
    clear_planes(c2, 4, 4, gx == 0)
    clear_planes(c2, 0, 4, gx <= 1)
    clear_planes(c2, 12, 4, gx == nx - 1)
    clear_planes(c2, 16, 4, gx >= nx - 2)
    clear_rows(c2, 8, 8, gy == 0)
    clear_rows(c2, 24, 8, gy == ny - 1)
    hand = [
        send(c1.at[:, :, core, 8:40], c1.at[:, :, core, 8:40], sibling),
        send(c2.at[:, core, 8:32], c2.at[:, core, 8:32], sibling),
    ]
    for copy in hand:
        copy.wait()

    lane32, lane24 = lanes(32), lanes(24)
    WL, UL, DL = slice(8, 40), slice(7, 39), slice(9, 41)
    W2, U2, D2 = slice(8, 32), slice(7, 31), slice(9, 33)

    def before_pair(halves, lane):
        turned = [roll_up(half) for half in halves]
        return [jnp.where(lane == 0, 0.0, turned[0]), jnp.where(lane == 0, turned[0], turned[1])]

    def after_pair(halves, lane):
        turned = [roll_down(half) for half in halves]
        return [jnp.where(lane == 127, turned[1], turned[0]), jnp.where(lane == 127, 0.0, turned[1])]

    def z_mid(ref, x):
        p0 = [ref[x, 0, t, WL, :] for t in range(2)]
        p1 = [ref[x, 1, t, WL, :] for t in range(2)]
        return [(before_pair(p1, lane32), p1), (p0, after_pair(p0, lane32))]

    @pl.loop(1, 15)
    def _(x):
        z_list = z_mid(c1, x)
        for q in range(2):
            for t in range(2):
                beside = [
                    c1[x - 1, q, t, WL, :], c1[x + 1, q, t, WL, :], c1[x, q, t, UL, :], c1[x, q, t, DL, :],
                    z_list[q][0][t], z_list[q][1][t],
                ]
                weights, diagonal, inverse = operator_parts(c1[x, q, t, WL, :], beside)
                for n, weight in enumerate(weights):
                    gL[n, x - 1, q, t] = weight
                dL[x, q, t] = diagonal
                x0L[x, q, t, WL, :] = inverse * (1.0 / THETA)

    def setup_low(first, last):
        @pl.loop(first, last)
        def _(x):
            halves = [c2[x, t, W2, :] for t in range(2)]
            low, high = before_pair(halves, lane24), after_pair(halves, lane24)
            for t in range(2):
                beside = [
                    c2[x - 1, t, W2, :], c2[x + 1, t, W2, :], c2[x, t, U2, :], c2[x, t, D2, :], low[t], high[t],
                ]
                weights, _, inverse = operator_parts(halves[t], beside)
                for n, weight in enumerate(weights):
                    g2[n, x - 1, t] = weight
                inv2[x, t] = inverse

    setup_low(8, 12)

    def scale_mid(first, last):
        @pl.loop(first, last)
        def _(x):
            for q in range(2):
                x1L[x, q, core, WL, :] = b1[x, q, core, WL, :] * x0L[x, q, core, WL, :]

        return send(
            x1L.at[first:last, :, core, 8:40], x1L.at[first:last, :, core, 8:40], sibling
        )

    for copy in halo_b1[-2:]:
        copy.wait()
    handed = [scale_mid(5, 11)]
    for copy in halo_b1[:-2]:
        copy.wait()
    for side, at in ((0, 3), (1, 11)):

        @pl.when((gx > 0) if side == 0 else (gx < nx - 1))
        def _(side=side, at=at):
            for n in range(2):
                for q in range(2):
                    b1[at + n, q, core, WL, :] = b1[at + n, q, core, WL, :] + stg[side, n, q, WL, :]

    handed += [scale_mid(1, 5), scale_mid(11, 15)]
    for copy in handed:
        copy.wait()

    def sum_mid(ref, x):
        z_list = z_mid(ref, x)
        return {
            (q, t): gL[0, x - 1, q, t] * ref[x - 1, q, t, WL, :]
            + gL[1, x - 1, q, t] * ref[x + 1, q, t, WL, :]
            + gL[2, x - 1, q, t] * ref[x, q, t, UL, :]
            + gL[3, x - 1, q, t] * ref[x, q, t, DL, :]
            + gL[4, x - 1, q, t] * z_list[q][0][t]
            + gL[5, x - 1, q, t] * z_list[q][1][t]
            for q in range(2)
            for t in range(2)
        }

    def sweep_mid(target, source, first, last, formula):
        def body(x):
            results = {at: formula(x, *at, total) for at, total in sum_mid(source, x).items()}

            def store_all():
                for (q, t), value in results.items():
                    target[x, q, t, WL, :] = value

            return store_all

        planes(first, last, 2, body)

    sweep_mid(
        x2L, x1L, 2, 14, lambda x, q, t, total: first * x1L[x, q, t, WL, :] + GAIN * total
    )
    sweep_mid(
        xpL, x2L, 3, 13,
        lambda x, q, t, total: dL[x, q, t] * (THETA * x1L[x, q, t, WL, :] - x2L[x, q, t, WL, :] + total),
    )

    lane8 = lanes(8)

    for i in range(4):
        for q in range(2):
            for t in range(2):
                t1[i, 2 * q + t, WL, :] = 0.125 * (
                    xpL[2 * i + 3, q, t, WL, :]
                    + 3.0 * (xpL[2 * i + 4, q, t, WL, :] + xpL[2 * i + 5, q, t, WL, :])
                    + xpL[2 * i + 6, q, t, WL, :]
                )
    for i in range(4):
        coarse = []
        for q in range(2):
            halves = []
            for t in range(2):
                part = [t1[i, 2 * q + t, pl.ds(s, 8, stride=2), :] for s in (15, 16, 17, 18)]
                halves.append(0.125 * (part[0] + 3.0 * (part[1] + part[2]) + part[3]))
            coarse.append(halves)
        low, high = before_pair(coarse[1], lane8), after_pair(coarse[0], lane8)
        pair = [0.125 * (low[t] + 3.0 * (coarse[0][t] + coarse[1][t]) + high[t]) for t in range(2)]
        mine = jnp.where(core == 0, pair[0], pair[1])
        bd2[i + 8, core, 16:24, :] = mine * inv2[i + 8, core, 8:16, :]

    halo_b2 = [
        send(
            bd2.at[8:12, core, 16:24],
            bd2.at[8 - 4 * dx : 12 - 4 * dx, core, 16 - 8 * dy : 24 - 8 * dy],
            peer(dx, dy),
        )
        for dx, dy in peers14
    ]
    far_mid = [
        send(x2L.at[8:10, :, :, 8:40], x2L.at[0:2, :, :, 8:40], peer(1, 0)),
        send(x2L.at[6:8, :, :, 8:40], x2L.at[14:16, :, :, 8:40], peer(-1, 0)),
    ]
    setup_low(1, 8)
    setup_low(12, 19)
    handed = []
    for group in (0, 1, 2):
        for (dx, dy), copy in zip(peers14, halo_b2):
            if abs(dx) == group:
                copy.wait()
        for at in sorted({8 - 4 * group, 8 + 4 * group}):
            block = bd2.at[at : at + 4, core, 8:32]
            handed.append(send(block, block, sibling))
    for copy in handed:
        copy.wait()

    def begin_low(x):
        scaled = [jnp.where(c2[x, t, W2, :] > 0.0, bd2[x, t, W2, :], 0.0) for t in range(2)]

        def store_all():
            for t in range(2):
                bd2[x, t, W2, :] = scaled[t]
                d2[x, t] = scaled[t] * (1.0 / THETA_LOW)
                xa[x, t, W2, :] = scaled[t] * (1.0 / THETA_LOW)

        return store_all

    planes(0, 20, 5, begin_low)

    now, later = xa, xb
    for number, (mom, gain) in enumerate(STEPS_LOW):

        def body(x, now=now, later=later, mom=mom, gain=gain):
            halves = [now[x, t, W2, :] for t in range(2)]
            low, high = before_pair(halves, lane24), after_pair(halves, lane24)
            steps = []
            for t in range(2):
                total = (
                    g2[0, x - 1, t] * now[x - 1, t, W2, :]
                    + g2[1, x - 1, t] * now[x + 1, t, W2, :]
                    + g2[2, x - 1, t] * now[x, t, U2, :]
                    + g2[3, x - 1, t] * now[x, t, D2, :]
                    + g2[4, x - 1, t] * low[t]
                    + g2[5, x - 1, t] * high[t]
                )
                steps.append(mom * d2[x, t] + gain * (bd2[x, t, W2, :] - halves[t] + total))

            def store_all():
                for t in range(2):
                    d2[x, t] = steps[t]
                    later[x, t, W2, :] = halves[t] + steps[t]

            return store_all

        planes(number + 1, 19 - number, 6, body)
        now, later = later, now
    bottom = now

    for copy in far_mid:
        copy.wait()

    def prolong_mid(i):
        results = []
        for odd in range(2):
            mixed = [
                0.75 * bottom[i + 6, t, W2, :] + 0.25 * bottom[i + 5 + 2 * odd, t, W2, :]
                for t in range(2)
            ]
            low, high = before_pair(mixed, lane24), after_pair(mixed, lane24)
            for q, side in ((0, low), (1, high)):
                for t in range(2):
                    results.append((odd, 2 * q + t, 0.75 * mixed[t] + 0.25 * side[t]))

        def store_all():
            for odd, slot, value in results:
                bF[2 * i + odd, slot, W2, :] = value

        return store_all

    def prolong_mid_rows(x):
        results = []
        for slot in range(4):
            centre = 0.75 * bF[x, slot, 12:28, :]
            results.append(
                (centre + 0.25 * bF[x, slot, 11:27, :], centre + 0.25 * bF[x, slot, 13:29, :])
            )

        def store_all():
            for slot, (even, odd) in enumerate(results):
                x0L[x, slot // 2, slot % 2, pl.ds(8, 16, stride=2), :] = even
                x0L[x, slot // 2, slot % 2, pl.ds(9, 16, stride=2), :] = odd

        return store_all

    def correct_mid(x):
        results = [
            (q, t, jnp.where(c1[x, q, t, WL, :] > 0.0, x2L[x, q, t, WL, :] + x0L[x, q, t, WL, :], 0.0))
            for q in range(2)
            for t in range(2)
        ]

        def store_all():
            for q, t, value in results:
                x0L[x, q, t, WL, :] = value

        return store_all

    planes(0, 8, 2, prolong_mid)
    planes(0, 16, 4, prolong_mid_rows)
    planes(0, 16, 2, correct_mid)

    def post_first(x, q, t, total):
        start = x0L[x, q, t, WL, :]
        return start + (THETA * x1L[x, q, t, WL, :] - start + total) * (1.0 / THETA)

    def post_second(x, q, t, total):
        here = xpL[x, q, t, WL, :]
        return (
            here
            + MOM * (here - x0L[x, q, t, WL, :])
            + GAIN * (THETA * x1L[x, q, t, WL, :] - here + total)
        )

    sweep_mid(xpL, x0L, 1, 15, post_first)
    sweep_mid(x2L, xpL, 2, 14, post_second)

    for copy in far:
        copy.wait()
    has_left = jnp.where(core == 1, 1.0, 0.0)
    has_right = jnp.where(core == 0, 1.0, 0.0)

    def prolong_fine(i):
        results = []
        for odd in range(2):

            def mixed(q, t):
                return 0.75 * x2L[i + 3, q, t, WL, :] + 0.25 * x2L[i + 2 + 2 * odd, q, t, WL, :]

            m0, m1 = mixed(0, core), mixed(1, core)
            before = roll_up(jnp.where(lane32 == 127, has_left * mixed(1, other), m1))
            after = roll_down(jnp.where(lane32 == 0, has_right * mixed(0, other), m0))
            results.append(
                (
                    0.75 * m0 + 0.25 * before, 0.75 * m0 + 0.25 * m1,
                    0.75 * m1 + 0.25 * m0, 0.75 * m1 + 0.25 * after,
                )
            )

        def store_all():
            for odd in range(2):
                for k in range(4):
                    bF[2 * i + 1 + odd, k, WL, :] = results[odd][k]

        return store_all

    def prolong_fine_rows(x):
        results = []
        for k in range(4):
            centre = 0.75 * bF[x, k, 14:34, :]
            results.append((centre + 0.25 * bF[x, k, 13:33, :], centre + 0.25 * bF[x, k, 15:35, :]))

        def store_all():
            for k, (even, odd) in enumerate(results):
                cF[x, k, pl.ds(8, 20, stride=2), :] = even
                cF[x, k, pl.ds(9, 20, stride=2), :] = odd

        return store_all

    def correct_fine(x):
        results = [cF[x, k, WIN, :] + x2F[x, k, WIN, :] for k in range(4)]

        def store_all():
            for k in range(4):
                cF[x, k, WIN, :] = results[k]

        return store_all

    planes(0, 10, 1, prolong_fine)
    planes(1, 21, 2, prolong_fine_rows)
    planes(1, 21, 2, correct_fine)

    def last_first(x, k, total):
        start = cF[x, k, WIN, :]
        return start + (THETA * xF[x, k, WIN, :] - start + total) * (1.0 / THETA)

    def last_second(x, k, total):
        here = rF[x, k, WIN, :]
        return (
            here
            + MOM * (here - cF[x, k, WIN, :])
            + GAIN * (THETA * xF[x, k, WIN, :] - here + total)
        )

    copy = swap(cF, e1, 2, 20, WIN)
    sweep_fine(rF, cF, e1, 2, 20, INNER, last_first)
    copy.wait()
    copy = edge_first(
        lambda phases: sweep_fine(rF, cF, e1, 2, 20, phases, last_first),
        lambda: swap(rF, e2, 3, 19, WIN),
    )
    sweep_fine(x2F, rF, e2, 3, 19, INNER, last_second)
    copy.wait()
    sweep_fine(x2F, rF, e2, 3, 19, OUTER, last_second)

    def store(part):
        planes_of = pl.ds(part * 4, 4)
        return pltpu.make_async_copy(out_vm.at[planes_of], out_hbm.at[planes_of], local_sem.at[2 + part])

    for part in range(4):
        total = None
        for k in range(4):
            rows = x2F[part * 4 + 3 : part * 4 + 7, k, 12:44, :].reshape(128, 128)
            high = rows.astype(BF16)
            low = (rows - high.astype(F32)).astype(BF16)
            table = perm[:, k * 128 : (k + 1) * 128]
            for piece in (high, low):
                product = lax.dot_general(piece, table, (((1,), (1,)), ((), ())), preferred_element_type=F32)
                total = product if total is None else total + product
        out_vm[part * 4 : part * 4 + 4] = total.reshape(4, 32, 512)
        store(part).start()
    for part in range(4):
        store(part).wait()


def copy_kernel(source, target, buffer, read_sem, write_sem):
    reads, writes = [], []
    for n in range(8):
        part = pl.ds(2 * n, 2)
        reads.append(pltpu.make_async_copy(source.at[part], buffer.at[part], read_sem.at[n]))
        writes.append(pltpu.make_async_copy(buffer.at[part], target.at[part], write_sem.at[n]))
    for copy in reads:
        copy.start()
    for copy, after in zip(reads, writes):
        copy.wait()
        after.start()
    for copy in writes:
        copy.wait()


def local(right_side, coefficient):
    def vmem(*shape):
        return pltpu.VMEM(shape, F32)

    inputs, fine, mid, low = (22, 4, 48, 128), (22, 4, 56, 128), (16, 2, 2, 48, 128), (20, 2, 40, 128)
    edge = (22, 2, 48, 128)
    scratch = [
        vmem(16, 32, 512), vmem(16, 32, 512), vmem(16, 32, 512), pltpu.VMEM((512, 512), BF16),
        vmem(*fine), vmem(*inputs), vmem(*fine), vmem(*fine), vmem(22, 4, 40, 128), vmem(*fine), vmem(6, 20, 4, 40, 128),
        vmem(*edge), vmem(*edge), vmem(*edge),
        vmem(2, 3, 32, 512), vmem(2, 2, 32, 512), vmem(2, 16, 8, 512), vmem(2, 22, 8, 512), vmem(2, 22, 4, 8, 128),
        vmem(10, 4, 48, 128), vmem(10, 4, 16, 128), vmem(10, 2, 16, 128),
        vmem(*mid), vmem(*mid), vmem(*mid), vmem(*mid), vmem(*mid), vmem(*mid), vmem(16, 2, 2, 32, 128),
        vmem(6, 14, 2, 2, 32, 128), vmem(2, 2, 2, 48, 128), vmem(2, 2, 2, 48, 128),
        vmem(*low), vmem(*low), vmem(*low), vmem(*low), vmem(20, 2, 24, 128), vmem(20, 2, 24, 128),
        vmem(6, 18, 2, 24, 128), vmem(2, 2, 2, 40, 128),
        pltpu.SemaphoreType.DMA((6,)), pltpu.SemaphoreType.DMA((80,)), pltpu.SemaphoreType.DMA((80,)),
    ]
    result = pl.pallas_call(
        kernel,
        out_shape=jax.ShapeDtypeStruct((16, 32, 512), F32),
        in_specs=[pl.BlockSpec(memory_space=pl.ANY)] * 2,
        out_specs=pl.BlockSpec(memory_space=pl.ANY),
        scratch_shapes=scratch,
        compiler_params=pltpu.CompilerParams(
            collective_id=0, has_side_effects=True, vmem_limit_bytes=63 * 2**20
        ),
    )(right_side, coefficient)
    return pl.pallas_call(
        copy_kernel,
        out_shape=jax.ShapeDtypeStruct((16, 32, 512), F32),
        in_specs=[pl.BlockSpec(memory_space=pl.ANY)],
        out_specs=pl.BlockSpec(memory_space=pl.ANY),
        scratch_shapes=[vmem(16, 32, 512), pltpu.SemaphoreType.DMA((8,)), pltpu.SemaphoreType.DMA((8,))],
    )(result)


def solution(mesh):
    return jax.shard_map(
        local,
        mesh=mesh,
        in_specs=(P("gx", "gy", "gz"), P("gx", "gy", "gz")),
        out_specs=P("gx", "gy", "gz"),
        check_vma=False,
    )
```
